128 devices in a mesh: slab: 2 (over z_lo), tile: 64 (over z_hi, x, y, core).
Axes of the slice: x: 4, y: 4, z: 4 (z_hi: 2, z_lo: 2; z = z_hi * 2 + z_lo), core: 2. Of those that a mesh axis runs over, the one named last changes fastest.
Arguments:
- transmission: float32 [4, 2, 8192, 384], P('slab', None, 'tile'), may hold values from -4.2 to 4.2
- probe: float32 [2, 256, 256], replicated, may hold values from -6 to 6
- scan_offsets: int32 [128, 2], P('tile'), may hold values from 0 to 128, as said below
- amplitudes: float32 [128, 256, 256], P('tile'), may hold values from 0.2 to 2
Outputs:
- object_grad: float32 [4, 2, 8192, 384], P('slab', None, 'tile')
- probe_grad: float32 [2, 256, 256], replicated
The draws below stay inside these ranges and needn't reach their ends.
Inputs may be any that keep to these rules, and one draw needn't show every extreme that they name: `scan_offsets`: column 0 lies within 0 to 128 and column 1 within 0 to 128; both ends of both columns occur.
All inputs are finite; a program needn't handle non-finite values.
Results may differ from the reference program's by a relative error of at most 0.0003.
Values sent between devices are 32-bit elements; how exact they have to be, the bound alone decides.
No kernel may reach another device: no remote copies, remote signals or barrier semaphores. Data moves between devices by JAX's collectives and lax.ppermute only.
A program may use at most 128 MiB of HBM per device.

```python
import jax
import jax.numpy as jnp
from jax import lax

W = 256
XW = 384
BAND = 128
HALO = 128
POS_DEV = 2
SLICES = 4
NY = 8192
POSITIONS = 128


def draw_scan_offsets(key, part):
    key = jax.random.fold_in(key, 11)
    keys = jax.random.split(key, 4)
    row_most = BAND + 2 * HALO - W
    col_most = XW - W
    rows = jax.random.randint(keys[0], (POSITIONS,), 0, row_most + 1)
    cols = jax.random.randint(keys[1], (POSITIONS,), 0, col_most + 1)
    blocks = POSITIONS // POS_DEV
    picked = jax.random.randint(keys[2], (blocks,), 0, POS_DEV)
    flipped = jax.random.randint(keys[3], (), 0, 2)
    index = jnp.arange(POSITIONS)
    block_of = index // POS_DEV
    chosen = index % POS_DEV == picked[block_of]
    upper = (block_of + flipped) % 2 == 1
    rows = jnp.where(chosen, jnp.where(upper, row_most, 0), rows)
    cols = jnp.where(chosen, jnp.where(upper, 0, col_most), cols)
    return jnp.stack([rows, cols], axis=1).astype(jnp.int32)


def shard_levels(stream_key, shape, pieces, low, high):
    factor_of = 1.0
    for dim, shards_of in pieces:
        heights = jax.random.uniform(jax.random.fold_in(jax.random.fold_in(stream_key, 6), dim), (shards_of,), jnp.float32, low / len(pieces), high / len(pieces))
        factor_of = factor_of * jnp.repeat(jnp.exp(heights), shape[dim] // shards_of).reshape((-1,) + (1,) * (len(shape) - 1 - dim))
    return factor_of


def centred(own_key, dims, deviation, limit, shards=(), kind=jnp.bfloat16):
    result = deviation * jax.random.normal(own_key, dims, jnp.float32)
    if shards:
        result = result * shard_levels(own_key, dims, shards, -0.22, 0.18)
    return jnp.clip(result, -limit, limit).astype(kind)


def setup_inputs(seed: int = 0) -> dict:
    splits = jax.random.split(jax.random.key(seed), 5)
    transmission = centred(splits[0], (SLICES, 2, NY, XW), 0.7, 4.2, ((0, 2), (2, 64)), jnp.float32)
    probe = centred(splits[1], (2, W, W), 1.0, 6.0, (), jnp.float32)
    scan_offsets = draw_scan_offsets(jax.random.fold_in(splits[4], 71), 0)
    amplitudes = jnp.clip(0.2 + 1.8 * jax.random.uniform(splits[3], (POSITIONS, W, W), jnp.float32) ** shard_levels(splits[3], (POSITIONS, W, W), ((0, 64),), -0.2, 0.2), 0.2, 2.0)
    return {"transmission": transmission, "probe": probe, "scan_offsets": scan_offsets, "amplitudes": amplitudes}


prop_strength = 12.0

def fresnel_kernel(width):
    index = jnp.arange(width)
    freq = ((index + width // 2) % width - width // 2).astype(jnp.float32) / width
    phase = -prop_strength * (freq[:, None] ** 2 + freq[None, :] ** 2)
    return jnp.cos(phase) + 1j * jnp.sin(phase)

def position_loss(windows, probe, target, kernel):
    wave = probe[0] + 1j * probe[1]
    for slice_index in range(SLICES):
        piece = windows[slice_index, 0] + 1j * windows[slice_index, 1]
        wave = jnp.fft.ifft2(kernel * jnp.fft.fft2(wave * piece, norm='ortho'), norm='ortho')
    far = jnp.fft.fft2(wave, norm='ortho')
    model = jnp.sqrt(jnp.real(far) ** 2 + jnp.imag(far) ** 2 + 1.0)
    return 0.5 * jnp.sum((model - target) ** 2)

def reference(transmission, probe, scan_offsets, amplitudes):
    kernel = fresnel_kernel(W)
    padded = jnp.concatenate([transmission[:, :, NY - HALO:], transmission, transmission[:, :, :HALO]], axis=2)
    grad_pad = jnp.zeros_like(padded)
    grad_probe = jnp.zeros_like(probe)

    def step(carry, item):
        grad_pad, grad_probe = carry
        position, offsets, target = item
        row_start = (position // POS_DEV * BAND + offsets[0]).astype(jnp.int32)
        col_start = offsets[1].astype(jnp.int32)
        zero = jnp.int32(0)
        windows = lax.dynamic_slice(padded, (zero, zero, row_start, col_start), (SLICES, 2, W, W))
        _, pull = jax.vjp(lambda wins, prb: position_loss(wins, prb, target, kernel), windows, probe)
        grad_win, grad_prb = pull(jnp.ones((), dtype=probe.dtype))
        current = lax.dynamic_slice(grad_pad, (zero, zero, row_start, col_start), (SLICES, 2, W, W))
        grad_pad = lax.dynamic_update_slice(grad_pad, current + grad_win, (zero, zero, row_start, col_start))
        return ((grad_pad, grad_probe + grad_prb), None)
    positions = jnp.arange(POSITIONS, dtype=jnp.int32)
    (grad_pad, grad_probe), _ = lax.scan(step, (grad_pad, grad_probe), (positions, scan_offsets, amplitudes))
    core = grad_pad[:, :, HALO:HALO + NY]
    head = core[:, :, :HALO] + grad_pad[:, :, HALO + NY:]
    tail = core[:, :, NY - HALO:] + grad_pad[:, :, :HALO]
    middle = core[:, :, HALO:NY - HALO]
    object_grad = jnp.concatenate([head, middle, tail], axis=2)
    return (object_grad, grad_probe)
```

```python
import jax
import jax.numpy as jnp
import numpy as np
from jax import lax
from jax.experimental import pallas as pl
from jax.experimental.pallas import tpu as pltpu
from jax.sharding import PartitionSpec as P

WIDTH = 256
HALO = 128
COLS = 384
ROWS = 392
PROP_STRENGTH = 12.0
BF16 = jnp.bfloat16
F32 = jnp.float32


def split_table(table):
    parts = []
    for part in (table.real, table.imag):
        part = part.astype(np.float32)
        high = part.astype(jnp.bfloat16)
        low = (part - high.astype(np.float32)).astype(jnp.bfloat16)
        parts += [high, low]
    return np.stack(parts)


def make_tables():
    index = np.arange(WIDTH)
    dft = np.exp(-2j * np.pi / WIDTH * (index[:, None] * index[None, :] % WIDTH)) / np.sqrt(WIDTH)
    freq = ((index + WIDTH // 2) % WIDTH - WIDTH // 2) / WIDTH
    phase = np.exp(-1j * PROP_STRENGTH * freq**2)
    prop = dft.conj() @ (phase[:, None] * dft)
    far = phase[:, None] * dft
    return np.stack([split_table(prop), split_table(far), split_table(far.T)])


def split(x):
    high = x.astype(BF16)
    low = (x - high.astype(F32)).astype(BF16)
    return high, low


def dot(a, b):
    return jnp.dot(a, b, preferred_element_type=F32)


def right_mult(x, table):
    (rh, rl), (ih, il) = split(x[0]), split(x[1])
    nh, nl = -ih, -il
    trh, trl, tih, til = (table[i] for i in range(4))
    re = dot(
        jnp.concatenate([rh, rl, rh, nh, nl, nh], axis=1),
        jnp.concatenate([trh, trh, trl, tih, tih, til], axis=0),
    )
    im = dot(
        jnp.concatenate([rh, rl, rh, ih, il, ih], axis=1),
        jnp.concatenate([tih, tih, til, trh, trh, trl], axis=0),
    )
    return re, im


def left_mult(table, x):
    (rh, rl), (ih, il) = split(x[0]), split(x[1])
    nh, nl = -ih, -il
    trh, trl, tih, til = (table[i] for i in range(4))
    left_re = jnp.concatenate([trh, trl, trh, tih, til, tih], axis=1)
    left_im = jnp.concatenate([tih, til, tih, trh, trl, trh], axis=1)
    re = dot(left_re, jnp.concatenate([rh, rh, rl, nh, nh, nl], axis=0))
    im = dot(left_im, jnp.concatenate([rh, rh, rl, ih, ih, il], axis=0))
    return re, im


def times(a, b):
    return a[0] * b[0] - a[1] * b[1], a[0] * b[1] + a[1] * b[0]


def kernel(
    place_ref,
    offsets_ref,
    tables_ref,
    probe_ref,
    amp_hbm,
    own_hbm,
    own_prev_hbm,
    own_next_hbm,
    oth_hbm,
    oth_prev_hbm,
    oth_next_hbm,
    probe_out,
    own_core_out,
    own_head_out,
    own_tail_out,
    oth_core_out,
    oth_head_out,
    oth_tail_out,
    ext,
    amp,
    windows,
    waves,
    grads,
    in_sem,
    amp_sem,
    out_sem,
):
    place = place_ref[0]
    row = offsets_ref[place, 0]
    col = offsets_ref[place, 1]
    fine = lax.rem(row, 8)
    base = pl.multiple_of(row - fine, 8)
    ins = ((own_prev_hbm, own_hbm, own_next_hbm), (oth_prev_hbm, oth_hbm, oth_next_hbm))
    outs = ((own_head_out, own_core_out, own_tail_out), (oth_head_out, oth_core_out, oth_tail_out))

    def in_copies(s, sources):
        return [
            pltpu.make_async_copy(
                sources[k].at[s % 2], ext.at[s, :, k * HALO : (k + 1) * HALO, :], in_sem.at[s, k]
            )
            for k in range(3)
        ]

    def out_copies(s, targets):
        return [
            pltpu.make_async_copy(
                grads.at[s, :, k * HALO : (k + 1) * HALO, :], targets[k].at[s % 2], out_sem.at[s, k]
            )
            for k in range(3)
        ]

    for s in range(4):
        mine = place == s // 2

        @pl.when(mine)
        def _():
            for copy in in_copies(s, ins[0]):
                copy.start()

        @pl.when(jnp.logical_not(mine))
        def _():
            for copy in in_copies(s, ins[1]):
                copy.start()

    amp_copy = pltpu.make_async_copy(amp_hbm.at[place], amp, amp_sem)
    amp_copy.start()

    prop, far, far_t = tables_ref.at[0], tables_ref.at[1], tables_ref.at[2]
    wave = (probe_ref[0], probe_ref[1])
    for s in range(4):
        for copy in in_copies(s, ins[0]):
            copy.wait()
        window = []
        for c in range(2):
            rows = ext[s, c, pl.ds(base, WIDTH + 8), :]
            rows = pltpu.roll(rows, lax.rem(WIDTH + 8 - fine, WIDTH + 8), 0)[:WIDTH]
            piece = pltpu.roll(rows, lax.rem(COLS - col, COLS), 1)[:, :WIDTH]
            window.append(piece)
            windows[s, c] = piece
            if s > 0:
                waves[s, c] = wave[c]
        prod = times(wave, window)
        if s < 3:
            wave = left_mult(prop, right_mult(prod, prop))
    field = left_mult(far, right_mult(prod, far_t))
    amp_copy.wait()
    model = jnp.sqrt(field[0] * field[0] + field[1] * field[1] + 1.0)
    ratio = (model - amp[...]) / model
    grad = (field[0] * ratio, -(field[1] * ratio))
    grad = left_mult(far_t, right_mult(grad, far))
    for s in range(3, -1, -1):
        window = (windows[s, 0], windows[s, 1])
        wave = (waves[s, 0], waves[s, 1]) if s > 0 else (probe_ref[0], probe_ref[1])
        object_grad = times(wave, grad)
        for c in range(2):
            value = object_grad[c] if c == 0 else -object_grad[c]
            wide = jnp.concatenate([value, jnp.zeros((WIDTH, COLS - WIDTH), F32)], axis=1)
            wide = pltpu.roll(wide, col, 1)
            wide = jnp.concatenate([wide, jnp.zeros((8, COLS), F32)], axis=0)
            grads[s, c, 0:HALO, :] = jnp.zeros((HALO, COLS), F32)
            grads[s, c, 2 * HALO : 3 * HALO, :] = jnp.zeros((HALO, COLS), F32)
            grads[s, c, pl.ds(base, WIDTH + 8), :] = pltpu.roll(wide, fine, 0)
        mine = place == s // 2

        @pl.when(mine)
        def _():
            for copy in out_copies(s, outs[0]):
                copy.start()

        @pl.when(jnp.logical_not(mine))
        def _():
            for copy in out_copies(s, outs[1]):
                copy.start()

        grad = times(window, grad)
        if s > 0:
            grad = left_mult(prop, right_mult(grad, prop))
    probe_out[0] = grad[0]
    probe_out[1] = -grad[1]
    for s in range(4):
        for copy in out_copies(s, outs[0]):
            copy.wait()


def position(place, offsets, tables, probe, amplitudes, own, oth):
    band = jax.ShapeDtypeStruct((2, 2, HALO, COLS), F32)
    vmem = pl.BlockSpec(memory_space=pltpu.VMEM)
    smem = pl.BlockSpec(memory_space=pltpu.SMEM)
    hbm = pl.BlockSpec(memory_space=pl.ANY)
    return pl.pallas_call(
        kernel,
        out_shape=(jax.ShapeDtypeStruct((2, WIDTH, WIDTH), F32),) + (band,) * 6,
        in_specs=[smem, smem, vmem, vmem] + [hbm] * 7,
        out_specs=(vmem,) + (hbm,) * 6,
        scratch_shapes=[
            pltpu.VMEM((4, 2, ROWS, COLS), F32),
            pltpu.VMEM((WIDTH, WIDTH), F32),
            pltpu.VMEM((4, 2, WIDTH, WIDTH), F32),
            pltpu.VMEM((4, 2, WIDTH, WIDTH), F32),
            pltpu.VMEM((4, 2, ROWS, COLS), F32),
            pltpu.SemaphoreType.DMA((4, 3)),
            pltpu.SemaphoreType.DMA,
            pltpu.SemaphoreType.DMA((4, 3)),
        ],
        compiler_params=pltpu.CompilerParams(vmem_limit_bytes=48 * 1024 * 1024),
        cost_estimate=pl.CostEstimate(flops=6_000_000_000, bytes_accessed=12_000_000, transcendentals=0),
        name="position",
    )(place, offsets, tables, probe, amplitudes, *own, *oth)


def along_tile(x, by):
    count = lax.axis_size("tile")
    return lax.ppermute(x, "tile", [(i, (i + by) % count) for i in range(count)])


def swap_slab(x):
    return lax.ppermute(x, "slab", [(0, 1), (1, 0)])


def shards(transmission, probe, scan_offsets, amplitudes):
    tables = jnp.asarray(make_tables())
    place = lax.axis_index("slab").astype(jnp.int32).reshape(1)
    own = transmission
    oth = swap_slab(own)
    own_prev, own_next = along_tile(own, 1), along_tile(own, -1)
    oth_prev, oth_next = along_tile(oth, 1), along_tile(oth, -1)
    probe_term, own_core, own_head, own_tail, oth_core, oth_head, oth_tail = position(
        place, scan_offsets, tables, probe, amplitudes, (own, own_prev, own_next), (oth, oth_prev, oth_next)
    )
    oth_sum = oth_core + along_tile(oth_head, -1) + along_tile(oth_tail, 1)
    own_sum = own_core + along_tile(own_head, -1) + along_tile(own_tail, 1)
    object_grad = own_sum + swap_slab(oth_sum)

    axes = ("slab", "tile")
    devices = lax.axis_size(axes)
    parts = probe_term.reshape(devices, 8, 128)
    mine = jnp.sum(lax.all_to_all(parts, axes, 0, 0, tiled=True), axis=0)
    spread = jnp.broadcast_to(mine[None], (devices, 8, 128))
    probe_grad = lax.all_to_all(spread, axes, 0, 0, tiled=True).reshape(probe.shape)
    return object_grad, probe_grad


def solution(mesh):
    placed = (P("slab", None, "tile", None), P(), P("tile", None), P("tile", None, None))
    return jax.shard_map(
        shards,
        mesh=mesh,
        in_specs=placed,
        out_specs=(P("slab", None, "tile", None), P()),
        check_vma=False,
    )
```

```python
import jax
import jax.numpy as jnp
import numpy as np
from jax import lax
from jax.experimental import pallas as pl
from jax.experimental.pallas import tpu as pltpu
from jax.sharding import PartitionSpec as P

WIDTH = 256
HALF = 128
HALO = 128
COLS = 384
PROP_STRENGTH = 12.0
BF16 = jnp.bfloat16
F32 = jnp.float32
VMEM = pl.BlockSpec(memory_space=pltpu.VMEM)
SMEM = pl.BlockSpec(memory_space=pltpu.SMEM)


def high_low(table):
    table = table.astype(np.float32)
    high = table.astype(jnp.bfloat16)
    low = (table - high.astype(np.float32)).astype(jnp.bfloat16)
    return np.stack([high, low])


def on_right(m):
    return high_low(np.block([[m.real, m.imag], [-m.imag, m.real]]))


def on_left(m):
    return high_low(np.block([[m.real, -m.imag], [m.imag, m.real]]))


def make_tables():
    index = np.arange(WIDTH)
    dft = np.exp(-2j * np.pi / WIDTH * (index[:, None] * index[None, :] % WIDTH)) / np.sqrt(WIDTH)
    freq = ((index + WIDTH // 2) % WIDTH - WIDTH // 2) / WIDTH
    phase = np.exp(-1j * PROP_STRENGTH * freq**2)
    prop = dft.conj() @ (phase[:, None] * dft)
    far = phase[:, None] * dft
    p, q = prop[:HALF, :HALF], prop[:HALF, HALF:]
    props = ((p + q) / 2, (p - q) / 2)
    fars = (far[0::2, :HALF], far[1::2, :HALF])
    return np.stack(
        [
            np.stack([on_right(m) for m in props]),
            np.stack([on_left(m) for m in props]),
            np.stack([on_right(m.T) for m in fars]),
            np.stack([on_left(m) for m in fars]),
            np.stack([on_right(m) for m in fars]),
            np.stack([on_left(m.T) for m in fars]),
        ]
    )


PROP_RIGHT, PROP_LEFT, FAR_RIGHT, FAR_LEFT, BACK_RIGHT, BACK_LEFT = range(6)


def split(x):
    high = x.astype(BF16)
    low = (x - high.astype(F32)).astype(BF16)
    return high, low


def dot(a, b):
    return jnp.dot(a, b, preferred_element_type=F32)


def fold(x):
    x = jnp.concatenate([x[:HALF] + x[HALF:], x[:HALF] - x[HALF:]], axis=0)
    return jnp.concatenate([x[:, :HALF] + x[:, HALF:], x[:, :HALF] - x[:, HALF:]], axis=1)


def right_mult(x, tables, which):
    re, im = [], []
    for h in range(2):
        part = slice(h * HALF, (h + 1) * HALF)
        high, low = split(jnp.concatenate([x[0][:, part], x[1][:, part]], axis=1))
        th, tl = tables[which, h, 0], tables[which, h, 1]
        out = dot(jnp.concatenate([high, low, high], axis=1), jnp.concatenate([th, th, tl], axis=0))
        re.append(out[:, :HALF])
        im.append(out[:, HALF:])
    return jnp.concatenate(re, axis=1), jnp.concatenate(im, axis=1)


def left_mult(x, tables, which):
    re, im = [], []
    for h in range(2):
        part = slice(h * HALF, (h + 1) * HALF)
        high, low = split(jnp.concatenate([x[0][part], x[1][part]], axis=0))
        th, tl = tables[which, h, 0], tables[which, h, 1]
        out = dot(jnp.concatenate([th, th, tl], axis=1), jnp.concatenate([high, low, high], axis=0))
        re.append(out[:HALF])
        im.append(out[HALF:])
    return jnp.concatenate(re, axis=0), jnp.concatenate(im, axis=0)


def propagate(x, tables):
    y = right_mult((fold(x[0]), fold(x[1])), tables, PROP_RIGHT)
    y = left_mult(y, tables, PROP_LEFT)
    return fold(y[0]), fold(y[1])


def times(a, b):
    return a[0] * b[0] - a[1] * b[1], a[0] * b[1] + a[1] * b[0]


def pick_columns(x, col):
    lane = lax.broadcasted_iota(jnp.int32, x.shape[:-1] + (HALF,), len(x.shape) - 1)
    left = jnp.where(lane >= col, x[..., :HALF], x[..., 2 * HALF :])
    return jnp.concatenate([left, x[..., HALF : 2 * HALF]], axis=-1)


def pick_rows(prev, after, row):
    line = lax.broadcasted_iota(jnp.int32, prev.shape, len(prev.shape) - 2)
    return jnp.where(line >= row, prev, after)


def roll_probe_kernel(place_ref, offsets_ref, probe_ref, out_ref):
    row, col = offsets_ref[place_ref[0], 0], offsets_ref[place_ref[0], 1]
    for c in range(2):
        out_ref[c] = pltpu.roll(pltpu.roll(probe_ref[c], row, 0), col, 1)


def core_kernel(place_ref, offsets_ref, own_ref, out_ref):
    col = offsets_ref[1 - place_ref[0], 1]
    out_ref[...] = pick_columns(own_ref[...], col)


def halo_kernel(place_ref, offsets_ref, prev_ref, next_ref, out_ref):
    other = 1 - place_ref[0]
    row, col = offsets_ref[other, 0], offsets_ref[other, 1]
    out_ref[...] = pick_columns(pick_rows(prev_ref[...], next_ref[...], row), col)


def window_kernel(place_ref, offsets_ref, own_ref, prev_ref, next_ref, out_ref):
    row, col = offsets_ref[place_ref[0], 0], offsets_ref[place_ref[0], 1]
    out_ref[:, :, :HALO] = pick_columns(pick_rows(prev_ref[...], next_ref[...], row), col)
    out_ref[:, :, HALO:] = pick_columns(own_ref[...], col)


def position_kernel(
    place_ref,
    offsets_ref,
    tables_ref,
    probe_ref,
    amp_ref,
    own_ref,
    core_ref,
    halo_ref,
    probe_out,
    own_out,
    oth_out,
    waves,
):
    place = place_ref[0]
    row, col = offsets_ref[place, 0], offsets_ref[place, 1]

    def window_of(s):
        mine = place == s // 2
        out = []
        for c in range(2):
            other = jnp.concatenate([halo_ref[s % 2, c], core_ref[s % 2, c]], axis=0)
            out.append(jnp.where(mine, own_ref[s % 2, c], other))
        return out

    wave = (probe_ref[0], probe_ref[1])
    for s in range(4):
        if s > 0:
            waves[s - 1, 0], waves[s - 1, 1] = wave
        prod = times(wave, window_of(s))
        if s < 3:
            wave = propagate(prod, tables_ref)
    field = right_mult((fold(prod[0]), fold(prod[1])), tables_ref, FAR_RIGHT)
    field = left_mult(field, tables_ref, FAR_LEFT)
    model = jnp.sqrt(field[0] * field[0] + field[1] * field[1] + 1.0)
    ratio = (model - amp_ref[...]) / model
    grad = (field[0] * ratio, -(field[1] * ratio))
    grad = right_mult(grad, tables_ref, BACK_RIGHT)
    grad = left_mult(grad, tables_ref, BACK_LEFT)
    grad = (fold(grad[0]), fold(grad[1]))
    for s in range(3, -1, -1):
        wave = (waves[s - 1, 0], waves[s - 1, 1]) if s > 0 else (probe_ref[0], probe_ref[1])
        object_grad = times(wave, grad)
        mine = place == s // 2

        @pl.when(mine)
        def _():
            own_out[s % 2, 0] = object_grad[0]
            own_out[s % 2, 1] = -object_grad[1]

        @pl.when(jnp.logical_not(mine))
        def _():
            oth_out[s % 2, 0] = object_grad[0]
            oth_out[s % 2, 1] = -object_grad[1]

        grad = times(window_of(s), grad)
        if s > 0:
            grad = propagate(grad, tables_ref)
    for c in range(2):
        value = grad[c] if c == 0 else -grad[c]
        value = pltpu.roll(value, lax.rem(WIDTH - row, WIDTH), 0)
        value = pltpu.roll(value, lax.rem(WIDTH - col, WIDTH), 1)
        for h in range(2):
            probe_out[c, :, h] = value[:, h * HALF : (h + 1) * HALF].reshape(WIDTH // 8, 8, HALF)


def spread_kernel(place_ref, offsets_ref, own_ref, got_ref, core_out, prev_out, next_out):
    place = place_ref[0]
    core = prev = after = 0.0
    for ref, index in ((own_ref, place), (got_ref, 1 - place)):
        row, col = offsets_ref[index, 0], offsets_ref[index, 1]
        grad = ref[...]
        lane = lax.broadcasted_iota(jnp.int32, grad.shape[:-1] + (HALF,), 3)
        kept = lane >= col
        wide = jnp.concatenate(
            [
                jnp.where(kept, grad[..., :HALF], 0.0),
                grad[..., HALF:],
                jnp.where(kept, 0.0, grad[..., :HALF]),
            ],
            axis=-1,
        )
        core = core + wide[:, :, HALO:]
        halo = wide[:, :, :HALO]
        line = lax.broadcasted_iota(jnp.int32, halo.shape, 2)
        prev = prev + jnp.where(line >= row, halo, 0.0)
        after = after + jnp.where(line >= row, 0.0, halo)
    core_out[...] = core
    prev_out[...] = prev
    next_out[...] = after


def call(kernel, shapes, smem, vmem, name, scratch=(), flops=0, nbytes=2_000_000):
    single = isinstance(shapes[0], int)
    shapes = (shapes,) if single else shapes
    out = pl.pallas_call(
        kernel,
        out_shape=tuple(jax.ShapeDtypeStruct(shape, F32) for shape in shapes),
        in_specs=[SMEM] * len(smem) + [VMEM] * len(vmem),
        out_specs=(VMEM,) * len(shapes),
        scratch_shapes=scratch,
        compiler_params=pltpu.CompilerParams(vmem_limit_bytes=40 * 1024 * 1024),
        cost_estimate=pl.CostEstimate(flops=flops, bytes_accessed=nbytes, transcendentals=0),
        name=name,
    )(*smem, *vmem)
    return out[0] if single else out


def along_tile(x, by):
    count = lax.axis_size("tile")
    return lax.ppermute(x, "tile", [(i, (i + by) % count) for i in range(count)])


def swap_slab(x):
    return lax.ppermute(x, "slab", [(0, 1), (1, 0)])


def shards(transmission, probe, scan_offsets, amplitudes):
    tables = jnp.asarray(make_tables())
    index = lax.axis_index("slab").astype(jnp.int32)
    where = (index.reshape(1), scan_offsets)
    own = transmission
    part, whole, band = (2, 2, HALO, WIDTH), (2, 2, WIDTH, WIDTH), (2, 2, HALO, COLS)

    core = swap_slab(call(core_kernel, part, where, (own,), "core"))
    prev, after = along_tile(own, 1), along_tile(own, -1)
    rolled = call(roll_probe_kernel, (2, WIDTH, WIDTH), where, (probe,), "roll")
    amp = lax.dynamic_index_in_dim(amplitudes, index, 0, keepdims=False)
    amp = amp.reshape(HALF, 2, HALF, 2).transpose(1, 0, 3, 2).reshape(WIDTH, WIDTH)
    halo = swap_slab(call(halo_kernel, part, where, (prev, after), "halo"))
    windows = call(window_kernel, whole, where, (own, prev, after), "window")

    tiles = (2, WIDTH // 8, 2, 8, HALF)
    probe_term, own_grad, oth_grad = call(
        position_kernel,
        (tiles, whole, whole),
        where,
        (tables, rolled, amp, windows, core, halo),
        "position",
        scratch=[pltpu.VMEM((3, 2, WIDTH, WIDTH), F32)],
        flops=3_300_000_000,
        nbytes=10_000_000,
    )
    got = swap_slab(oth_grad)
    axes = ("slab", "tile")
    devices = lax.axis_size(axes)
    parts = probe_term.reshape(devices, 8, HALF)
    mine = jnp.sum(lax.all_to_all(parts, axes, 0, 0, tiled=True), axis=0)
    spread = jnp.broadcast_to(mine[None], (devices, 8, HALF))
    probe_grad = lax.all_to_all(spread, axes, 0, 0, tiled=True).reshape(tiles)
    probe_grad = probe_grad.transpose(0, 1, 3, 2, 4).reshape(probe.shape)

    own_sum, to_prev, to_next = call(spread_kernel, (band,) * 3, where, (own_grad, got), "spread")
    object_grad = own_sum + along_tile(to_prev, -1) + along_tile(to_next, 1)
    return object_grad, probe_grad


def solution(mesh):
    placed = (P("slab", None, "tile", None), P(), P("tile", None), P("tile", None, None))
    return jax.shard_map(
        shards,
        mesh=mesh,
        in_specs=placed,
        out_specs=(P("slab", None, "tile", None), P()),
        check_vma=False,
    )
```

```python
import functools

import jax
import jax.numpy as jnp
import numpy as np
from jax import lax
from jax.experimental import pallas as pl
from jax.experimental.pallas import tpu as pltpu
from jax.sharding import PartitionSpec as P

WIDTH = 256
HALF = 128
HALO = 128
COLS = 384
PROP_STRENGTH = 12.0
BF16 = jnp.bfloat16
F32 = jnp.float32
VMEM = pl.BlockSpec(memory_space=pltpu.VMEM)
SMEM = pl.BlockSpec(memory_space=pltpu.SMEM)


def high_low(table):
    table = table.astype(np.float32)
    high = table.astype(jnp.bfloat16)
    low = (table - high.astype(np.float32)).astype(jnp.bfloat16)
    return np.stack([high, low])


def on_right(m):
    return high_low(np.block([[m.real, m.imag], [-m.imag, m.real]]))


def on_left(m):
    return high_low(np.block([[m.real, -m.imag], [m.imag, m.real]]))


def make_tables():
    index = np.arange(WIDTH)
    dft = np.exp(-2j * np.pi / WIDTH * (index[:, None] * index[None, :] % WIDTH)) / np.sqrt(WIDTH)
    freq = ((index + WIDTH // 2) % WIDTH - WIDTH // 2) / WIDTH
    phase = np.exp(-1j * PROP_STRENGTH * freq**2)
    prop = dft.conj() @ (phase[:, None] * dft)
    far = phase[:, None] * dft
    p, q = prop[:HALF, :HALF], prop[:HALF, HALF:]
    props = ((p + q) / 2, (p - q) / 2)
    fars = (far[0::2, :HALF], far[1::2, :HALF])
    return np.stack(
        [
            np.stack([on_right(m) for m in props]),
            np.stack([on_left(m) for m in props]),
            np.stack([on_right(m.T) for m in fars]),
            np.stack([on_left(m) for m in fars]),
            np.stack([on_right(m) for m in fars]),
            np.stack([on_left(m.T) for m in fars]),
        ]
    )


PROP_RIGHT, PROP_LEFT, FAR_RIGHT, FAR_LEFT, BACK_RIGHT, BACK_LEFT = range(6)


def split(x):
    high = x.astype(BF16)
    low = (x - high.astype(F32)).astype(BF16)
    return high, low


def dot(a, b):
    return jnp.dot(a, b, preferred_element_type=F32)


def fold(x):
    x = jnp.concatenate([x[:HALF] + x[HALF:], x[:HALF] - x[HALF:]], axis=0)
    return jnp.concatenate([x[:, :HALF] + x[:, HALF:], x[:, :HALF] - x[:, HALF:]], axis=1)


def right_mult(x, tables, which):
    re, im = [], []
    for h in range(2):
        part = slice(h * HALF, (h + 1) * HALF)
        high, low = split(jnp.concatenate([x[0][:, part], x[1][:, part]], axis=1))
        th, tl = tables[which, h, 0], tables[which, h, 1]
        out = dot(jnp.concatenate([high, low, high], axis=1), jnp.concatenate([th, th, tl], axis=0))
        re.append(out[:, :HALF])
        im.append(out[:, HALF:])
    return jnp.concatenate(re, axis=1), jnp.concatenate(im, axis=1)


def left_mult(x, tables, which):
    re, im = [], []
    for h in range(2):
        part = slice(h * HALF, (h + 1) * HALF)
        high, low = split(jnp.concatenate([x[0][part], x[1][part]], axis=0))
        th, tl = tables[which, h, 0], tables[which, h, 1]
        out = dot(jnp.concatenate([th, th, tl], axis=1), jnp.concatenate([high, low, high], axis=0))
        re.append(out[:HALF])
        im.append(out[HALF:])
    return jnp.concatenate(re, axis=0), jnp.concatenate(im, axis=0)


def propagate(x, tables):
    y = right_mult((fold(x[0]), fold(x[1])), tables, PROP_RIGHT)
    y = left_mult(y, tables, PROP_LEFT)
    return fold(y[0]), fold(y[1])


def times(a, b):
    return a[0] * b[0] - a[1] * b[1], a[0] * b[1] + a[1] * b[0]


def pick_columns(x, col):
    lane = lax.broadcasted_iota(jnp.int32, x.shape[:-1] + (HALF,), len(x.shape) - 1)
    left = jnp.where(lane >= col, x[..., :HALF], x[..., 2 * HALF :])
    return jnp.concatenate([left, x[..., HALF : 2 * HALF]], axis=-1)


def pick_rows(across, beside, row, odd):
    line = lax.broadcasted_iota(jnp.int32, across.shape, len(across.shape) - 2)
    return jnp.where(jnp.where(line >= row, 1, 0) == odd, beside, across)


def roll_probe_kernel(place_ref, offsets_ref, probe_ref, out_ref):
    row, col = offsets_ref[place_ref[0], 0], offsets_ref[place_ref[0], 1]
    for c in range(2):
        out_ref[c] = pltpu.roll(pltpu.roll(probe_ref[c], row, 0), col, 1)


def core_kernel(place_ref, offsets_ref, own_ref, out_ref, copy_ref):
    col = offsets_ref[1 - place_ref[0], 1]
    own = own_ref[...]
    out_ref[...] = pick_columns(own, col)
    copy_ref[...] = own


def amp_kernel(place_ref, offsets_ref, amp_ref, out_ref):
    x = amp_ref[place_ref[0]]
    line = lax.broadcasted_iota(jnp.int32, (WIDTH, WIDTH), 0)
    lane = lax.broadcasted_iota(jnp.int32, (WIDTH, WIDTH), 1)
    rows = jnp.where(lane == 2 * (line % HALF) + line // HALF, 1.0, 0.0).astype(BF16)
    cols = jnp.where(line == 2 * (lane % HALF) + lane // HALF, 1.0, 0.0).astype(BF16)

    def parts(value):
        high, rest = split(value)
        return high, rest, (value - high.astype(F32) - rest.astype(F32)).astype(BF16)

    x = sum(dot(rows, part) for part in parts(x))
    out_ref[...] = sum(dot(part, cols) for part in parts(x))


def halo_kernel(place_ref, offsets_ref, across_ref, beside_ref, out_ref):
    other = 1 - place_ref[0]
    row, col = offsets_ref[other, 0], offsets_ref[other, 1]
    out_ref[...] = pick_columns(pick_rows(across_ref[...], beside_ref[...], row, place_ref[1]), col)


def window_kernel(place_ref, offsets_ref, own_ref, across_ref, beside_ref, out_ref):
    row, col = offsets_ref[place_ref[0], 0], offsets_ref[place_ref[0], 1]
    out_ref[:, :, :HALO] = pick_columns(pick_rows(across_ref[...], beside_ref[...], row, place_ref[1]), col)
    out_ref[:, :, HALO:] = pick_columns(own_ref[...], col)


def position_kernel(
    place_ref,
    offsets_ref,
    tables_ref,
    probe_ref,
    amp_ref,
    own_ref,
    core_ref,
    halo_ref,
    probe_out,
    core_out,
    halo_out,
    waves,
):
    place = place_ref[0]
    row, col = offsets_ref[place, 0], offsets_ref[place, 1]
    line = lax.broadcasted_iota(jnp.int32, (HALO, WIDTH), 0)
    turned = jnp.where(jnp.where(line >= row, 1, 0) == place_ref[1], 0, place_ref[2])

    def window_of(s):
        mine = jnp.where(place == s // 2, 1, 0)
        out = []
        for c in range(2):
            halo = jnp.where(turned == mine, halo_ref[s % 2, c], own_ref[s % 2, c, :HALO])
            core = jnp.where(mine == 1, own_ref[s % 2, c, HALO:], core_ref[s % 2, c])
            out.append(jnp.concatenate([halo, core], axis=0))
        return out

    wave = (probe_ref[0], probe_ref[1])
    for s in range(4):
        if s > 0:
            waves[s - 1, 0], waves[s - 1, 1] = wave
        prod = times(wave, window_of(s))
        if s < 3:
            wave = propagate(prod, tables_ref)
    field = right_mult((fold(prod[0]), fold(prod[1])), tables_ref, FAR_RIGHT)
    field = left_mult(field, tables_ref, FAR_LEFT)
    model = jnp.sqrt(field[0] * field[0] + field[1] * field[1] + 1.0)
    ratio = (model - amp_ref[...]) / model
    grad = (field[0] * ratio, -(field[1] * ratio))
    grad = right_mult(grad, tables_ref, BACK_RIGHT)
    grad = left_mult(grad, tables_ref, BACK_LEFT)
    grad = (fold(grad[0]), fold(grad[1]))
    for s in range(3, -1, -1):
        wave = (waves[s - 1, 0], waves[s - 1, 1]) if s > 0 else (probe_ref[0], probe_ref[1])
        object_grad = times(wave, grad)
        slot = jnp.where(place == s // 2, s % 2, 2 + s % 2)
        for c in range(2):
            value = object_grad[c] if c == 0 else -object_grad[c]
            core_out[slot, c] = value[HALO:]
            start = pl.multiple_of((slot * 2 + c) * HALO, HALO)
            halo_out[pl.ds(start, HALO)] = value[:HALO]
        grad = times(window_of(s), grad)
        if s > 0:
            grad = propagate(grad, tables_ref)
    meta = lax.broadcasted_iota(jnp.int32, (8, WIDTH), 0)
    halo_out[8 * HALO :] = jnp.where(meta == 0, row, col).astype(F32)
    for c in range(2):
        value = grad[c] if c == 0 else -grad[c]
        value = pltpu.roll(value, lax.rem(WIDTH - row, WIDTH), 0)
        value = pltpu.roll(value, lax.rem(WIDTH - col, WIDTH), 1)
        for h in range(2):
            probe_out[c, :, h] = value[:, h * HALF : (h + 1) * HALF].reshape(WIDTH // 8, 8, HALF)


def widen(x, kept):
    left, right = x[..., :HALF], x[..., HALF:]
    return jnp.concatenate([jnp.where(kept, left, 0.0), right, jnp.where(kept, 0.0, left)], axis=-1)


def sum_kernel(place_ref, offsets_ref, core_ref, across_ref, beside_ref, out_ref, *, first):
    col = offsets_ref[place_ref[0], 1]
    lane = lax.broadcasted_iota(jnp.int32, (HALO, HALF), 1)
    line = lax.broadcasted_iota(jnp.int32, (HALO, WIDTH), 0).astype(F32)
    column = lax.broadcasted_iota(jnp.int32, (HALO, HALF), 1).astype(F32)
    sides = []
    odd = place_ref[1]
    for ref, after, turned in ((across_ref, odd, place_ref[2]), (beside_ref, 1 - odd, 0)):
        base = pl.multiple_of(((first + 2 * turned) % 4) * 2 * HALO, HALO)
        row = ref[8 * HALO : 8 * HALO + 1]
        kept = column >= ref[8 * HALO + 1 : 8 * HALO + 2, :HALF]
        mask = jnp.where(line >= row, 1, 0) == after
        sides.append((ref, base, mask, kept))
    for j in range(2):
        for c in range(2):
            total = widen(core_ref[first + j, c], lane >= col)
            for ref, base, mask, kept in sides:
                part = jnp.where(mask, ref[pl.ds(base + (j * 2 + c) * HALO, HALO)], 0.0)
                total = total + widen(part, kept)
            out_ref[j, c] = total


def call(kernel, shapes, smem, vmem, name, scratch=(), flops=0, nbytes=2_000_000):
    single = isinstance(shapes[0], int)
    shapes = (shapes,) if single else shapes
    out = pl.pallas_call(
        kernel,
        out_shape=tuple(jax.ShapeDtypeStruct(shape, F32) for shape in shapes),
        in_specs=[SMEM] * len(smem) + [VMEM] * len(vmem),
        out_specs=(VMEM,) * len(shapes),
        scratch_shapes=scratch,
        compiler_params=pltpu.CompilerParams(vmem_limit_bytes=40 * 1024 * 1024),
        cost_estimate=pl.CostEstimate(flops=flops, bytes_accessed=nbytes, transcendentals=0),
        name=name,
    )(*smem, *vmem)
    return out[0] if single else out


def swap_tile(x, beside):
    slabs, tiles = lax.axis_size("slab"), lax.axis_size("tile")
    pairs = []
    for slab in range(slabs):
        for tile in range(tiles):
            to = (tile + (1 if tile % 2 != beside else -1)) % tiles
            turned = tile // (tiles // 2) != to // (tiles // 2)
            pairs.append((slab * tiles + tile, (slab ^ turned) * tiles + to))
    return lax.ppermute(x, ("slab", "tile"), pairs)


def swap_slab(x):
    return lax.ppermute(x, "slab", [(0, 1), (1, 0)])


def shards(transmission, probe, scan_offsets, amplitudes):
    tables = jnp.asarray(make_tables())
    index = lax.axis_index("slab").astype(jnp.int32)
    half = lax.axis_size("tile") // 2
    within = lax.axis_index("tile").astype(jnp.int32) % half
    turned = (within == 0) | (within == half - 1)
    flags = jnp.stack([index, within % 2, jnp.int32(turned)])
    where = (flags, scan_offsets)
    own = transmission
    part, whole, band = (2, 2, HALO, WIDTH), (2, 2, WIDTH, WIDTH), (2, 2, HALO, COLS)

    core, own = call(core_kernel, (part, band), where, (own,), "core")
    core = swap_slab(core)
    beside, across = swap_tile(own, 1), swap_tile(own, 0)
    rolled = call(roll_probe_kernel, (2, WIDTH, WIDTH), where, (probe,), "roll")
    amp = call(amp_kernel, (WIDTH, WIDTH), where, (amplitudes,), "amp")
    halo = swap_slab(call(halo_kernel, part, where, (across, beside), "halo"))
    windows = call(window_kernel, whole, where, (own, across, beside), "window")

    tiles = (2, WIDTH // 8, 2, 8, HALF)
    probe_term, cores, halos = call(
        position_kernel,
        (tiles, (4, 2, HALO, WIDTH), (8 * HALO + 8, WIDTH)),
        where,
        (tables, rolled, amp, windows, core, halo),
        "position",
        scratch=[pltpu.VMEM((3, 2, WIDTH, WIDTH), F32)],
        flops=3_300_000_000,
        nbytes=10_000_000,
    )
    sides = (cores, swap_tile(halos, 0), swap_tile(halos, 1))
    oth_sum = call(functools.partial(sum_kernel, first=2), band, where, sides, "sum_other")
    got = swap_slab(oth_sum)
    own_sum = call(functools.partial(sum_kernel, first=0), band, where, sides, "sum_own")
    axes = ("slab", "tile")
    devices = lax.axis_size(axes)
    parts = probe_term.reshape(devices, 8, HALF)
    mine = jnp.sum(lax.all_to_all(parts, axes, 0, 0, tiled=True), axis=0)
    spread = jnp.broadcast_to(mine[None], (devices, 8, HALF))
    probe_grad = lax.all_to_all(spread, axes, 0, 0, tiled=True).reshape(tiles)
    probe_grad = probe_grad.transpose(0, 1, 3, 2, 4).reshape(probe.shape)

    object_grad = own_sum + got
    return object_grad, probe_grad


def solution(mesh):
    placed = (P("slab", None, "tile", None), P(), P("tile", None), P("tile", None, None))
    return jax.shard_map(
        shards,
        mesh=mesh,
        in_specs=placed,
        out_specs=(P("slab", None, "tile", None), P()),
        check_vma=False,
    )
```

```python
import functools

import jax
import jax.numpy as jnp
import numpy as np
from jax import lax
from jax.experimental import pallas as pl
from jax.experimental.pallas import tpu as pltpu
from jax.sharding import PartitionSpec as P

WIDTH = 256
HALF = 128
HALO = 128
COLS = 384
PROP_STRENGTH = 12.0
BF16 = jnp.bfloat16
F32 = jnp.float32
VMEM = pl.BlockSpec(memory_space=pltpu.VMEM)
SMEM = pl.BlockSpec(memory_space=pltpu.SMEM)
HBM = pl.BlockSpec(memory_space=pltpu.HBM)


def high_low(table):
    table = table.astype(np.float32)
    high = table.astype(jnp.bfloat16)
    low = (table - high.astype(np.float32)).astype(jnp.bfloat16)
    return np.stack([high, low])


def on_right(m):
    return high_low(np.block([[m.real, m.imag], [-m.imag, m.real]]))


def on_left(m):
    return high_low(np.block([[m.real, -m.imag], [m.imag, m.real]]))


def make_tables():
    index = np.arange(WIDTH)
    dft = np.exp(-2j * np.pi / WIDTH * (index[:, None] * index[None, :] % WIDTH)) / np.sqrt(WIDTH)
    freq = ((index + WIDTH // 2) % WIDTH - WIDTH // 2) / WIDTH
    phase = np.exp(-1j * PROP_STRENGTH * freq**2)
    prop = dft.conj() @ (phase[:, None] * dft)
    far = phase[:, None] * dft
    p, q = prop[:HALF, :HALF], prop[:HALF, HALF:]
    props = ((p + q) / 2, (p - q) / 2)
    fars = (far[0::2, :HALF], far[1::2, :HALF])
    return np.stack(
        [
            np.stack([on_right(m) for m in props]),
            np.stack([on_left(m) for m in props]),
            np.stack([on_right(m.T) for m in fars]),
            np.stack([on_left(m) for m in fars]),
            np.stack([on_right(m) for m in fars]),
            np.stack([on_left(m.T) for m in fars]),
        ]
    )


PROP_RIGHT, PROP_LEFT, FAR_RIGHT, FAR_LEFT, BACK_RIGHT, BACK_LEFT = range(6)


def split(x):
    high = x.astype(BF16)
    low = (x - high.astype(F32)).astype(BF16)
    return high, low


def dot(a, b):
    return jnp.dot(a, b, preferred_element_type=F32)


def fold(x):
    x = jnp.concatenate([x[:HALF] + x[HALF:], x[:HALF] - x[HALF:]], axis=0)
    return jnp.concatenate([x[:, :HALF] + x[:, HALF:], x[:, :HALF] - x[:, HALF:]], axis=1)


def right_mult(x, tables, which):
    re, im = [], []
    for h in range(2):
        part = slice(h * HALF, (h + 1) * HALF)
        high, low = split(jnp.concatenate([x[0][:, part], x[1][:, part]], axis=1))
        th, tl = tables[which, h, 0], tables[which, h, 1]
        out = dot(jnp.concatenate([high, low, high], axis=1), jnp.concatenate([th, th, tl], axis=0))
        re.append(out[:, :HALF])
        im.append(out[:, HALF:])
    return jnp.concatenate(re, axis=1), jnp.concatenate(im, axis=1)


def left_mult(x, tables, which):
    re, im = [], []
    for h in range(2):
        part = slice(h * HALF, (h + 1) * HALF)
        high, low = split(jnp.concatenate([x[0][part], x[1][part]], axis=0))
        th, tl = tables[which, h, 0], tables[which, h, 1]
        out = dot(jnp.concatenate([th, th, tl], axis=1), jnp.concatenate([high, low, high], axis=0))
        re.append(out[:HALF])
        im.append(out[HALF:])
    return jnp.concatenate(re, axis=0), jnp.concatenate(im, axis=0)


def propagate(x, tables):
    y = right_mult((fold(x[0]), fold(x[1])), tables, PROP_RIGHT)
    y = left_mult(y, tables, PROP_LEFT)
    return fold(y[0]), fold(y[1])


def times(a, b):
    return a[0] * b[0] - a[1] * b[1], a[0] * b[1] + a[1] * b[0]


def pick_columns(x, col):
    lane = lax.broadcasted_iota(jnp.int32, x.shape[:-1] + (HALF,), len(x.shape) - 1)
    left = jnp.where(lane >= col, x[..., :HALF], x[..., 2 * HALF :])
    return jnp.concatenate([left, x[..., HALF : 2 * HALF]], axis=-1)


def pick_rows(across, beside, row, odd):
    line = lax.broadcasted_iota(jnp.int32, across.shape, len(across.shape) - 2)
    return jnp.where(jnp.where(line >= row, 1, 0) == odd, beside, across)


def roll_probe_kernel(place_ref, offsets_ref, probe_ref, out_ref):
    row, col = offsets_ref[place_ref[0], 0], offsets_ref[place_ref[0], 1]
    for c in range(2):
        out_ref[c] = pltpu.roll(pltpu.roll(probe_ref[c], row, 0), col, 1)


def core_kernel(place_ref, offsets_ref, own_ref, out_ref):
    col = offsets_ref[1 - place_ref[0], 1]
    out_ref[...] = pick_columns(own_ref[...], col)


def amp_kernel(place_ref, offsets_ref, amp_ref, out_ref):
    x = amp_ref[place_ref[0]]
    line = lax.broadcasted_iota(jnp.int32, (WIDTH, WIDTH), 0)
    lane = lax.broadcasted_iota(jnp.int32, (WIDTH, WIDTH), 1)
    rows = jnp.where(lane == 2 * (line % HALF) + line // HALF, 1.0, 0.0).astype(BF16)
    cols = jnp.where(line == 2 * (lane % HALF) + lane // HALF, 1.0, 0.0).astype(BF16)

    def parts(value):
        high, rest = split(value)
        return high, rest, (value - high.astype(F32) - rest.astype(F32)).astype(BF16)

    x = sum(dot(rows, part) for part in parts(x))
    out_ref[...] = sum(dot(part, cols) for part in parts(x))


def halo_kernel(place_ref, offsets_ref, across_ref, beside_ref, out_ref):
    other = 1 - place_ref[0]
    row, col = offsets_ref[other, 0], offsets_ref[other, 1]
    out_ref[...] = pick_columns(pick_rows(across_ref[...], beside_ref[...], row, place_ref[1]), col)


def window_kernel(place_ref, offsets_ref, own_ref, across_ref, beside_ref, out_ref):
    row, col = offsets_ref[place_ref[0], 0], offsets_ref[place_ref[0], 1]
    out_ref[:, :, :HALO] = pick_columns(pick_rows(across_ref[...], beside_ref[...], row, place_ref[1]), col)
    out_ref[:, :, HALO:] = pick_columns(own_ref[...], col)


def position_kernel(
    place_ref,
    offsets_ref,
    tables_ref,
    probe_ref,
    amp_ref,
    own_ref,
    core_ref,
    halo_ref,
    keep_out,
    send_out,
    core_out,
    halo_out,
    waves,
    halos,
    sems,
):
    place = place_ref[0]
    row, col = offsets_ref[place, 0], offsets_ref[place, 1]
    line = lax.broadcasted_iota(jnp.int32, (HALO, WIDTH), 0)
    turned = jnp.where(jnp.where(line >= row, 1, 0) == place_ref[1], 0, place_ref[2])

    def window_of(s):
        mine = jnp.where(place == s // 2, 1, 0)
        out = []
        for c in range(2):
            halo = jnp.where(turned == mine, halo_ref[s % 2, c], own_ref[s % 2, c, :HALO])
            core = jnp.where(mine == 1, own_ref[s % 2, c, HALO:], core_ref[s % 2, c])
            out.append(jnp.concatenate([halo, core], axis=0))
        return out

    wave = (probe_ref[0], probe_ref[1])
    for s in range(4):
        if s > 0:
            waves[s - 1, 0], waves[s - 1, 1] = wave
        prod = times(wave, window_of(s))
        if s < 3:
            wave = propagate(prod, tables_ref)
    field = right_mult((fold(prod[0]), fold(prod[1])), tables_ref, FAR_RIGHT)
    field = left_mult(field, tables_ref, FAR_LEFT)
    model = jnp.sqrt(field[0] * field[0] + field[1] * field[1] + 1.0)
    ratio = (model - amp_ref[...]) / model
    grad = (field[0] * ratio, -(field[1] * ratio))
    grad = right_mult(grad, tables_ref, BACK_RIGHT)
    grad = left_mult(grad, tables_ref, BACK_LEFT)
    grad = (fold(grad[0]), fold(grad[1]))
    copies = []
    for s in range(3, -1, -1):
        wave = (waves[s - 1, 0], waves[s - 1, 1]) if s > 0 else (probe_ref[0], probe_ref[1])
        object_grad = times(wave, grad)
        slot = jnp.where(place == s // 2, s % 2, 2 + s % 2)
        for c in range(2):
            value = object_grad[c] if c == 0 else -object_grad[c]
            core_out[slot, c] = value[HALO:]
            halos[slot, pl.ds(c * HALO, HALO)] = value[:HALO]
        start = pl.multiple_of(slot * 2 * HALO, HALO)
        copy = pltpu.make_async_copy(halos.at[slot], halo_out.at[pl.ds(start, 2 * HALO)], sems.at[s])
        copy.start()
        copies.append(copy)
        grad = times(window_of(s), grad)
        if s > 0:
            grad = propagate(grad, tables_ref)
    meta = lax.broadcasted_iota(jnp.int32, (8, WIDTH), 0)
    halos[4, :8] = jnp.where(meta == 0, row, col).astype(F32)
    copy = pltpu.make_async_copy(halos.at[4, :8], halo_out.at[8 * HALO :], sems.at[4])
    copy.start()
    copies.append(copy)
    odd = place_ref[1]
    value = [grad[0], -grad[1]]
    for c in range(2):
        value[c] = pltpu.roll(value[c], lax.rem(WIDTH - row, WIDTH), 0)
        value[c] = pltpu.roll(value[c], lax.rem(WIDTH - col, WIDTH), 1)
    for ref, which in ((keep_out, odd), (send_out, 1 - odd)):
        part = jnp.where(which == 0, value[0], value[1])
        for h in range(2):
            ref[:, h] = part[:, h * HALF : (h + 1) * HALF].reshape(WIDTH // 8, 8, HALF)
    for copy in copies:
        copy.wait()


def widen(x, kept):
    left, right = x[..., :HALF], x[..., HALF:]
    return jnp.concatenate([jnp.where(kept, left, 0.0), right, jnp.where(kept, 0.0, left)], axis=-1)


def add_halos(place_ref, offsets_ref, core_ref, across_ref, beside_ref, out_ref, first, extra=None):
    col = offsets_ref[place_ref[0], 1]
    lane = lax.broadcasted_iota(jnp.int32, (HALO, HALF), 1)
    line = lax.broadcasted_iota(jnp.int32, (HALO, WIDTH), 0).astype(F32)
    column = lax.broadcasted_iota(jnp.int32, (HALO, HALF), 1).astype(F32)
    sides = []
    odd = place_ref[1]
    for ref, after, turned in ((across_ref, odd, place_ref[2]), (beside_ref, 1 - odd, 0)):
        base = pl.multiple_of(((first + 2 * turned) % 4) * 2 * HALO, HALO)
        row = ref[8 * HALO : 8 * HALO + 1]
        kept = column >= ref[8 * HALO + 1 : 8 * HALO + 2, :HALF]
        mask = jnp.where(line >= row, 1, 0) == after
        sides.append((ref, base, mask, kept))
    for j in range(2):
        for c in range(2):
            total = widen(core_ref[first + j, c], lane >= col)
            for ref, base, mask, kept in sides:
                part = jnp.where(mask, ref[pl.ds(base + (j * 2 + c) * HALO, HALO)], 0.0)
                total = total + widen(part, kept)
            out_ref[j, c] = total if extra is None else total + extra[j, c]


def add_kernel(keep_ref, got_ref, out_ref):
    out_ref[...] = keep_ref[...] + got_ref[...]


def sum_kernel(
    place_ref, offsets_ref, core_ref, across_ref, beside_ref, parts_ref, sum_out, spread_out
):
    add_halos(place_ref, offsets_ref, core_ref, across_ref, beside_ref, sum_out, 2)
    total = jnp.sum(parts_ref[...], axis=0, keepdims=True)
    spread_out[...] = jnp.broadcast_to(total, spread_out.shape)


def finish_kernel(
    place_ref,
    offsets_ref,
    core_ref,
    across_ref,
    beside_ref,
    swapped_ref,
    keep_ref,
    got_ref,
    object_out,
    probe_out,
):
    add_halos(
        place_ref, offsets_ref, core_ref, across_ref, beside_ref, object_out, 0, swapped_ref
    )
    odd = place_ref[1]
    for ref, which in ((keep_ref, odd), (got_ref, 1 - odd)):
        for h in range(2):
            probe_out[which, :, h * HALF : (h + 1) * HALF] = ref[:, h].reshape(WIDTH, HALF)


def call(kernel, shapes, smem, vmem, name, scratch=(), flops=0, nbytes=2_000_000, outs=None):
    single = isinstance(shapes[0], int)
    shapes = (shapes,) if single else shapes
    out = pl.pallas_call(
        kernel,
        out_shape=tuple(jax.ShapeDtypeStruct(shape, F32) for shape in shapes),
        in_specs=[SMEM] * len(smem) + [VMEM] * len(vmem),
        out_specs=outs or (VMEM,) * len(shapes),
        scratch_shapes=scratch,
        compiler_params=pltpu.CompilerParams(vmem_limit_bytes=40 * 1024 * 1024),
        cost_estimate=pl.CostEstimate(flops=flops, bytes_accessed=nbytes, transcendentals=0),
        name=name,
    )(*smem, *vmem)
    return out[0] if single else out


def swap_tile(x, beside):
    slabs, tiles = lax.axis_size("slab"), lax.axis_size("tile")
    pairs = []
    for slab in range(slabs):
        for tile in range(tiles):
            to = (tile + (1 if tile % 2 != beside else -1)) % tiles
            turned = tile // (tiles // 2) != to // (tiles // 2)
            pairs.append((slab * tiles + tile, (slab ^ turned) * tiles + to))
    return lax.ppermute(x, ("slab", "tile"), pairs)


def swap_core(x):
    count = lax.axis_size("tile")
    return lax.ppermute(x, "tile", [(i, i ^ 1) for i in range(count)])


def among_chips(x):
    axes = ("slab", "tile")
    devices = lax.axis_size(axes)
    groups = [list(range(core, devices, 2)) for core in range(2)]
    return lax.all_to_all(x, axes, 0, 0, tiled=True, axis_index_groups=groups)


def swap_slab(x):
    return lax.ppermute(x, "slab", [(0, 1), (1, 0)])


def shards(transmission, probe, scan_offsets, amplitudes):
    tables = jnp.asarray(make_tables())
    index = lax.axis_index("slab").astype(jnp.int32)
    half = lax.axis_size("tile") // 2
    within = lax.axis_index("tile").astype(jnp.int32) % half
    turned = (within == 0) | (within == half - 1)
    flags = jnp.stack([index, within % 2, jnp.int32(turned)])
    where = (flags, scan_offsets)
    own = transmission
    part, whole, band = (2, 2, HALO, WIDTH), (2, 2, WIDTH, WIDTH), (2, 2, HALO, COLS)

    core = swap_slab(call(core_kernel, part, where, (own,), "core"))
    beside, across = swap_tile(own, 1), swap_tile(own, 0)
    rolled = call(roll_probe_kernel, (2, WIDTH, WIDTH), where, (probe,), "roll")
    amp = call(amp_kernel, (WIDTH, WIDTH), where, (amplitudes,), "amp")
    halo = swap_slab(call(halo_kernel, part, where, (across, beside), "halo"))
    windows = call(window_kernel, whole, where, (own, across, beside), "window")

    tiles = (WIDTH // 8, 2, 8, HALF)
    keep, send, cores, halos = call(
        position_kernel,
        (tiles, tiles, (4, 2, HALO, WIDTH), (8 * HALO + 8, WIDTH)),
        where,
        (tables, rolled, amp, windows, core, halo),
        "position",
        scratch=[
            pltpu.VMEM((3, 2, WIDTH, WIDTH), F32),
            pltpu.VMEM((5, 2 * HALO, WIDTH), F32),
            pltpu.SemaphoreType.DMA((5,)),
        ],
        flops=3_300_000_000,
        nbytes=10_000_000,
        outs=(VMEM, VMEM, VMEM, HBM),
    )
    sides = (cores, swap_tile(halos, 0), swap_tile(halos, 1))
    parts = (WIDTH // 4, 8, HALF)
    kept = call(add_kernel, tiles, (), (keep, swap_core(send)), "add").reshape(parts)
    kept = among_chips(kept)
    oth_sum, spread = call(sum_kernel, (band, parts), where, sides + (kept,), "sum")
    got = swap_slab(oth_sum)
    kept = among_chips(spread)
    object_grad, probe_grad = call(
        finish_kernel,
        (band, probe.shape),
        where,
        sides + (got, kept.reshape(tiles), swap_core(kept).reshape(tiles)),
        "finish",
    )
    return object_grad, probe_grad


def solution(mesh):
    placed = (P("slab", None, "tile", None), P(), P("tile", None), P("tile", None, None))
    return jax.shard_map(
        shards,
        mesh=mesh,
        in_specs=placed,
        out_specs=(P("slab", None, "tile", None), P()),
        check_vma=False,
    )
```

```python
import functools

import jax
import jax.numpy as jnp
import numpy as np
from jax import lax
from jax.experimental import pallas as pl
from jax.experimental.pallas import tpu as pltpu
from jax.sharding import PartitionSpec as P

WIDTH = 256
HALF = 128
HALO = 128
COLS = 384
PROP_STRENGTH = 12.0
BF16 = jnp.bfloat16
F32 = jnp.float32
VMEM = pl.BlockSpec(memory_space=pltpu.VMEM)
SMEM = pl.BlockSpec(memory_space=pltpu.SMEM)
HBM = pl.BlockSpec(memory_space=pltpu.HBM)


def high_low(table):
    table = table.astype(np.float32)
    high = table.astype(jnp.bfloat16)
    low = (table - high.astype(np.float32)).astype(jnp.bfloat16)
    return np.stack([high, low])


def on_right(m):
    return high_low(np.block([[m.real, m.imag], [-m.imag, m.real]]))


def on_left(m):
    return high_low(np.block([[m.real, -m.imag], [m.imag, m.real]]))


def make_tables():
    index = np.arange(WIDTH)
    dft = np.exp(-2j * np.pi / WIDTH * (index[:, None] * index[None, :] % WIDTH)) / np.sqrt(WIDTH)
    freq = ((index + WIDTH // 2) % WIDTH - WIDTH // 2) / WIDTH
    phase = np.exp(-1j * PROP_STRENGTH * freq**2)
    prop = dft.conj() @ (phase[:, None] * dft)
    far = phase[:, None] * dft
    p, q = prop[:HALF, :HALF], prop[:HALF, HALF:]
    props = ((p + q) / 2, (p - q) / 2)
    fars = (far[0::2, :HALF], far[1::2, :HALF])
    return np.stack(
        [
            np.stack([on_right(m) for m in props]),
            np.stack([on_left(m) for m in props]),
            np.stack([on_right(m.T) for m in fars]),
            np.stack([on_left(m) for m in fars]),
            np.stack([on_right(m) for m in fars]),
            np.stack([on_left(m.T) for m in fars]),
        ]
    )


PROP_RIGHT, PROP_LEFT, FAR_RIGHT, FAR_LEFT, BACK_RIGHT, BACK_LEFT = range(6)


def split(x):
    high = x.astype(BF16)
    low = (x - high.astype(F32)).astype(BF16)
    return high, low


def dot(a, b):
    return jnp.dot(a, b, preferred_element_type=F32)


def fold(x):
    x = jnp.concatenate([x[:HALF] + x[HALF:], x[:HALF] - x[HALF:]], axis=0)
    return jnp.concatenate([x[:, :HALF] + x[:, HALF:], x[:, :HALF] - x[:, HALF:]], axis=1)


def right_mult(x, tables, which):
    re, im = [], []
    for h in range(2):
        part = slice(h * HALF, (h + 1) * HALF)
        high, low = split(jnp.concatenate([x[0][:, part], x[1][:, part]], axis=1))
        th, tl = tables[which, h, 0], tables[which, h, 1]
        out = dot(jnp.concatenate([high, low, high], axis=1), jnp.concatenate([th, th, tl], axis=0))
        re.append(out[:, :HALF])
        im.append(out[:, HALF:])
    return jnp.concatenate(re, axis=1), jnp.concatenate(im, axis=1)


def left_mult(x, tables, which):
    re, im = [], []
    for h in range(2):
        part = slice(h * HALF, (h + 1) * HALF)
        high, low = split(jnp.concatenate([x[0][part], x[1][part]], axis=0))
        th, tl = tables[which, h, 0], tables[which, h, 1]
        out = dot(jnp.concatenate([th, th, tl], axis=1), jnp.concatenate([high, low, high], axis=0))
        re.append(out[:HALF])
        im.append(out[HALF:])
    return jnp.concatenate(re, axis=0), jnp.concatenate(im, axis=0)


def propagate(x, tables):
    y = right_mult((fold(x[0]), fold(x[1])), tables, PROP_RIGHT)
    y = left_mult(y, tables, PROP_LEFT)
    return fold(y[0]), fold(y[1])


def times(a, b):
    return a[0] * b[0] - a[1] * b[1], a[0] * b[1] + a[1] * b[0]


def here():
    half = lax.axis_size("tile") // 2
    within = lax.axis_index("tile") % half
    turned = jnp.where((within == 0) | (within == half - 1), 1, 0)
    return lax.axis_index("slab"), within % 2, turned


def masks(info_ref, which):
    row = jnp.broadcast_to(info_ref[2 * which : 2 * which + 1], (HALO, HALF))
    col = jnp.broadcast_to(info_ref[2 * which + 1 : 2 * which + 2], (HALO, HALF))
    line = lax.broadcasted_iota(jnp.int32, (HALO, HALF), 0)
    lane = lax.broadcasted_iota(jnp.int32, (HALO, HALF), 1)
    return jnp.where(line >= row, 1, 0) == here()[1], lane >= col


def columns_of(x, kept):
    return jnp.where(kept, x(0), x(2)), x(1)


def halo_of(across_ref, beside_ref, at, from_beside, kept):
    def column(i):
        cols = slice(i * HALF, (i + 1) * HALF)
        return jnp.where(from_beside, beside_ref[at + (slice(None), cols)], across_ref[at + (slice(None), cols)])

    return columns_of(column, kept)


def roll_probe_kernel(place_ref, offsets_ref, probe_ref, out_ref):
    row, col = offsets_ref[place_ref[0], 0], offsets_ref[place_ref[0], 1]
    for c in range(2):
        out_ref[c] = pltpu.roll(pltpu.roll(probe_ref[c], row, 0), col, 1)


def core_kernel(offsets_ref, own_ref, out_ref, offsets, cols, sems, out_sems):
    load = pltpu.make_async_copy(offsets_ref, offsets, sems.at[4])
    load.start()
    loads = [pltpu.make_async_copy(own_ref.at[i // 2, i % 2], cols.at[i], sems.at[i]) for i in range(4)]
    for copy in loads:
        copy.start()
    load.wait()
    lane = lax.broadcasted_iota(jnp.int32, (HALO, HALF), 1)
    kept = lane >= offsets[1 - lax.axis_index("slab"), 1]
    stores = []
    for i in range(4):
        loads[i].wait()
        cols[i, :, :HALF] = jnp.where(kept, cols[i, :, :HALF], cols[i, :, 2 * HALF :])
        store = pltpu.make_async_copy(cols.at[i, :, :WIDTH], out_ref.at[i // 2, i % 2], out_sems.at[i])
        store.start()
        stores.append(store)
    for copy in stores:
        copy.wait()


def amp_kernel(place_ref, offsets_ref, amp_ref, out_ref):
    x = amp_ref[place_ref[0]]
    line = lax.broadcasted_iota(jnp.int32, (WIDTH, WIDTH), 0)
    lane = lax.broadcasted_iota(jnp.int32, (WIDTH, WIDTH), 1)
    rows = jnp.where(lane == 2 * (line % HALF) + line // HALF, 1.0, 0.0).astype(BF16)
    cols = jnp.where(line == 2 * (lane % HALF) + lane // HALF, 1.0, 0.0).astype(BF16)

    def parts(value):
        high, rest = split(value)
        return high, rest, (value - high.astype(F32) - rest.astype(F32)).astype(BF16)

    x = sum(dot(rows, part) for part in parts(x))
    out_ref[...] = sum(dot(part, cols) for part in parts(x))


def halo_kernel(info_ref, across_ref, beside_ref, out_ref):
    from_beside, kept = masks(info_ref, 1)
    for j in range(2):
        for c in range(2):
            left, right = halo_of(across_ref, beside_ref, (j, c), from_beside, kept)
            out_ref[j, c, :, :HALF] = left
            out_ref[j, c, :, HALF:] = right


def window_kernel(info_ref, own_ref, across_ref, beside_ref, out_ref):
    from_beside, kept = masks(info_ref, 0)
    for j in range(2):
        for c in range(2):
            left, right = halo_of(across_ref, beside_ref, (j, c), from_beside, kept)
            out_ref[j, c, :HALO, :HALF] = left
            out_ref[j, c, :HALO, HALF:] = right
            left, right = columns_of(lambda i: own_ref[j, c, :, i * HALF : (i + 1) * HALF], kept)
            out_ref[j, c, HALO:, :HALF] = left
            out_ref[j, c, HALO:, HALF:] = right


def position_kernel(
    info_ref,
    offsets_ref,
    tables_ref,
    probe_ref,
    amp_ref,
    own_ref,
    core_ref,
    halo_ref,
    keep_out,
    send_out,
    core_out,
    halo_out,
    waves,
    halos,
    offsets,
    sems,
):
    place, odd, turned = here()
    load = pltpu.make_async_copy(offsets_ref, offsets, sems.at[5])
    load.start()
    from_beside = masks(info_ref, 0)[0]
    turned = jnp.where(jnp.concatenate([from_beside, from_beside], axis=1), 0, turned)

    def window_of(s):
        mine = jnp.where(place == s // 2, 1, 0)
        out = []
        for c in range(2):
            halo = jnp.where(turned == mine, halo_ref[s % 2, c], own_ref[s % 2, c, :HALO])
            core = jnp.where(mine == 1, own_ref[s % 2, c, HALO:], core_ref[s % 2, c])
            out.append(jnp.concatenate([halo, core], axis=0))
        return out

    wave = (probe_ref[0], probe_ref[1])
    for s in range(4):
        if s > 0:
            waves[s - 1, 0], waves[s - 1, 1] = wave
        prod = times(wave, window_of(s))
        if s < 3:
            wave = propagate(prod, tables_ref)
    field = right_mult((fold(prod[0]), fold(prod[1])), tables_ref, FAR_RIGHT)
    field = left_mult(field, tables_ref, FAR_LEFT)
    model = jnp.sqrt(field[0] * field[0] + field[1] * field[1] + 1.0)
    ratio = (model - amp_ref[...]) / model
    grad = (field[0] * ratio, -(field[1] * ratio))
    grad = right_mult(grad, tables_ref, BACK_RIGHT)
    grad = left_mult(grad, tables_ref, BACK_LEFT)
    grad = (fold(grad[0]), fold(grad[1]))
    copies = []
    for s in range(3, -1, -1):
        wave = (waves[s - 1, 0], waves[s - 1, 1]) if s > 0 else (probe_ref[0], probe_ref[1])
        object_grad = times(wave, grad)
        slot = jnp.where(place == s // 2, s % 2, 2 + s % 2)
        for c in range(2):
            value = object_grad[c] if c == 0 else -object_grad[c]
            core_out[slot, c] = value[HALO:]
            halos[slot, pl.ds(c * HALO, HALO)] = value[:HALO]
        start = pl.multiple_of(slot * 2 * HALO, HALO)
        copy = pltpu.make_async_copy(halos.at[slot], halo_out.at[pl.ds(start, 2 * HALO)], sems.at[s])
        copy.start()
        copies.append(copy)
        grad = times(window_of(s), grad)
        if s > 0:
            grad = propagate(grad, tables_ref)
    meta = info_ref[...].astype(F32)
    halos[4, :8] = jnp.concatenate([meta, meta], axis=1)
    copy = pltpu.make_async_copy(halos.at[4, :8], halo_out.at[8 * HALO :], sems.at[4])
    copy.start()
    copies.append(copy)
    load.wait()
    row, col = offsets[place, 0], offsets[place, 1]
    value = [grad[0], -grad[1]]
    for c in range(2):
        value[c] = pltpu.roll(value[c], lax.rem(WIDTH - row, WIDTH), 0)
        value[c] = pltpu.roll(value[c], lax.rem(WIDTH - col, WIDTH), 1)
    for ref, which in ((keep_out, odd), (send_out, 1 - odd)):
        part = jnp.where(which == 0, value[0], value[1])
        for h in range(2):
            ref[:, h] = part[:, h * HALF : (h + 1) * HALF].reshape(WIDTH // 8, 8, HALF)
    for copy in copies:
        copy.wait()


def widen(x, kept):
    left, right = x[..., :HALF], x[..., HALF:]
    return jnp.concatenate([jnp.where(kept, left, 0.0), right, jnp.where(kept, 0.0, left)], axis=-1)


def add_halos(info_ref, core_ref, across_ref, beside_ref, out_ref, first, extra=None):
    _, odd, turned = here()
    own_kept = masks(info_ref, 0)[1]
    line = lax.broadcasted_iota(jnp.int32, (HALO, WIDTH), 0).astype(F32)
    column = lax.broadcasted_iota(jnp.int32, (HALO, HALF), 1).astype(F32)
    sides = []
    for ref, after, shift in ((across_ref, odd, turned), (beside_ref, 1 - odd, 0)):
        base = pl.multiple_of(((first + 2 * shift) % 4) * 2 * HALO, HALO)
        row = ref[8 * HALO : 8 * HALO + 1]
        kept = column >= ref[8 * HALO + 1 : 8 * HALO + 2, :HALF]
        mask = jnp.where(line >= row, 1, 0) == after
        sides.append((ref, base, mask, kept))
    for j in range(2):
        for c in range(2):
            total = widen(core_ref[first + j, c], own_kept)
            for ref, base, mask, kept in sides:
                part = jnp.where(mask, ref[pl.ds(base + (j * 2 + c) * HALO, HALO)], 0.0)
                total = total + widen(part, kept)
            out_ref[j, c] = total if extra is None else total + extra[j, c]


def add_kernel(keep_ref, got_ref, out_ref):
    out_ref[...] = keep_ref[...] + got_ref[...]


def reduce_kernel(parts_ref, out_ref):
    out_ref[...] = jnp.sum(parts_ref[...], axis=0)


def total_kernel(first_ref, second_ref, third_ref, fourth_ref, out_ref):
    total = (first_ref[...] + second_ref[...]) + (third_ref[...] + fourth_ref[...])
    out_ref[...] = jnp.broadcast_to(total[None], out_ref.shape)


def sum_kernel(info_ref, core_ref, across_ref, beside_ref, after_ref, out_ref):
    add_halos(info_ref, core_ref, across_ref, beside_ref, out_ref, 2)


def finish_kernel(
    info_ref,
    core_ref,
    across_ref,
    beside_ref,
    swapped_ref,
    keep_ref,
    got_ref,
    object_out,
    probe_out,
):
    add_halos(info_ref, core_ref, across_ref, beside_ref, object_out, 0, swapped_ref)
    odd = here()[1]
    for ref, which in ((keep_ref, odd), (got_ref, 1 - odd)):
        for h in range(2):
            probe_out[which, :, h * HALF : (h + 1) * HALF] = ref[:, h].reshape(WIDTH, HALF)


def call(kernel, shapes, smem, vmem, name, scratch=(), flops=0, nbytes=2_000_000, ins=None, outs=None, vmem_limit=40):
    single = isinstance(shapes[0], int)
    shapes = (shapes,) if single else shapes
    out = pl.pallas_call(
        kernel,
        out_shape=tuple(jax.ShapeDtypeStruct(shape, F32) for shape in shapes),
        in_specs=[SMEM] * len(smem) + list(ins or [VMEM] * len(vmem)),
        out_specs=outs or (VMEM,) * len(shapes),
        scratch_shapes=scratch,
        compiler_params=pltpu.CompilerParams(vmem_limit_bytes=vmem_limit * 1024 * 1024),
        cost_estimate=pl.CostEstimate(flops=flops, bytes_accessed=nbytes, transcendentals=0),
        name=name,
    )(*smem, *vmem)
    return out[0] if single else out


def swap_tile(x, beside):
    slabs, tiles = lax.axis_size("slab"), lax.axis_size("tile")
    pairs = []
    for slab in range(slabs):
        for tile in range(tiles):
            to = (tile + (1 if tile % 2 != beside else -1)) % tiles
            turned = tile // (tiles // 2) != to // (tiles // 2)
            pairs.append((slab * tiles + tile, (slab ^ turned) * tiles + to))
    return lax.ppermute(x, ("slab", "tile"), pairs)


def swap_core(x):
    count = lax.axis_size("tile")
    return lax.ppermute(x, "tile", [(i, i ^ 1) for i in range(count)])


def among_columns(x):
    slabs, tiles = lax.axis_size("slab"), lax.axis_size("tile")
    half = tiles // 2
    planes = [slab * tiles + far * half for slab in range(slabs) for far in range(2)]
    groups = [[plane + i for i in range(core, half, 2)] for plane in planes for core in range(2)]
    return lax.all_to_all(x, ("slab", "tile"), 0, 0, tiled=True, axis_index_groups=groups)


def along_z(x, by):
    slabs, tiles = lax.axis_size("slab"), lax.axis_size("tile")
    half = tiles // 2
    pairs = []
    for z in range(2 * slabs):
        to = (z + by) % (2 * slabs)
        for i in range(half):
            source = z % slabs * tiles + z // slabs * half + i
            pairs.append((source, to % slabs * tiles + to // slabs * half + i))
    return lax.ppermute(x, ("slab", "tile"), pairs)


def swap_slab(x):
    return lax.ppermute(x, "slab", [(0, 1), (1, 0)])


def shards(transmission, probe, scan_offsets, amplitudes):
    tables = jnp.asarray(make_tables())
    index = lax.axis_index("slab").astype(jnp.int32)
    where = (index.reshape(1), scan_offsets)
    info = jnp.where(index == 0, scan_offsets, scan_offsets[::-1]).reshape(4, 1)
    info = jnp.broadcast_to(jnp.concatenate([info, info]), (8, HALF))
    own = transmission
    part, whole, band = (2, 2, HALO, WIDTH), (2, 2, WIDTH, WIDTH), (2, 2, HALO, COLS)

    core = call(
        core_kernel,
        part,
        (),
        (scan_offsets, own),
        "core",
        scratch=[
            pltpu.SMEM((2, 2), jnp.int32),
            pltpu.VMEM((4, HALO, COLS), F32),
            pltpu.SemaphoreType.DMA((5,)),
            pltpu.SemaphoreType.DMA((4,)),
        ],
        ins=(HBM, HBM),
        outs=(HBM,),
        vmem_limit=60,
    )
    core = swap_slab(core)
    beside, across = swap_tile(own, 1), swap_tile(own, 0)
    rolled = call(roll_probe_kernel, (2, WIDTH, WIDTH), where, (probe,), "roll")
    amp = call(amp_kernel, (WIDTH, WIDTH), where, (amplitudes,), "amp")
    halo = swap_slab(call(halo_kernel, part, (), (info, across, beside), "halo"))
    windows = call(window_kernel, whole, (), (info, own, across, beside), "window")

    tiles = (WIDTH // 8, 2, 8, HALF)
    keep, send, cores, halos = call(
        position_kernel,
        (tiles, tiles, (4, 2, HALO, WIDTH), (8 * HALO + 8, WIDTH)),
        (),
        (info, scan_offsets, tables, rolled, amp, windows, core, halo),
        "position",
        scratch=[
            pltpu.VMEM((3, 2, WIDTH, WIDTH), F32),
            pltpu.VMEM((5, 2 * HALO, WIDTH), F32),
            pltpu.SMEM((2, 2), jnp.int32),
            pltpu.SemaphoreType.DMA((6,)),
        ],
        ins=(VMEM, HBM) + (VMEM,) * 6,
        flops=3_300_000_000,
        nbytes=10_000_000,
        outs=(VMEM, VMEM, VMEM, HBM),
    )
    sides = (info, cores, swap_tile(halos, 0), swap_tile(halos, 1))
    parts = (WIDTH // 16, 4, 8, HALF)
    kept = call(add_kernel, tiles, (), (keep, swap_core(send)), "add").reshape(parts)
    kept = call(reduce_kernel, parts[1:], (), (among_columns(kept),), "reduce")
    planes = (kept, along_z(kept, 1), along_z(kept, 3), along_z(kept, 2))
    kept = call(total_kernel, parts, (), planes, "total")
    got = swap_slab(call(sum_kernel, band, (), sides + (kept,), "sum"))
    kept = among_columns(kept)
    object_grad, probe_grad = call(
        finish_kernel,
        (band, probe.shape),
        (),
        sides + (got, kept.reshape(tiles), swap_core(kept).reshape(tiles)),
        "finish",
    )
    return object_grad, probe_grad


def solution(mesh):
    placed = (P("slab", None, "tile", None), P(), P("tile", None), P("tile", None, None))
    return jax.shard_map(
        shards,
        mesh=mesh,
        in_specs=placed,
        out_specs=(P("slab", None, "tile", None), P()),
        check_vma=False,
    )
```

```python
import functools

import jax
import jax.numpy as jnp
import numpy as np
from jax import lax
from jax.experimental import pallas as pl
from jax.experimental.pallas import tpu as pltpu
from jax.sharding import PartitionSpec as P

WIDTH = 256
HALF = 128
HALO = 128
COLS = 384
PROP_STRENGTH = 12.0
BF16 = jnp.bfloat16
F32 = jnp.float32
VMEM = pl.BlockSpec(memory_space=pltpu.VMEM)
SMEM = pl.BlockSpec(memory_space=pltpu.SMEM)
HBM = pl.BlockSpec(memory_space=pltpu.HBM)


def high_low(table):
    table = table.astype(np.float32)
    high = table.astype(jnp.bfloat16)
    low = (table - high.astype(np.float32)).astype(jnp.bfloat16)
    return np.stack([high, low])


def on_right(m):
    return high_low(np.block([[m.real, m.imag], [-m.imag, m.real]]))


def on_left(m):
    return high_low(np.block([[m.real, -m.imag], [m.imag, m.real]]))


def make_tables():
    index = np.arange(WIDTH)
    dft = np.exp(-2j * np.pi / WIDTH * (index[:, None] * index[None, :] % WIDTH)) / np.sqrt(WIDTH)
    freq = ((index + WIDTH // 2) % WIDTH - WIDTH // 2) / WIDTH
    phase = np.exp(-1j * PROP_STRENGTH * freq**2)
    prop = dft.conj() @ (phase[:, None] * dft)
    far = phase[:, None] * dft
    p, q = prop[:HALF, :HALF], prop[:HALF, HALF:]
    props = ((p + q) / 2, (p - q) / 2)
    fars = (far[0::2, :HALF], far[1::2, :HALF])
    return np.stack(
        [
            np.stack([on_right(m) for m in props]),
            np.stack([on_left(m) for m in props]),
            np.stack([on_right(m.T) for m in fars]),
            np.stack([on_left(m) for m in fars]),
            np.stack([on_right(m) for m in fars]),
            np.stack([on_left(m.T) for m in fars]),
        ]
    )


PROP_RIGHT, PROP_LEFT, FAR_RIGHT, FAR_LEFT, BACK_RIGHT, BACK_LEFT = range(6)


def split(x):
    high = x.astype(BF16)
    low = (x - high.astype(F32)).astype(BF16)
    return high, low


def dot(a, b):
    return jnp.dot(a, b, preferred_element_type=F32)


def fold(x):
    x = jnp.concatenate([x[:HALF] + x[HALF:], x[:HALF] - x[HALF:]], axis=0)
    return jnp.concatenate([x[:, :HALF] + x[:, HALF:], x[:, :HALF] - x[:, HALF:]], axis=1)


def right_mult(x, tables, which):
    re, im = [], []
    for h in range(2):
        part = slice(h * HALF, (h + 1) * HALF)
        high, low = split(jnp.concatenate([x[0][:, part], x[1][:, part]], axis=1))
        th, tl = tables[which, h, 0], tables[which, h, 1]
        out = dot(jnp.concatenate([high, low, high], axis=1), jnp.concatenate([th, th, tl], axis=0))
        re.append(out[:, :HALF])
        im.append(out[:, HALF:])
    return jnp.concatenate(re, axis=1), jnp.concatenate(im, axis=1)


def left_mult(x, tables, which):
    re, im = [], []
    for h in range(2):
        part = slice(h * HALF, (h + 1) * HALF)
        high, low = split(jnp.concatenate([x[0][part], x[1][part]], axis=0))
        th, tl = tables[which, h, 0], tables[which, h, 1]
        out = dot(jnp.concatenate([th, th, tl], axis=1), jnp.concatenate([high, low, high], axis=0))
        re.append(out[:HALF])
        im.append(out[HALF:])
    return jnp.concatenate(re, axis=0), jnp.concatenate(im, axis=0)


def propagate(x, tables):
    y = right_mult((fold(x[0]), fold(x[1])), tables, PROP_RIGHT)
    y = left_mult(y, tables, PROP_LEFT)
    return fold(y[0]), fold(y[1])


def times(a, b):
    return a[0] * b[0] - a[1] * b[1], a[0] * b[1] + a[1] * b[0]


def here():
    half = lax.axis_size("tile") // 2
    within = lax.axis_index("tile") % half
    turned = jnp.where((within == 0) | (within == half - 1), 1, 0)
    return lax.axis_index("slab"), within % 2, turned


def masks(info_ref, which):
    row = jnp.broadcast_to(info_ref[2 * which : 2 * which + 1], (HALO, HALF))
    col = jnp.broadcast_to(info_ref[2 * which + 1 : 2 * which + 2], (HALO, HALF))
    line = lax.broadcasted_iota(jnp.int32, (HALO, HALF), 0)
    lane = lax.broadcasted_iota(jnp.int32, (HALO, HALF), 1)
    return jnp.where(line >= row, 1, 0) == here()[1], lane >= col


def columns_of(x, kept):
    return jnp.where(kept, x(0), x(2)), x(1)


def halo_of(across_ref, beside_ref, at, from_beside, kept):
    def column(i):
        cols = slice(i * HALF, (i + 1) * HALF)
        return jnp.where(from_beside, beside_ref[at + (slice(None), cols)], across_ref[at + (slice(None), cols)])

    return columns_of(column, kept)


def roll_probe_kernel(place_ref, offsets_ref, probe_ref, out_ref):
    row, col = offsets_ref[place_ref[0], 0], offsets_ref[place_ref[0], 1]
    for c in range(2):
        out_ref[c] = pltpu.roll(pltpu.roll(probe_ref[c], row, 0), col, 1)


def core_kernel(offsets_ref, own_ref, out_ref, offsets, cols, sems, out_sems):
    load = pltpu.make_async_copy(offsets_ref, offsets, sems.at[4])
    load.start()
    loads = [pltpu.make_async_copy(own_ref.at[i // 2, i % 2], cols.at[i], sems.at[i]) for i in range(4)]
    for copy in loads:
        copy.start()
    load.wait()
    lane = lax.broadcasted_iota(jnp.int32, (HALO, HALF), 1)
    kept = lane >= offsets[1 - lax.axis_index("slab"), 1]
    stores = []
    for i in range(4):
        loads[i].wait()
        cols[i, :, :HALF] = jnp.where(kept, cols[i, :, :HALF], cols[i, :, 2 * HALF :])
        store = pltpu.make_async_copy(cols.at[i, :, :WIDTH], out_ref.at[i // 2, i % 2], out_sems.at[i])
        store.start()
        stores.append(store)
    for copy in stores:
        copy.wait()


def amp_kernel(place_ref, offsets_ref, amp_ref, out_ref):
    x = amp_ref[place_ref[0]]
    line = lax.broadcasted_iota(jnp.int32, (WIDTH, WIDTH), 0)
    lane = lax.broadcasted_iota(jnp.int32, (WIDTH, WIDTH), 1)
    rows = jnp.where(lane == 2 * (line % HALF) + line // HALF, 1.0, 0.0).astype(BF16)
    cols = jnp.where(line == 2 * (lane % HALF) + lane // HALF, 1.0, 0.0).astype(BF16)

    def parts(value):
        high, rest = split(value)
        return high, rest, (value - high.astype(F32) - rest.astype(F32)).astype(BF16)

    x = sum(dot(rows, part) for part in parts(x))
    out_ref[...] = sum(dot(part, cols) for part in parts(x))


def halo_kernel(info_ref, across_ref, beside_ref, out_ref):
    from_beside, kept = masks(info_ref, 1)
    for j in range(2):
        for c in range(2):
            left, right = halo_of(across_ref, beside_ref, (j, c), from_beside, kept)
            out_ref[j, c, :, :HALF] = left
            out_ref[j, c, :, HALF:] = right


def window_kernel(info_ref, own_ref, across_ref, beside_ref, out_ref):
    from_beside, kept = masks(info_ref, 0)
    for j in range(2):
        for c in range(2):
            left, right = halo_of(across_ref, beside_ref, (j, c), from_beside, kept)
            out_ref[j, c, :HALO, :HALF] = left
            out_ref[j, c, :HALO, HALF:] = right
            left, right = columns_of(lambda i: own_ref[j, c, :, i * HALF : (i + 1) * HALF], kept)
            out_ref[j, c, HALO:, :HALF] = left
            out_ref[j, c, HALO:, HALF:] = right


def position_kernel(
    info_ref,
    offsets_ref,
    tables_ref,
    probe_ref,
    amp_ref,
    own_ref,
    core_ref,
    halo_ref,
    keep_out,
    send_out,
    core_out,
    beside_out,
    early_out,
    late_out,
    waves,
    halos,
    offsets,
    sems,
):
    place, odd, turned = here()
    load = pltpu.make_async_copy(offsets_ref, offsets, sems.at[0, 5])
    load.start()
    from_beside = masks(info_ref, 0)[0]
    across_turned = turned
    turned = jnp.where(jnp.concatenate([from_beside, from_beside], axis=1), 0, turned)

    def window_of(s):
        mine = jnp.where(place == s // 2, 1, 0)
        out = []
        for c in range(2):
            halo = jnp.where(turned == mine, halo_ref[s % 2, c], own_ref[s % 2, c, :HALO])
            core = jnp.where(mine == 1, own_ref[s % 2, c, HALO:], core_ref[s % 2, c])
            out.append(jnp.concatenate([halo, core], axis=0))
        return out

    wave = (probe_ref[0], probe_ref[1])
    for s in range(4):
        if s > 0:
            waves[s - 1, 0], waves[s - 1, 1] = wave
        prod = times(wave, window_of(s))
        if s < 3:
            wave = propagate(prod, tables_ref)
    field = right_mult((fold(prod[0]), fold(prod[1])), tables_ref, FAR_RIGHT)
    field = left_mult(field, tables_ref, FAR_LEFT)
    model = jnp.sqrt(field[0] * field[0] + field[1] * field[1] + 1.0)
    ratio = (model - amp_ref[...]) / model
    grad = (field[0] * ratio, -(field[1] * ratio))
    grad = right_mult(grad, tables_ref, BACK_RIGHT)
    grad = left_mult(grad, tables_ref, BACK_LEFT)
    grad = (fold(grad[0]), fold(grad[1]))
    copies = []
    for s in range(3, -1, -1):
        wave = (waves[s - 1, 0], waves[s - 1, 1]) if s > 0 else (probe_ref[0], probe_ref[1])
        object_grad = times(wave, grad)
        slot = jnp.where(place == s // 2, s % 2, 2 + s % 2)
        for c in range(2):
            value = object_grad[c] if c == 0 else -object_grad[c]
            core_out[slot, c] = value[HALO:]
            halos[slot, pl.ds(c * HALO, HALO)] = value[:HALO]
        start = pl.multiple_of(slot * 2 * HALO, HALO)
        copy = pltpu.make_async_copy(halos.at[slot], beside_out.at[pl.ds(start, 2 * HALO)], sems.at[0, s])
        copy.start()
        copies.append(copy)
        start = pl.multiple_of(s % 2 * 2 * HALO, HALO)
        early = jnp.where(slot // 2 == 1, 1, 0) != across_turned
        for which, ref in enumerate((late_out, early_out)):
            copy = pltpu.make_async_copy(halos.at[slot], ref.at[pl.ds(start, 2 * HALO)], sems.at[1, s])

            @pl.when(early == (which == 1))
            def _():
                copy.start()

        copies.append(copy)
        grad = times(window_of(s), grad)
        if s > 0:
            grad = propagate(grad, tables_ref)
    meta = info_ref[...].astype(F32)
    halos[4, :8] = jnp.concatenate([meta, meta], axis=1)
    for i, (ref, start) in enumerate(((beside_out, 8 * HALO), (early_out, 4 * HALO))):
        copy = pltpu.make_async_copy(halos.at[4, :8], ref.at[pl.ds(start, 8)], sems.at[i, 4])
        copy.start()
        copies.append(copy)
    load.wait()
    row, col = offsets[place, 0], offsets[place, 1]
    value = [grad[0], -grad[1]]
    for c in range(2):
        value[c] = pltpu.roll(value[c], lax.rem(WIDTH - row, WIDTH), 0)
        value[c] = pltpu.roll(value[c], lax.rem(WIDTH - col, WIDTH), 1)
    for ref, which in ((keep_out, odd), (send_out, 1 - odd)):
        part = jnp.where(which == 0, value[0], value[1])
        for h in range(2):
            ref[:, h] = part[:, h * HALF : (h + 1) * HALF].reshape(WIDTH // 8, 8, HALF)
    for copy in copies:
        copy.wait()


def widen(x, kept):
    left, right = x[..., :HALF], x[..., HALF:]
    return jnp.concatenate([jnp.where(kept, left, 0.0), right, jnp.where(kept, 0.0, left)], axis=-1)


def add_halos(info_ref, core_ref, across_ref, early_ref, beside_ref, out_ref, first, extra=None):
    odd = here()[1]
    own_kept = masks(info_ref, 0)[1]
    line = lax.broadcasted_iota(jnp.int32, (HALO, WIDTH), 0).astype(F32)
    column = lax.broadcasted_iota(jnp.int32, (HALO, HALF), 1).astype(F32)
    sides = []
    for ref, base, meta, after in (
        (across_ref, 0, early_ref[4 * HALO :], odd),
        (beside_ref, first * 2 * HALO, beside_ref[8 * HALO :], 1 - odd),
    ):
        kept = column >= meta[1:2, :HALF]
        mask = jnp.where(line >= meta[0:1], 1, 0) == after
        sides.append((ref, base, mask, kept))
    for j in range(2):
        for c in range(2):
            total = widen(core_ref[first + j, c], own_kept)
            for ref, base, mask, kept in sides:
                start = base + (j * 2 + c) * HALO
                total = total + widen(jnp.where(mask, ref[start : start + HALO], 0.0), kept)
            out_ref[j, c] = total if extra is None else total + extra[j, c]


def add_kernel(keep_ref, got_ref, out_ref):
    out_ref[...] = keep_ref[...] + got_ref[...]


def reduce_kernel(parts_ref, out_ref):
    out_ref[...] = jnp.sum(parts_ref[...], axis=0)


def total_kernel(first_ref, second_ref, third_ref, fourth_ref, out_ref):
    total = (first_ref[...] + second_ref[...]) + (third_ref[...] + fourth_ref[...])
    out_ref[...] = jnp.broadcast_to(total[None], out_ref.shape)


def sum_kernel(info_ref, core_ref, early_ref, beside_ref, after_ref, out_ref):
    add_halos(info_ref, core_ref, early_ref, early_ref, beside_ref, out_ref, 2)


def finish_kernel(
    info_ref,
    core_ref,
    early_ref,
    beside_ref,
    late_ref,
    swapped_ref,
    keep_ref,
    got_ref,
    object_out,
    probe_out,
):
    add_halos(info_ref, core_ref, late_ref, early_ref, beside_ref, object_out, 0, swapped_ref)
    odd = here()[1]
    for ref, which in ((keep_ref, odd), (got_ref, 1 - odd)):
        for h in range(2):
            probe_out[which, :, h * HALF : (h + 1) * HALF] = ref[:, h].reshape(WIDTH, HALF)


def call(kernel, shapes, smem, vmem, name, scratch=(), flops=0, nbytes=2_000_000, ins=None, outs=None, vmem_limit=40):
    single = isinstance(shapes[0], int)
    shapes = (shapes,) if single else shapes
    out = pl.pallas_call(
        kernel,
        out_shape=tuple(jax.ShapeDtypeStruct(shape, F32) for shape in shapes),
        in_specs=[SMEM] * len(smem) + list(ins or [VMEM] * len(vmem)),
        out_specs=outs or (VMEM,) * len(shapes),
        scratch_shapes=scratch,
        compiler_params=pltpu.CompilerParams(vmem_limit_bytes=vmem_limit * 1024 * 1024),
        cost_estimate=pl.CostEstimate(flops=flops, bytes_accessed=nbytes, transcendentals=0),
        name=name,
    )(*smem, *vmem)
    return out[0] if single else out


def swap_tile(x, beside):
    slabs, tiles = lax.axis_size("slab"), lax.axis_size("tile")
    pairs = []
    for slab in range(slabs):
        for tile in range(tiles):
            to = (tile + (1 if tile % 2 != beside else -1)) % tiles
            turned = tile // (tiles // 2) != to // (tiles // 2)
            pairs.append((slab * tiles + tile, (slab ^ turned) * tiles + to))
    return lax.ppermute(x, ("slab", "tile"), pairs)


def swap_core(x):
    count = lax.axis_size("tile")
    return lax.ppermute(x, "tile", [(i, i ^ 1) for i in range(count)])


def among_columns(x):
    slabs, tiles = lax.axis_size("slab"), lax.axis_size("tile")
    half = tiles // 2
    planes = [slab * tiles + far * half for slab in range(slabs) for far in range(2)]
    groups = [[plane + i for i in range(core, half, 2)] for plane in planes for core in range(2)]
    return lax.all_to_all(x, ("slab", "tile"), 0, 0, tiled=True, axis_index_groups=groups)


def along_z(x, by):
    slabs, tiles = lax.axis_size("slab"), lax.axis_size("tile")
    half = tiles // 2
    pairs = []
    for z in range(2 * slabs):
        to = (z + by) % (2 * slabs)
        for i in range(half):
            source = z % slabs * tiles + z // slabs * half + i
            pairs.append((source, to % slabs * tiles + to // slabs * half + i))
    return lax.ppermute(x, ("slab", "tile"), pairs)


def swap_slab(x):
    return lax.ppermute(x, "slab", [(0, 1), (1, 0)])


def shards(transmission, probe, scan_offsets, amplitudes):
    tables = jnp.asarray(make_tables())
    index = lax.axis_index("slab").astype(jnp.int32)
    where = (index.reshape(1), scan_offsets)
    info = jnp.where(index == 0, scan_offsets, scan_offsets[::-1]).reshape(4, 1)
    info = jnp.broadcast_to(jnp.concatenate([info, info]), (8, HALF))
    own = transmission
    part, whole, band = (2, 2, HALO, WIDTH), (2, 2, WIDTH, WIDTH), (2, 2, HALO, COLS)

    core = call(
        core_kernel,
        part,
        (),
        (scan_offsets, own),
        "core",
        scratch=[
            pltpu.SMEM((2, 2), jnp.int32),
            pltpu.VMEM((4, HALO, COLS), F32),
            pltpu.SemaphoreType.DMA((5,)),
            pltpu.SemaphoreType.DMA((4,)),
        ],
        ins=(HBM, HBM),
        outs=(HBM,),
        vmem_limit=60,
    )
    core = swap_slab(core)
    beside, across = swap_tile(own, 1), swap_tile(own, 0)
    rolled = call(roll_probe_kernel, (2, WIDTH, WIDTH), where, (probe,), "roll")
    amp = call(amp_kernel, (WIDTH, WIDTH), where, (amplitudes,), "amp")
    halo = swap_slab(call(halo_kernel, part, (), (info, across, beside), "halo"))
    windows = call(window_kernel, whole, (), (info, own, across, beside), "window")

    tiles = (WIDTH // 8, 2, 8, HALF)
    keep, send, cores, beside, early, late = call(
        position_kernel,
        (tiles, tiles, (4, 2, HALO, WIDTH), (8 * HALO + 8, WIDTH), (4 * HALO + 8, WIDTH), (4 * HALO, WIDTH)),
        (),
        (info, scan_offsets, tables, rolled, amp, windows, core, halo),
        "position",
        scratch=[
            pltpu.VMEM((3, 2, WIDTH, WIDTH), F32),
            pltpu.VMEM((5, 2 * HALO, WIDTH), F32),
            pltpu.SMEM((2, 2), jnp.int32),
            pltpu.SemaphoreType.DMA((2, 6)),
        ],
        ins=(VMEM, HBM) + (VMEM,) * 6,
        flops=3_300_000_000,
        nbytes=10_000_000,
        outs=(VMEM, VMEM, VMEM, HBM, HBM, HBM),
    )
    sides = (info, cores, swap_tile(early, 0), swap_tile(beside, 1))
    parts = (WIDTH // 16, 4, 8, HALF)
    kept = call(add_kernel, tiles, (), (keep, swap_core(send)), "add").reshape(parts)
    kept = call(reduce_kernel, parts[1:], (), (among_columns(kept),), "reduce")
    late, kept = lax.optimization_barrier((late, kept))
    late = swap_tile(late, 0)
    planes = (kept, along_z(kept, 1), along_z(kept, 3), along_z(kept, 2))
    kept = call(total_kernel, parts, (), planes, "total")
    got = swap_slab(call(sum_kernel, band, (), sides + (kept,), "sum"))
    kept = among_columns(kept)
    object_grad, probe_grad = call(
        finish_kernel,
        (band, probe.shape),
        (),
        sides + (late, got, kept.reshape(tiles), swap_core(kept).reshape(tiles)),
        "finish",
    )
    return object_grad, probe_grad


def solution(mesh):
    placed = (P("slab", None, "tile", None), P(), P("tile", None), P("tile", None, None))
    return jax.shard_map(
        shards,
        mesh=mesh,
        in_specs=placed,
        out_specs=(P("slab", None, "tile", None), P()),
        check_vma=False,
    )
```

```python
import functools

import jax
import jax.numpy as jnp
import numpy as np
from jax import lax
from jax.experimental import pallas as pl
from jax.experimental.pallas import tpu as pltpu
from jax.sharding import PartitionSpec as P

WIDTH = 256
HALF = 128
HALO = 128
COLS = 384
PROP_STRENGTH = 12.0
BF16 = jnp.bfloat16
F32 = jnp.float32
VMEM = pl.BlockSpec(memory_space=pltpu.VMEM)
SMEM = pl.BlockSpec(memory_space=pltpu.SMEM)
HBM = pl.BlockSpec(memory_space=pltpu.HBM)


def high_low(table):
    table = table.astype(np.float32)
    high = table.astype(jnp.bfloat16)
    low = (table - high.astype(np.float32)).astype(jnp.bfloat16)
    return np.stack([high, low])


def on_right(m):
    return high_low(np.block([[m.real, m.imag], [-m.imag, m.real]]))


def on_left(m):
    return high_low(np.block([[m.real, -m.imag], [m.imag, m.real]]))


def make_tables():
    index = np.arange(WIDTH)
    dft = np.exp(-2j * np.pi / WIDTH * (index[:, None] * index[None, :] % WIDTH)) / np.sqrt(WIDTH)
    freq = ((index + WIDTH // 2) % WIDTH - WIDTH // 2) / WIDTH
    phase = np.exp(-1j * PROP_STRENGTH * freq**2)
    prop = dft.conj() @ (phase[:, None] * dft)
    far = phase[:, None] * dft
    p, q = prop[:HALF, :HALF], prop[:HALF, HALF:]
    props = ((p + q) / 2, (p - q) / 2)
    fars = (far[0::2, :HALF], far[1::2, :HALF])
    return np.stack(
        [
            np.stack([on_right(m) for m in props]),
            np.stack([on_left(m) for m in props]),
            np.stack([on_right(m.T) for m in fars]),
            np.stack([on_left(m) for m in fars]),
            np.stack([on_right(m) for m in fars]),
            np.stack([on_left(m.T) for m in fars]),
        ]
    )


PROP_RIGHT, PROP_LEFT, FAR_RIGHT, FAR_LEFT, BACK_RIGHT, BACK_LEFT = range(6)


def split(x):
    high = x.astype(BF16)
    low = (x - high.astype(F32)).astype(BF16)
    return high, low


def dot(a, b):
    return jnp.dot(a, b, preferred_element_type=F32)


def fold(x):
    x = jnp.concatenate([x[:HALF] + x[HALF:], x[:HALF] - x[HALF:]], axis=0)
    return jnp.concatenate([x[:, :HALF] + x[:, HALF:], x[:, :HALF] - x[:, HALF:]], axis=1)


def right_mult(x, tables, which):
    re, im = [], []
    for h in range(2):
        part = slice(h * HALF, (h + 1) * HALF)
        high, low = split(jnp.concatenate([x[0][:, part], x[1][:, part]], axis=1))
        th, tl = tables[which, h, 0], tables[which, h, 1]
        out = dot(jnp.concatenate([high, low, high], axis=1), jnp.concatenate([th, th, tl], axis=0))
        re.append(out[:, :HALF])
        im.append(out[:, HALF:])
    return jnp.concatenate(re, axis=1), jnp.concatenate(im, axis=1)


def left_mult(x, tables, which):
    re, im = [], []
    for h in range(2):
        part = slice(h * HALF, (h + 1) * HALF)
        high, low = split(jnp.concatenate([x[0][part], x[1][part]], axis=0))
        th, tl = tables[which, h, 0], tables[which, h, 1]
        out = dot(jnp.concatenate([th, th, tl], axis=1), jnp.concatenate([high, low, high], axis=0))
        re.append(out[:HALF])
        im.append(out[HALF:])
    return jnp.concatenate(re, axis=0), jnp.concatenate(im, axis=0)


def propagate(x, tables):
    y = right_mult((fold(x[0]), fold(x[1])), tables, PROP_RIGHT)
    y = left_mult(y, tables, PROP_LEFT)
    return fold(y[0]), fold(y[1])


def times(a, b):
    return a[0] * b[0] - a[1] * b[1], a[0] * b[1] + a[1] * b[0]


def here():
    half = lax.axis_size("tile") // 2
    within = lax.axis_index("tile") % half
    turned = jnp.where((within == 0) | (within == half - 1), 1, 0)
    return lax.axis_index("slab"), within % 2, turned


def masks(info_ref, which):
    row = jnp.broadcast_to(info_ref[2 * which : 2 * which + 1], (HALO, HALF))
    col = jnp.broadcast_to(info_ref[2 * which + 1 : 2 * which + 2], (HALO, HALF))
    line = lax.broadcasted_iota(jnp.int32, (HALO, HALF), 0)
    lane = lax.broadcasted_iota(jnp.int32, (HALO, HALF), 1)
    return jnp.where(line >= row, 1, 0) == here()[1], lane >= col


def columns_of(x, kept):
    return jnp.where(kept, x(0), x(2)), x(1)


def halo_of(across_ref, beside_ref, at, from_beside, kept):
    def column(i):
        cols = slice(i * HALF, (i + 1) * HALF)
        return jnp.where(from_beside, beside_ref[at + (slice(None), cols)], across_ref[at + (slice(None), cols)])

    return columns_of(column, kept)


def roll_probe_kernel(place_ref, offsets_ref, probe_ref, out_ref):
    row, col = offsets_ref[place_ref[0], 0], offsets_ref[place_ref[0], 1]
    for c in range(2):
        out_ref[c] = pltpu.roll(pltpu.roll(probe_ref[c], row, 0), col, 1)


def core_kernel(offsets_ref, own_ref, out_ref, offsets, left, right, sems):
    load = pltpu.make_async_copy(offsets_ref, offsets, sems.at[0, 4])
    load.start()
    loads = []
    for i in range(4):
        at = (i // 2, i % 2, slice(None))
        loads.append(
            [
                pltpu.make_async_copy(own_ref.at[at + (slice(0, HALF),)], left.at[i], sems.at[0, i]),
                pltpu.make_async_copy(own_ref.at[at + (slice(WIDTH, COLS),)], right.at[i], sems.at[1, i]),
                pltpu.make_async_copy(
                    own_ref.at[at + (slice(HALF, WIDTH),)], out_ref.at[at + (slice(HALF, WIDTH),)], sems.at[2, i]
                ),
            ]
        )
        for copy in loads[i]:
            copy.start()
    load.wait()
    lane = lax.broadcasted_iota(jnp.int32, (HALO, HALF), 1)
    kept = lane >= offsets[1 - lax.axis_index("slab"), 1]
    for i in range(4):
        loads[i][0].wait()
        loads[i][1].wait()
        out_ref[i // 2, i % 2, :, :HALF] = jnp.where(kept, left[i], right[i])
    for i in range(4):
        loads[i][2].wait()


def amp_kernel(place_ref, offsets_ref, amp_ref, out_ref):
    x = amp_ref[place_ref[0]]
    line = lax.broadcasted_iota(jnp.int32, (WIDTH, WIDTH), 0)
    lane = lax.broadcasted_iota(jnp.int32, (WIDTH, WIDTH), 1)
    rows = jnp.where(lane == 2 * (line % HALF) + line // HALF, 1.0, 0.0).astype(BF16)
    cols = jnp.where(line == 2 * (lane % HALF) + lane // HALF, 1.0, 0.0).astype(BF16)

    def parts(value):
        high, rest = split(value)
        return high, rest, (value - high.astype(F32) - rest.astype(F32)).astype(BF16)

    x = sum(dot(rows, part) for part in parts(x))
    out_ref[...] = sum(dot(part, cols) for part in parts(x))


def halo_kernel(info_ref, across_ref, beside_ref, out_ref):
    from_beside, kept = masks(info_ref, 1)
    for j in range(2):
        for c in range(2):
            left, right = halo_of(across_ref, beside_ref, (j, c), from_beside, kept)
            out_ref[j, c, :, :HALF] = left
            out_ref[j, c, :, HALF:] = right


def window_kernel(info_ref, own_ref, across_ref, beside_ref, out_ref):
    from_beside, kept = masks(info_ref, 0)
    for j in range(2):
        for c in range(2):
            left, right = halo_of(across_ref, beside_ref, (j, c), from_beside, kept)
            out_ref[j, c, :HALO, :HALF] = left
            out_ref[j, c, :HALO, HALF:] = right
            left, right = columns_of(lambda i: own_ref[j, c, :, i * HALF : (i + 1) * HALF], kept)
            out_ref[j, c, HALO:, :HALF] = left
            out_ref[j, c, HALO:, HALF:] = right


def position_kernel(
    info_ref,
    offsets_ref,
    tables_ref,
    probe_ref,
    amp_ref,
    own_ref,
    core_ref,
    halo_ref,
    keep_out,
    send_out,
    core_out,
    beside_out,
    early_out,
    late_out,
    waves,
    halos,
    offsets,
    sems,
):
    place, odd, turned = here()
    load = pltpu.make_async_copy(offsets_ref, offsets, sems.at[0, 5])
    load.start()
    from_beside = masks(info_ref, 0)[0]
    across_turned = turned
    turned = jnp.where(jnp.concatenate([from_beside, from_beside], axis=1), 0, turned)

    def window_of(s):
        mine = jnp.where(place == s // 2, 1, 0)
        out = []
        for c in range(2):
            halo = jnp.where(turned == mine, halo_ref[s % 2, c], own_ref[s % 2, c, :HALO])
            core = jnp.where(mine == 1, own_ref[s % 2, c, HALO:], core_ref[s % 2, c])
            out.append(jnp.concatenate([halo, core], axis=0))
        return out

    wave = (probe_ref[0], probe_ref[1])
    for s in range(4):
        if s > 0:
            waves[s - 1, 0], waves[s - 1, 1] = wave
        prod = times(wave, window_of(s))
        if s < 3:
            wave = propagate(prod, tables_ref)
    field = right_mult((fold(prod[0]), fold(prod[1])), tables_ref, FAR_RIGHT)
    field = left_mult(field, tables_ref, FAR_LEFT)
    model = jnp.sqrt(field[0] * field[0] + field[1] * field[1] + 1.0)
    ratio = (model - amp_ref[...]) / model
    grad = (field[0] * ratio, -(field[1] * ratio))
    grad = right_mult(grad, tables_ref, BACK_RIGHT)
    grad = left_mult(grad, tables_ref, BACK_LEFT)
    grad = (fold(grad[0]), fold(grad[1]))
    copies = []
    for s in range(3, -1, -1):
        wave = (waves[s - 1, 0], waves[s - 1, 1]) if s > 0 else (probe_ref[0], probe_ref[1])
        object_grad = times(wave, grad)
        slot = jnp.where(place == s // 2, s % 2, 2 + s % 2)
        for c in range(2):
            value = object_grad[c] if c == 0 else -object_grad[c]
            core_out[slot, c] = value[HALO:]
            halos[slot, pl.ds(c * HALO, HALO)] = value[:HALO]
        start = pl.multiple_of(slot * 2 * HALO, HALO)
        copy = pltpu.make_async_copy(halos.at[slot], beside_out.at[pl.ds(start, 2 * HALO)], sems.at[0, s])
        copy.start()
        copies.append(copy)
        start = pl.multiple_of(s % 2 * 2 * HALO, HALO)
        early = jnp.where(slot // 2 == 1, 1, 0) != across_turned
        for which, ref in enumerate((late_out, early_out)):
            copy = pltpu.make_async_copy(halos.at[slot], ref.at[pl.ds(start, 2 * HALO)], sems.at[1, s])

            @pl.when(early == (which == 1))
            def _():
                copy.start()

        copies.append(copy)
        grad = times(window_of(s), grad)
        if s > 0:
            grad = propagate(grad, tables_ref)
    meta = info_ref[...].astype(F32)
    halos[4, :8] = jnp.concatenate([meta, meta], axis=1)
    for i, (ref, start) in enumerate(((beside_out, 8 * HALO), (early_out, 4 * HALO))):
        copy = pltpu.make_async_copy(halos.at[4, :8], ref.at[pl.ds(start, 8)], sems.at[i, 4])
        copy.start()
        copies.append(copy)
    load.wait()
    row, col = offsets[place, 0], offsets[place, 1]
    value = [grad[0], -grad[1]]
    for c in range(2):
        value[c] = pltpu.roll(value[c], lax.rem(WIDTH - row, WIDTH), 0)
        value[c] = pltpu.roll(value[c], lax.rem(WIDTH - col, WIDTH), 1)
    for ref, which in ((keep_out, odd), (send_out, 1 - odd)):
        part = jnp.where(which == 0, value[0], value[1])
        for h in range(2):
            ref[:, h] = part[:, h * HALF : (h + 1) * HALF].reshape(WIDTH // 8, 8, HALF)
    for copy in copies:
        copy.wait()


def widen(x, kept):
    left, right = x[..., :HALF], x[..., HALF:]
    return jnp.concatenate([jnp.where(kept, left, 0.0), right, jnp.where(kept, 0.0, left)], axis=-1)


def add_halos(info_ref, core_ref, across_ref, early_ref, beside_ref, out_ref, first, extra=None):
    odd = here()[1]
    own_kept = masks(info_ref, 0)[1]
    line = lax.broadcasted_iota(jnp.int32, (HALO, WIDTH), 0).astype(F32)
    column = lax.broadcasted_iota(jnp.int32, (HALO, HALF), 1).astype(F32)
    sides = []
    for ref, base, meta, after in (
        (across_ref, 0, early_ref[4 * HALO :], odd),
        (beside_ref, first * 2 * HALO, beside_ref[8 * HALO :], 1 - odd),
    ):
        kept = column >= meta[1:2, :HALF]
        mask = jnp.where(line >= meta[0:1], 1, 0) == after
        sides.append((ref, base, mask, kept))
    for j in range(2):
        for c in range(2):
            total = widen(core_ref[first + j, c], own_kept)
            for ref, base, mask, kept in sides:
                start = base + (j * 2 + c) * HALO
                total = total + widen(jnp.where(mask, ref[start : start + HALO], 0.0), kept)
            out_ref[j, c] = total if extra is None else total + extra[j, c]


def add_kernel(keep_ref, got_ref, out_ref):
    out_ref[...] = keep_ref[...] + got_ref[...]


def reduce_kernel(parts_ref, out_ref):
    out_ref[...] = jnp.sum(parts_ref[...], axis=0)


def total_kernel(first_ref, second_ref, out_ref):
    total = first_ref[...] + second_ref[...]
    out_ref[...] = jnp.broadcast_to(total[None], out_ref.shape)


def sum_kernel(info_ref, core_ref, early_ref, beside_ref, after_ref, out_ref):
    add_halos(info_ref, core_ref, early_ref, early_ref, beside_ref, out_ref, 2)


def finish_kernel(
    info_ref,
    core_ref,
    early_ref,
    beside_ref,
    late_ref,
    swapped_ref,
    keep_ref,
    got_ref,
    object_out,
    probe_out,
):
    add_halos(info_ref, core_ref, late_ref, early_ref, beside_ref, object_out, 0, swapped_ref)
    odd = here()[1]
    for ref, which in ((keep_ref, odd), (got_ref, 1 - odd)):
        for h in range(2):
            probe_out[which, :, h * HALF : (h + 1) * HALF] = ref[:, h].reshape(WIDTH, HALF)


def call(kernel, shapes, smem, vmem, name, scratch=(), flops=0, nbytes=2_000_000, ins=None, outs=None, vmem_limit=40):
    single = isinstance(shapes[0], int)
    shapes = (shapes,) if single else shapes
    out = pl.pallas_call(
        kernel,
        out_shape=tuple(jax.ShapeDtypeStruct(shape, F32) for shape in shapes),
        in_specs=[SMEM] * len(smem) + list(ins or [VMEM] * len(vmem)),
        out_specs=outs or (VMEM,) * len(shapes),
        scratch_shapes=scratch,
        compiler_params=pltpu.CompilerParams(vmem_limit_bytes=vmem_limit * 1024 * 1024),
        cost_estimate=pl.CostEstimate(flops=flops, bytes_accessed=nbytes, transcendentals=0),
        name=name,
    )(*smem, *vmem)
    return out[0] if single else out


def swap_tile(x, beside):
    slabs, tiles = lax.axis_size("slab"), lax.axis_size("tile")
    pairs = []
    for slab in range(slabs):
        for tile in range(tiles):
            to = (tile + (1 if tile % 2 != beside else -1)) % tiles
            turned = tile // (tiles // 2) != to // (tiles // 2)
            pairs.append((slab * tiles + tile, (slab ^ turned) * tiles + to))
    return lax.ppermute(x, ("slab", "tile"), pairs)


def swap_core(x):
    count = lax.axis_size("tile")
    return lax.ppermute(x, "tile", [(i, i ^ 1) for i in range(count)])


def among_columns(x):
    slabs, tiles = lax.axis_size("slab"), lax.axis_size("tile")
    half = tiles // 2
    planes = [slab * tiles + far * half for slab in range(slabs) for far in range(2)]
    groups = [[plane + i for i in range(core, half, 2)] for plane in planes for core in range(2)]
    return lax.all_to_all(x, ("slab", "tile"), 0, 0, tiled=True, axis_index_groups=groups)


def swap_far(x):
    slabs, tiles = lax.axis_size("slab"), lax.axis_size("tile")
    half = tiles // 2
    pairs = [
        (slab * tiles + tile, (slabs - 1 - slab) * tiles + (tile + half) % tiles)
        for slab in range(slabs)
        for tile in range(tiles)
    ]
    return lax.ppermute(x, ("slab", "tile"), pairs)


def swap_slab(x):
    return lax.ppermute(x, "slab", [(0, 1), (1, 0)])


def shards(transmission, probe, scan_offsets, amplitudes):
    tables = jnp.asarray(make_tables())
    index = lax.axis_index("slab").astype(jnp.int32)
    where = (index.reshape(1), scan_offsets)
    info = jnp.where(index == 0, scan_offsets, scan_offsets[::-1]).reshape(4, 1)
    info = jnp.broadcast_to(jnp.concatenate([info, info]), (8, HALF))
    own = transmission
    part, whole, band = (2, 2, HALO, WIDTH), (2, 2, WIDTH, WIDTH), (2, 2, HALO, COLS)

    own_hbm, offsets_hbm = (pltpu.with_memory_space_constraint(x, pltpu.HBM) for x in (own, scan_offsets))
    core = call(
        core_kernel,
        part,
        (),
        (offsets_hbm, own_hbm),
        "core",
        scratch=[
            pltpu.SMEM((2, 2), jnp.int32),
            pltpu.VMEM((4, HALO, HALF), F32),
            pltpu.VMEM((4, HALO, HALF), F32),
            pltpu.SemaphoreType.DMA((3, 5)),
        ],
        ins=(HBM, HBM),
    )
    core = swap_slab(core)
    beside, across = swap_tile(own, 1), swap_tile(own, 0)
    rolled = call(roll_probe_kernel, (2, WIDTH, WIDTH), where, (probe,), "roll")
    amp = call(amp_kernel, (WIDTH, WIDTH), where, (amplitudes,), "amp")
    halo = swap_slab(call(halo_kernel, part, (), (info, across, beside), "halo"))
    windows = call(window_kernel, whole, (), (info, own, across, beside), "window")

    tiles = (WIDTH // 8, 2, 8, HALF)
    keep, send, cores, beside, early, late = call(
        position_kernel,
        (tiles, tiles, (4, 2, HALO, WIDTH), (8 * HALO + 8, WIDTH), (4 * HALO + 8, WIDTH), (4 * HALO, WIDTH)),
        (),
        (info, scan_offsets, tables, rolled, amp, windows, core, halo),
        "position",
        scratch=[
            pltpu.VMEM((3, 2, WIDTH, WIDTH), F32),
            pltpu.VMEM((5, 2 * HALO, WIDTH), F32),
            pltpu.SMEM((2, 2), jnp.int32),
            pltpu.SemaphoreType.DMA((2, 6)),
        ],
        ins=(VMEM, HBM) + (VMEM,) * 6,
        flops=3_300_000_000,
        nbytes=10_000_000,
        outs=(VMEM, VMEM, VMEM, HBM, HBM, HBM),
    )
    sides = (info, cores, swap_tile(early, 0), swap_tile(beside, 1))
    parts = (WIDTH // 16, 4, 8, HALF)
    kept = call(add_kernel, tiles, (), (keep, swap_core(send)), "add").reshape(parts)
    kept = call(reduce_kernel, parts[1:], (), (among_columns(kept),), "reduce")
    late, kept = lax.optimization_barrier((late, kept))
    late = swap_tile(late, 0)
    kept = call(add_kernel, parts[1:], (), (kept, swap_slab(kept)), "add_slabs")
    got = swap_slab(call(sum_kernel, band, (), sides + (kept,), "sum"))
    kept = call(total_kernel, parts, (), (kept, swap_far(kept)), "total")
    kept = among_columns(kept)
    object_grad, probe_grad = call(
        finish_kernel,
        (band, probe.shape),
        (),
        sides + (late, got, kept.reshape(tiles), swap_core(kept).reshape(tiles)),
        "finish",
    )
    return object_grad, probe_grad


def solution(mesh):
    placed = (P("slab", None, "tile", None), P(), P("tile", None), P("tile", None, None))
    return jax.shard_map(
        shards,
        mesh=mesh,
        in_specs=placed,
        out_specs=(P("slab", None, "tile", None), P()),
        check_vma=False,
    )
```

```python
import functools

import jax
import jax.numpy as jnp
import numpy as np
from jax import lax
from jax.experimental import pallas as pl
from jax.experimental.pallas import tpu as pltpu
from jax.sharding import PartitionSpec as P

WIDTH = 256
HALF = 128
HALO = 128
COLS = 384
PROP_STRENGTH = 12.0
BF16 = jnp.bfloat16
F32 = jnp.float32
VMEM = pl.BlockSpec(memory_space=pltpu.VMEM)
SMEM = pl.BlockSpec(memory_space=pltpu.SMEM)
HBM = pl.BlockSpec(memory_space=pltpu.HBM)


def high_low(table):
    table = table.astype(np.float32)
    high = table.astype(jnp.bfloat16)
    low = (table - high.astype(np.float32)).astype(jnp.bfloat16)
    return np.stack([high, low])


def on_right(m):
    return high_low(np.block([[m.real, m.imag], [-m.imag, m.real]]))


def on_left(m):
    return high_low(np.block([[m.real, -m.imag], [m.imag, m.real]]))


def make_tables():
    index = np.arange(WIDTH)
    dft = np.exp(-2j * np.pi / WIDTH * (index[:, None] * index[None, :] % WIDTH)) / np.sqrt(WIDTH)
    freq = ((index + WIDTH // 2) % WIDTH - WIDTH // 2) / WIDTH
    phase = np.exp(-1j * PROP_STRENGTH * freq**2)
    prop = dft.conj() @ (phase[:, None] * dft)
    far = phase[:, None] * dft
    p, q = prop[:HALF, :HALF], prop[:HALF, HALF:]
    props = ((p + q) / 2, (p - q) / 2)
    fars = (far[0::2, :HALF], far[1::2, :HALF])
    return np.stack(
        [
            np.stack([on_right(m) for m in props]),
            np.stack([on_left(m) for m in props]),
            np.stack([on_right(m.T) for m in fars]),
            np.stack([on_left(m) for m in fars]),
            np.stack([on_right(m) for m in fars]),
            np.stack([on_left(m.T) for m in fars]),
        ]
    )


PROP_RIGHT, PROP_LEFT, FAR_RIGHT, FAR_LEFT, BACK_RIGHT, BACK_LEFT = range(6)


def split(x):
    high = x.astype(BF16)
    low = (x - high.astype(F32)).astype(BF16)
    return high, low


def dot(a, b):
    return jnp.dot(a, b, preferred_element_type=F32)


def fold(x):
    x = jnp.concatenate([x[:HALF] + x[HALF:], x[:HALF] - x[HALF:]], axis=0)
    return jnp.concatenate([x[:, :HALF] + x[:, HALF:], x[:, :HALF] - x[:, HALF:]], axis=1)


def right_mult(x, tables, which):
    re, im = [], []
    for h in range(2):
        part = slice(h * HALF, (h + 1) * HALF)
        high, low = split(jnp.concatenate([x[0][:, part], x[1][:, part]], axis=1))
        th, tl = tables[which, h, 0], tables[which, h, 1]
        out = dot(jnp.concatenate([high, low, high], axis=1), jnp.concatenate([th, th, tl], axis=0))
        re.append(out[:, :HALF])
        im.append(out[:, HALF:])
    return jnp.concatenate(re, axis=1), jnp.concatenate(im, axis=1)


def left_mult(x, tables, which):
    re, im = [], []
    for h in range(2):
        part = slice(h * HALF, (h + 1) * HALF)
        high, low = split(jnp.concatenate([x[0][part], x[1][part]], axis=0))
        th, tl = tables[which, h, 0], tables[which, h, 1]
        out = dot(jnp.concatenate([th, th, tl], axis=1), jnp.concatenate([high, low, high], axis=0))
        re.append(out[:HALF])
        im.append(out[HALF:])
    return jnp.concatenate(re, axis=0), jnp.concatenate(im, axis=0)


def propagate(x, tables):
    y = right_mult((fold(x[0]), fold(x[1])), tables, PROP_RIGHT)
    y = left_mult(y, tables, PROP_LEFT)
    return fold(y[0]), fold(y[1])


def times(a, b):
    return a[0] * b[0] - a[1] * b[1], a[0] * b[1] + a[1] * b[0]


def here():
    half = lax.axis_size("tile") // 2
    within = lax.axis_index("tile") % half
    turned = jnp.where((within == 0) | (within == half - 1), 1, 0)
    return lax.axis_index("slab"), within % 2, turned


def masks(info_ref, which):
    row = jnp.broadcast_to(info_ref[2 * which : 2 * which + 1], (HALO, HALF))
    col = jnp.broadcast_to(info_ref[2 * which + 1 : 2 * which + 2], (HALO, HALF))
    line = lax.broadcasted_iota(jnp.int32, (HALO, HALF), 0)
    lane = lax.broadcasted_iota(jnp.int32, (HALO, HALF), 1)
    return jnp.where(line >= row, 1, 0) == here()[1], lane >= col


def columns_of(x, kept):
    return jnp.where(kept, x(0), x(2)), x(1)


def halo_of(across_ref, beside_ref, at, from_beside, kept):
    def column(i):
        cols = slice(i * HALF, (i + 1) * HALF)
        return jnp.where(from_beside, beside_ref[at + (slice(None), cols)], across_ref[at + (slice(None), cols)])

    return columns_of(column, kept)


def roll_probe_kernel(place_ref, offsets_ref, probe_ref, out_ref):
    row, col = offsets_ref[place_ref[0], 0], offsets_ref[place_ref[0], 1]
    for c in range(2):
        out_ref[c] = pltpu.roll(pltpu.roll(probe_ref[c], row, 0), col, 1)


def core_kernel(offsets_ref, own_ref, out_ref, offsets, left, right, sems):
    load = pltpu.make_async_copy(offsets_ref, offsets, sems.at[0, 4])
    load.start()
    loads = []
    for i in range(4):
        at = (i // 2, i % 2, slice(None))
        loads.append(
            [
                pltpu.make_async_copy(own_ref.at[at + (slice(0, HALF),)], left.at[i], sems.at[0, i]),
                pltpu.make_async_copy(own_ref.at[at + (slice(WIDTH, COLS),)], right.at[i], sems.at[1, i]),
                pltpu.make_async_copy(
                    own_ref.at[at + (slice(HALF, WIDTH),)], out_ref.at[at + (slice(HALF, WIDTH),)], sems.at[2, i]
                ),
            ]
        )
        for copy in loads[i]:
            copy.start()
    load.wait()
    lane = lax.broadcasted_iota(jnp.int32, (HALO, HALF), 1)
    kept = lane >= offsets[1 - lax.axis_index("slab"), 1]
    for i in range(4):
        loads[i][0].wait()
        loads[i][1].wait()
        out_ref[i // 2, i % 2, :, :HALF] = jnp.where(kept, left[i], right[i])
    for i in range(4):
        loads[i][2].wait()


def amp_kernel(place_ref, offsets_ref, amp_ref, out_ref):
    x = amp_ref[place_ref[0]]
    line = lax.broadcasted_iota(jnp.int32, (WIDTH, WIDTH), 0)
    lane = lax.broadcasted_iota(jnp.int32, (WIDTH, WIDTH), 1)
    rows = jnp.where(lane == 2 * (line % HALF) + line // HALF, 1.0, 0.0).astype(BF16)
    cols = jnp.where(line == 2 * (lane % HALF) + lane // HALF, 1.0, 0.0).astype(BF16)

    def parts(value):
        high, rest = split(value)
        return high, rest, (value - high.astype(F32) - rest.astype(F32)).astype(BF16)

    x = sum(dot(rows, part) for part in parts(x))
    out_ref[...] = sum(dot(part, cols) for part in parts(x))


def halo_kernel(info_ref, across_ref, beside_ref, out_ref):
    from_beside, kept = masks(info_ref, 1)
    for j in range(2):
        for c in range(2):
            left, right = halo_of(across_ref, beside_ref, (j, c), from_beside, kept)
            out_ref[j, c, :, :HALF] = left
            out_ref[j, c, :, HALF:] = right


def window_kernel(info_ref, own_ref, across_ref, beside_ref, out_ref):
    from_beside, kept = masks(info_ref, 0)
    for j in range(2):
        for c in range(2):
            left, right = halo_of(across_ref, beside_ref, (j, c), from_beside, kept)
            out_ref[j, c, :HALO, :HALF] = left
            out_ref[j, c, :HALO, HALF:] = right
            left, right = columns_of(lambda i: own_ref[j, c, :, i * HALF : (i + 1) * HALF], kept)
            out_ref[j, c, HALO:, :HALF] = left
            out_ref[j, c, HALO:, HALF:] = right


def position_kernel(
    info_ref,
    offsets_ref,
    tables_ref,
    probe_ref,
    amp_ref,
    own_ref,
    core_ref,
    halo_ref,
    keep_out,
    send_out,
    core_out,
    beside_out,
    early_out,
    late_out,
    waves,
    windows,
    halos,
    offsets,
    sems,
):
    place, odd, turned = here()
    load = pltpu.make_async_copy(offsets_ref, offsets, sems.at[0, 5])
    load.start()
    from_beside = masks(info_ref, 0)[0]
    across_turned = turned
    turned = jnp.where(jnp.concatenate([from_beside, from_beside], axis=1), 0, turned)

    def window_of(s):
        mine = jnp.where(place == s // 2, 1, 0)
        out = []
        for c in range(2):
            halo = jnp.where(turned == mine, halo_ref[s % 2, c], own_ref[s % 2, c, :HALO])
            core = jnp.where(mine == 1, own_ref[s % 2, c, HALO:], core_ref[s % 2, c])
            out.append(jnp.concatenate([halo, core], axis=0))
        return out

    wave = (probe_ref[0], probe_ref[1])
    for s in range(4):
        if s > 0:
            waves[s - 1, 0], waves[s - 1, 1] = wave
        window = window_of(s)
        windows[s, 0], windows[s, 1] = window
        prod = times(wave, window)
        if s < 3:
            wave = propagate(prod, tables_ref)
    field = right_mult((fold(prod[0]), fold(prod[1])), tables_ref, FAR_RIGHT)
    field = left_mult(field, tables_ref, FAR_LEFT)
    model = jnp.sqrt(field[0] * field[0] + field[1] * field[1] + 1.0)
    ratio = (model - amp_ref[...]) / model
    grad = (field[0] * ratio, -(field[1] * ratio))
    grad = right_mult(grad, tables_ref, BACK_RIGHT)
    grad = left_mult(grad, tables_ref, BACK_LEFT)
    grad = (fold(grad[0]), fold(grad[1]))
    copies = []
    for s in range(3, -1, -1):
        wave = (waves[s - 1, 0], waves[s - 1, 1]) if s > 0 else (probe_ref[0], probe_ref[1])
        object_grad = times(wave, grad)
        slot = jnp.where(place == s // 2, s % 2, 2 + s % 2)
        for c in range(2):
            value = object_grad[c] if c == 0 else -object_grad[c]
            core_out[slot, c] = value[HALO:]
            halos[slot, pl.ds(c * HALO, HALO)] = value[:HALO]
        start = pl.multiple_of(slot * 2 * HALO, HALO)
        copy = pltpu.make_async_copy(halos.at[slot], beside_out.at[pl.ds(start, 2 * HALO)], sems.at[0, s])
        copy.start()
        copies.append(copy)
        start = pl.multiple_of(s % 2 * 2 * HALO, HALO)
        early = jnp.where(slot // 2 == 1, 1, 0) != across_turned
        for which, ref in enumerate((late_out, early_out)):
            copy = pltpu.make_async_copy(halos.at[slot], ref.at[pl.ds(start, 2 * HALO)], sems.at[1, s])

            @pl.when(early == (which == 1))
            def _():
                copy.start()

        copies.append(copy)
        grad = times((windows[s, 0], windows[s, 1]), grad)
        if s > 0:
            grad = propagate(grad, tables_ref)
    meta = info_ref[...].astype(F32)
    halos[4, :8] = jnp.concatenate([meta, meta], axis=1)
    for i, (ref, start) in enumerate(((beside_out, 8 * HALO), (early_out, 4 * HALO))):
        copy = pltpu.make_async_copy(halos.at[4, :8], ref.at[pl.ds(start, 8)], sems.at[i, 4])
        copy.start()
        copies.append(copy)
    load.wait()
    row, col = offsets[place, 0], offsets[place, 1]
    value = [grad[0], -grad[1]]
    for c in range(2):
        value[c] = pltpu.roll(value[c], lax.rem(WIDTH - row, WIDTH), 0)
        value[c] = pltpu.roll(value[c], lax.rem(WIDTH - col, WIDTH), 1)
    for ref, which in ((keep_out, odd), (send_out, 1 - odd)):
        part = jnp.where(which == 0, value[0], value[1])
        for h in range(2):
            ref[:, h] = part[:, h * HALF : (h + 1) * HALF].reshape(WIDTH // 8, 8, HALF)
    for copy in copies:
        copy.wait()


def widen(x, kept):
    left, right = x[..., :HALF], x[..., HALF:]
    return jnp.concatenate([jnp.where(kept, left, 0.0), right, jnp.where(kept, 0.0, left)], axis=-1)


def add_halos(info_ref, core_ref, across_ref, early_ref, beside_ref, out_ref, first, extra=None):
    odd = here()[1]
    own_kept = masks(info_ref, 0)[1]
    line = lax.broadcasted_iota(jnp.int32, (HALO, WIDTH), 0).astype(F32)
    column = lax.broadcasted_iota(jnp.int32, (HALO, HALF), 1).astype(F32)
    sides = []
    for ref, base, meta, after in (
        (across_ref, 0, early_ref[4 * HALO :], odd),
        (beside_ref, first * 2 * HALO, beside_ref[8 * HALO :], 1 - odd),
    ):
        kept = column >= meta[1:2, :HALF]
        mask = jnp.where(line >= meta[0:1], 1, 0) == after
        sides.append((ref, base, mask, kept))
    for j in range(2):
        for c in range(2):
            total = widen(core_ref[first + j, c], own_kept)
            for ref, base, mask, kept in sides:
                start = base + (j * 2 + c) * HALO
                total = total + widen(jnp.where(mask, ref[start : start + HALO], 0.0), kept)
            out_ref[j, c] = total if extra is None else total + extra[j, c]


def add_kernel(keep_ref, got_ref, out_ref):
    out_ref[...] = keep_ref[...] + got_ref[...]


def reduce_kernel(parts_ref, out_ref):
    out_ref[...] = jnp.sum(parts_ref[...], axis=0)


def total_kernel(first_ref, second_ref, out_ref):
    total = first_ref[...] + second_ref[...]
    out_ref[...] = jnp.broadcast_to(total[None], out_ref.shape)


def sum_kernel(info_ref, core_ref, early_ref, beside_ref, after_ref, out_ref):
    add_halos(info_ref, core_ref, early_ref, early_ref, beside_ref, out_ref, 2)


def finish_kernel(
    info_ref,
    core_ref,
    early_ref,
    beside_ref,
    late_ref,
    swapped_ref,
    keep_ref,
    got_ref,
    object_out,
    probe_out,
):
    add_halos(info_ref, core_ref, late_ref, early_ref, beside_ref, object_out, 0, swapped_ref)
    odd = here()[1]
    for ref, which in ((keep_ref, odd), (got_ref, 1 - odd)):
        for h in range(2):
            probe_out[which, :, h * HALF : (h + 1) * HALF] = ref[:, h].reshape(WIDTH, HALF)


def call(kernel, shapes, smem, vmem, name, scratch=(), flops=0, nbytes=2_000_000, ins=None, outs=None, vmem_limit=40):
    single = isinstance(shapes[0], int)
    shapes = (shapes,) if single else shapes
    out = pl.pallas_call(
        kernel,
        out_shape=tuple(jax.ShapeDtypeStruct(shape, F32) for shape in shapes),
        in_specs=[SMEM] * len(smem) + list(ins or [VMEM] * len(vmem)),
        out_specs=outs or (VMEM,) * len(shapes),
        scratch_shapes=scratch,
        compiler_params=pltpu.CompilerParams(vmem_limit_bytes=vmem_limit * 1024 * 1024),
        cost_estimate=pl.CostEstimate(flops=flops, bytes_accessed=nbytes, transcendentals=0),
        name=name,
    )(*smem, *vmem)
    return out[0] if single else out


def swap_tile(x, beside):
    slabs, tiles = lax.axis_size("slab"), lax.axis_size("tile")
    pairs = []
    for slab in range(slabs):
        for tile in range(tiles):
            to = (tile + (1 if tile % 2 != beside else -1)) % tiles
            turned = tile // (tiles // 2) != to // (tiles // 2)
            pairs.append((slab * tiles + tile, (slab ^ turned) * tiles + to))
    return lax.ppermute(x, ("slab", "tile"), pairs)


def swap_core(x):
    count = lax.axis_size("tile")
    return lax.ppermute(x, "tile", [(i, i ^ 1) for i in range(count)])


def among_columns(x):
    slabs, tiles = lax.axis_size("slab"), lax.axis_size("tile")
    half = tiles // 2
    planes = [slab * tiles + far * half for slab in range(slabs) for far in range(2)]
    groups = [[plane + i for i in range(core, half, 2)] for plane in planes for core in range(2)]
    return lax.all_to_all(x, ("slab", "tile"), 0, 0, tiled=True, axis_index_groups=groups)


def swap_far(x):
    slabs, tiles = lax.axis_size("slab"), lax.axis_size("tile")
    half = tiles // 2
    pairs = [
        (slab * tiles + tile, (slabs - 1 - slab) * tiles + (tile + half) % tiles)
        for slab in range(slabs)
        for tile in range(tiles)
    ]
    return lax.ppermute(x, ("slab", "tile"), pairs)


def swap_slab(x):
    return lax.ppermute(x, "slab", [(0, 1), (1, 0)])


def shards(transmission, probe, scan_offsets, amplitudes):
    tables = jnp.asarray(make_tables())
    index = lax.axis_index("slab").astype(jnp.int32)
    where = (index.reshape(1), scan_offsets)
    info = jnp.where(index == 0, scan_offsets, scan_offsets[::-1]).reshape(4, 1)
    info = jnp.broadcast_to(jnp.concatenate([info, info]), (8, HALF))
    own = transmission
    part, whole, band = (2, 2, HALO, WIDTH), (2, 2, WIDTH, WIDTH), (2, 2, HALO, COLS)

    own_hbm, offsets_hbm = (pltpu.with_memory_space_constraint(x, pltpu.HBM) for x in (own, scan_offsets))
    core = call(
        core_kernel,
        part,
        (),
        (offsets_hbm, own_hbm),
        "core",
        scratch=[
            pltpu.SMEM((2, 2), jnp.int32),
            pltpu.VMEM((4, HALO, HALF), F32),
            pltpu.VMEM((4, HALO, HALF), F32),
            pltpu.SemaphoreType.DMA((3, 5)),
        ],
        ins=(HBM, HBM),
    )
    core = swap_slab(core)
    beside, across = swap_tile(own, 1), swap_tile(own, 0)
    rolled = call(roll_probe_kernel, (2, WIDTH, WIDTH), where, (probe,), "roll")
    amp = call(amp_kernel, (WIDTH, WIDTH), where, (amplitudes,), "amp")
    halo = swap_slab(call(halo_kernel, part, (), (info, across, beside), "halo"))
    windows = call(window_kernel, whole, (), (info, own, across, beside), "window")

    tiles = (WIDTH // 8, 2, 8, HALF)
    keep, send, cores, beside, early, late = call(
        position_kernel,
        (tiles, tiles, (4, 2, HALO, WIDTH), (8 * HALO + 8, WIDTH), (4 * HALO + 8, WIDTH), (4 * HALO, WIDTH)),
        (),
        (info, scan_offsets, tables, rolled, amp, windows, core, halo),
        "position",
        scratch=[
            pltpu.VMEM((3, 2, WIDTH, WIDTH), F32),
            pltpu.VMEM((4, 2, WIDTH, WIDTH), F32),
            pltpu.VMEM((5, 2 * HALO, WIDTH), F32),
            pltpu.SMEM((2, 2), jnp.int32),
            pltpu.SemaphoreType.DMA((2, 6)),
        ],
        ins=(VMEM, HBM) + (VMEM,) * 6,
        flops=3_300_000_000,
        nbytes=10_000_000,
        outs=(VMEM, VMEM, VMEM, HBM, HBM, HBM),
    )
    sides = (info, cores, swap_tile(early, 0), swap_tile(beside, 1))
    parts = (WIDTH // 16, 4, 8, HALF)
    kept = call(add_kernel, tiles, (), (keep, swap_core(send)), "add").reshape(parts)
    kept = call(reduce_kernel, parts[1:], (), (among_columns(kept),), "reduce")
    late, kept = lax.optimization_barrier((late, kept))
    late = swap_tile(late, 0)
    kept = call(add_kernel, parts[1:], (), (kept, swap_slab(kept)), "add_slabs")
    got = swap_slab(call(sum_kernel, band, (), sides + (kept,), "sum"))
    kept = call(total_kernel, parts, (), (kept, swap_far(kept)), "total")
    kept = among_columns(kept)
    object_grad, probe_grad = call(
        finish_kernel,
        (band, probe.shape),
        (),
        sides + (late, got, kept.reshape(tiles), swap_core(kept).reshape(tiles)),
        "finish",
    )
    return object_grad, probe_grad


def solution(mesh):
    placed = (P("slab", None, "tile", None), P(), P("tile", None), P("tile", None, None))
    return jax.shard_map(
        shards,
        mesh=mesh,
        in_specs=placed,
        out_specs=(P("slab", None, "tile", None), P()),
        check_vma=False,
    )
```

```python
import functools

import jax
import jax.numpy as jnp
import numpy as np
from jax import lax
from jax.experimental import pallas as pl
from jax.experimental.pallas import tpu as pltpu
from jax.sharding import PartitionSpec as P

WIDTH = 256
HALF = 128
HALO = 128
COLS = 384
PROP_STRENGTH = 12.0
BF16 = jnp.bfloat16
F32 = jnp.float32
VMEM = pl.BlockSpec(memory_space=pltpu.VMEM)
SMEM = pl.BlockSpec(memory_space=pltpu.SMEM)
HBM = pl.BlockSpec(memory_space=pltpu.HBM)


def high_low(table):
    table = table.astype(np.float32)
    high = table.astype(jnp.bfloat16)
    low = (table - high.astype(np.float32)).astype(jnp.bfloat16)
    return np.stack([high, low])


def on_right(m):
    return high_low(np.block([[m.real, m.imag], [-m.imag, m.real]]))


def on_left(m):
    return high_low(np.block([[m.real, -m.imag], [m.imag, m.real]]))


def make_tables():
    index = np.arange(WIDTH)
    dft = np.exp(-2j * np.pi / WIDTH * (index[:, None] * index[None, :] % WIDTH)) / np.sqrt(WIDTH)
    freq = ((index + WIDTH // 2) % WIDTH - WIDTH // 2) / WIDTH
    phase = np.exp(-1j * PROP_STRENGTH * freq**2)
    prop = dft.conj() @ (phase[:, None] * dft)
    far = phase[:, None] * dft
    p, q = prop[:HALF, :HALF], prop[:HALF, HALF:]
    props = ((p + q) / 2, (p - q) / 2)
    fars = (far[0::2, :HALF], far[1::2, :HALF])
    return np.stack(
        [
            np.stack([on_right(m) for m in props]),
            np.stack([on_left(m) for m in props]),
            np.stack([on_right(m.T) for m in fars]),
            np.stack([on_left(m) for m in fars]),
            np.stack([on_right(m) for m in fars]),
            np.stack([on_left(m.T) for m in fars]),
        ]
    )


PROP_RIGHT, PROP_LEFT, FAR_RIGHT, FAR_LEFT, BACK_RIGHT, BACK_LEFT = range(6)


def split(x):
    high = x.astype(BF16)
    low = (x - high.astype(F32)).astype(BF16)
    return high, low


def dot(a, b):
    return jnp.dot(a, b, preferred_element_type=F32)


def fold(x):
    x = jnp.concatenate([x[:HALF] + x[HALF:], x[:HALF] - x[HALF:]], axis=0)
    return jnp.concatenate([x[:, :HALF] + x[:, HALF:], x[:, :HALF] - x[:, HALF:]], axis=1)


def right_mult(x, tables, which):
    re, im = [], []
    for h in range(2):
        part = slice(h * HALF, (h + 1) * HALF)
        high, low = split(jnp.concatenate([x[0][:, part], x[1][:, part]], axis=1))
        th, tl = tables[which, h, 0], tables[which, h, 1]
        out = dot(jnp.concatenate([high, low, high], axis=1), jnp.concatenate([th, th, tl], axis=0))
        re.append(out[:, :HALF])
        im.append(out[:, HALF:])
    return jnp.concatenate(re, axis=1), jnp.concatenate(im, axis=1)


def left_mult(x, tables, which):
    re, im = [], []
    for h in range(2):
        part = slice(h * HALF, (h + 1) * HALF)
        high, low = split(jnp.concatenate([x[0][part], x[1][part]], axis=0))
        th, tl = tables[which, h, 0], tables[which, h, 1]
        out = dot(jnp.concatenate([th, th, tl], axis=1), jnp.concatenate([high, low, high], axis=0))
        re.append(out[:HALF])
        im.append(out[HALF:])
    return jnp.concatenate(re, axis=0), jnp.concatenate(im, axis=0)


def propagate(x, tables):
    y = right_mult((fold(x[0]), fold(x[1])), tables, PROP_RIGHT)
    y = left_mult(y, tables, PROP_LEFT)
    return fold(y[0]), fold(y[1])


def times(a, b):
    return a[0] * b[0] - a[1] * b[1], a[0] * b[1] + a[1] * b[0]


def here():
    half = lax.axis_size("tile") // 2
    within = lax.axis_index("tile") % half
    turned = jnp.where((within == 0) | (within == half - 1), 1, 0)
    return lax.axis_index("slab"), within % 2, turned


def masks(info_ref, which):
    row = jnp.broadcast_to(info_ref[2 * which : 2 * which + 1], (HALO, HALF))
    col = jnp.broadcast_to(info_ref[2 * which + 1 : 2 * which + 2], (HALO, HALF))
    line = lax.broadcasted_iota(jnp.int32, (HALO, HALF), 0)
    lane = lax.broadcasted_iota(jnp.int32, (HALO, HALF), 1)
    return jnp.where(line >= row, 1, 0) == here()[1], lane >= col


def columns_of(x, kept):
    return jnp.where(kept, x(0), x(2)), x(1)


def halo_of(across_ref, beside_ref, at, from_beside, kept):
    def column(i):
        cols = slice(i * HALF, (i + 1) * HALF)
        return jnp.where(from_beside, beside_ref[at + (slice(None), cols)], across_ref[at + (slice(None), cols)])

    return columns_of(column, kept)


def roll_probe_kernel(place_ref, offsets_ref, probe_ref, out_ref):
    row, col = offsets_ref[place_ref[0], 0], offsets_ref[place_ref[0], 1]
    for c in range(2):
        out_ref[c] = pltpu.roll(pltpu.roll(probe_ref[c], row, 0), col, 1)


def core_kernel(offsets_ref, own_ref, out_ref, offsets, left, right, sems):
    load = pltpu.make_async_copy(offsets_ref, offsets, sems.at[0, 4])
    load.start()
    loads = []
    for i in range(4):
        at = (i // 2, i % 2, slice(None))
        loads.append(
            [
                pltpu.make_async_copy(own_ref.at[at + (slice(0, HALF),)], left.at[i], sems.at[0, i]),
                pltpu.make_async_copy(own_ref.at[at + (slice(WIDTH, COLS),)], right.at[i], sems.at[1, i]),
                pltpu.make_async_copy(
                    own_ref.at[at + (slice(HALF, WIDTH),)], out_ref.at[at + (slice(HALF, WIDTH),)], sems.at[2, i]
                ),
            ]
        )
        for copy in loads[i]:
            copy.start()
    load.wait()
    lane = lax.broadcasted_iota(jnp.int32, (HALO, HALF), 1)
    kept = lane >= offsets[1 - lax.axis_index("slab"), 1]
    for i in range(4):
        loads[i][0].wait()
        loads[i][1].wait()
        out_ref[i // 2, i % 2, :, :HALF] = jnp.where(kept, left[i], right[i])
    for i in range(4):
        loads[i][2].wait()


def amp_kernel(place_ref, offsets_ref, amp_ref, out_ref):
    x = amp_ref[place_ref[0]]
    line = lax.broadcasted_iota(jnp.int32, (WIDTH, WIDTH), 0)
    lane = lax.broadcasted_iota(jnp.int32, (WIDTH, WIDTH), 1)
    rows = jnp.where(lane == 2 * (line % HALF) + line // HALF, 1.0, 0.0).astype(BF16)
    cols = jnp.where(line == 2 * (lane % HALF) + lane // HALF, 1.0, 0.0).astype(BF16)

    def parts(value):
        high, rest = split(value)
        return high, rest, (value - high.astype(F32) - rest.astype(F32)).astype(BF16)

    x = sum(dot(rows, part) for part in parts(x))
    out_ref[...] = sum(dot(part, cols) for part in parts(x))


def halo_kernel(info_ref, across_ref, beside_ref, out_ref):
    from_beside, kept = masks(info_ref, 1)
    for j in range(2):
        for c in range(2):
            left, right = halo_of(across_ref, beside_ref, (j, c), from_beside, kept)
            out_ref[j, c, :, :HALF] = left
            out_ref[j, c, :, HALF:] = right


def window_kernel(info_ref, own_ref, across_ref, beside_ref, out_ref):
    from_beside, kept = masks(info_ref, 0)
    for j in range(2):
        for c in range(2):
            left, right = halo_of(across_ref, beside_ref, (j, c), from_beside, kept)
            out_ref[j, c, :HALO, :HALF] = left
            out_ref[j, c, :HALO, HALF:] = right
            left, right = columns_of(lambda i: own_ref[j, c, :, i * HALF : (i + 1) * HALF], kept)
            out_ref[j, c, HALO:, :HALF] = left
            out_ref[j, c, HALO:, HALF:] = right


def position_kernel(
    info_ref,
    offsets_ref,
    tables_ref,
    probe_ref,
    amp_ref,
    own_ref,
    core_ref,
    halo_ref,
    keep_out,
    send_out,
    core_out,
    beside_out,
    early_out,
    late_out,
    waves,
    windows,
    halos,
    offsets,
    sems,
):
    place, odd, turned = here()
    load = pltpu.make_async_copy(offsets_ref, offsets, sems.at[0, 5])
    load.start()
    from_beside = masks(info_ref, 0)[0]
    across_turned = turned
    turned = jnp.where(jnp.concatenate([from_beside, from_beside], axis=1), 0, turned)

    def window_of(s):
        mine = jnp.where(place == s // 2, 1, 0)
        out = []
        for c in range(2):
            halo = jnp.where(turned == mine, halo_ref[s % 2, c], own_ref[s % 2, c, :HALO])
            core = jnp.where(mine == 1, own_ref[s % 2, c, HALO:], core_ref[s % 2, c])
            out.append(jnp.concatenate([halo, core], axis=0))
        return out

    wave = (probe_ref[0], probe_ref[1])
    for s in range(4):
        if s > 0:
            waves[s - 1, 0], waves[s - 1, 1] = wave
        window = window_of(s)
        windows[s, 0], windows[s, 1] = window
        prod = times(wave, window)
        if s < 3:
            wave = propagate(prod, tables_ref)
    field = right_mult((fold(prod[0]), fold(prod[1])), tables_ref, FAR_RIGHT)
    field = left_mult(field, tables_ref, FAR_LEFT)
    model = jnp.sqrt(field[0] * field[0] + field[1] * field[1] + 1.0)
    ratio = (model - amp_ref[...]) / model
    grad = (field[0] * ratio, -(field[1] * ratio))
    grad = right_mult(grad, tables_ref, BACK_RIGHT)
    grad = left_mult(grad, tables_ref, BACK_LEFT)
    grad = (fold(grad[0]), fold(grad[1]))
    copies = []
    for s in range(3, -1, -1):
        wave = (waves[s - 1, 0], waves[s - 1, 1]) if s > 0 else (probe_ref[0], probe_ref[1])
        object_grad = times(wave, grad)
        slot = jnp.where(place == s // 2, s % 2, 2 + s % 2)
        for c in range(2):
            value = object_grad[c] if c == 0 else -object_grad[c]
            core_out[slot, c] = value[HALO:]
            halos[slot, pl.ds(c * HALO, HALO)] = value[:HALO]
        start = pl.multiple_of(slot * 2 * HALO, HALO)
        copy = pltpu.make_async_copy(halos.at[slot], beside_out.at[pl.ds(start, 2 * HALO)], sems.at[0, s])
        copy.start()
        copies.append(copy)
        start = pl.multiple_of(s % 2 * 2 * HALO, HALO)
        early = jnp.where(slot // 2 == 1, 1, 0) != across_turned
        for which, ref in enumerate((late_out, early_out)):
            copy = pltpu.make_async_copy(halos.at[slot], ref.at[pl.ds(start, 2 * HALO)], sems.at[1, s])

            @pl.when(early == (which == 1))
            def _():
                copy.start()

        copies.append(copy)
        grad = times((windows[s, 0], windows[s, 1]), grad)
        if s > 0:
            grad = propagate(grad, tables_ref)
    meta = info_ref[...].astype(F32)
    halos[4, :8] = jnp.concatenate([meta, meta], axis=1)
    for i, (ref, start) in enumerate(((beside_out, 8 * HALO), (early_out, 4 * HALO))):
        copy = pltpu.make_async_copy(halos.at[4, :8], ref.at[pl.ds(start, 8)], sems.at[i, 4])
        copy.start()
        copies.append(copy)
    load.wait()
    row, col = offsets[place, 0], offsets[place, 1]
    value = [grad[0], -grad[1]]
    for c in range(2):
        value[c] = pltpu.roll(value[c], lax.rem(WIDTH - row, WIDTH), 0)
        value[c] = pltpu.roll(value[c], lax.rem(WIDTH - col, WIDTH), 1)
    for ref, which in ((keep_out, odd), (send_out, 1 - odd)):
        part = jnp.where(which == 0, value[0], value[1])
        for h in range(2):
            ref[:, h] = part[:, h * HALF : (h + 1) * HALF].reshape(WIDTH // 8, 8, HALF)
    for copy in copies:
        copy.wait()


def widen(x, kept):
    left, right = x[..., :HALF], x[..., HALF:]
    return jnp.concatenate([jnp.where(kept, left, 0.0), right, jnp.where(kept, 0.0, left)], axis=-1)


def add_halos(info_ref, core_ref, across_ref, early_ref, beside_ref, out_ref, first, extra=None):
    odd = here()[1]
    own_kept = masks(info_ref, 0)[1]
    line = lax.broadcasted_iota(jnp.int32, (HALO, WIDTH), 0).astype(F32)
    column = lax.broadcasted_iota(jnp.int32, (HALO, HALF), 1).astype(F32)
    sides = []
    for ref, base, meta, after in (
        (across_ref, 0, early_ref[4 * HALO :], odd),
        (beside_ref, first * 2 * HALO, beside_ref[8 * HALO :], 1 - odd),
    ):
        kept = column >= meta[1:2, :HALF]
        mask = jnp.where(line >= meta[0:1], 1, 0) == after
        sides.append((ref, base, mask, kept))
    for j in range(2):
        for c in range(2):
            total = widen(core_ref[first + j, c], own_kept)
            for ref, base, mask, kept in sides:
                start = base + (j * 2 + c) * HALO
                total = total + widen(jnp.where(mask, ref[start : start + HALO], 0.0), kept)
            out_ref[j, c] = total if extra is None else total + extra[j, c]


def add_kernel(keep_ref, got_ref, out_ref):
    out_ref[...] = keep_ref[...] + got_ref[...]


def reduce_kernel(parts_ref, out_ref):
    out_ref[...] = jnp.sum(parts_ref[...], axis=0)


def total_kernel(first_ref, second_ref, out_ref):
    total = first_ref[...] + second_ref[...]
    out_ref[...] = jnp.broadcast_to(total[None], out_ref.shape)


def sum_kernel(info_ref, core_ref, early_ref, beside_ref, after_ref, out_ref):
    add_halos(info_ref, core_ref, early_ref, early_ref, beside_ref, out_ref, 2)


def object_kernel(info_ref, core_ref, early_ref, beside_ref, late_ref, swapped_ref, after_ref, out_ref, token_ref):
    token_ref[...] = jnp.zeros(token_ref.shape, F32)
    add_halos(info_ref, core_ref, late_ref, early_ref, beside_ref, out_ref, 0, swapped_ref)


def probe_kernel(after_ref, keep_ref, got_ref, out_ref):
    odd = here()[1]
    for ref, which in ((keep_ref, odd), (got_ref, 1 - odd)):
        for h in range(2):
            out_ref[which, :, h * HALF : (h + 1) * HALF] = ref[:, h].reshape(WIDTH, HALF)


def call(kernel, shapes, smem, vmem, name, scratch=(), flops=0, nbytes=2_000_000, ins=None, outs=None, vmem_limit=40):
    single = isinstance(shapes[0], int)
    shapes = (shapes,) if single else shapes
    out = pl.pallas_call(
        kernel,
        out_shape=tuple(jax.ShapeDtypeStruct(shape, F32) for shape in shapes),
        in_specs=[SMEM] * len(smem) + list(ins or [VMEM] * len(vmem)),
        out_specs=outs or (VMEM,) * len(shapes),
        scratch_shapes=scratch,
        compiler_params=pltpu.CompilerParams(vmem_limit_bytes=vmem_limit * 1024 * 1024),
        cost_estimate=pl.CostEstimate(flops=flops, bytes_accessed=nbytes, transcendentals=0),
        name=name,
    )(*smem, *vmem)
    return out[0] if single else out


def swap_tile(x, beside):
    slabs, tiles = lax.axis_size("slab"), lax.axis_size("tile")
    pairs = []
    for slab in range(slabs):
        for tile in range(tiles):
            to = (tile + (1 if tile % 2 != beside else -1)) % tiles
            turned = tile // (tiles // 2) != to // (tiles // 2)
            pairs.append((slab * tiles + tile, (slab ^ turned) * tiles + to))
    return lax.ppermute(x, ("slab", "tile"), pairs)


def swap_core(x):
    count = lax.axis_size("tile")
    return lax.ppermute(x, "tile", [(i, i ^ 1) for i in range(count)])


def among_columns(x):
    slabs, tiles = lax.axis_size("slab"), lax.axis_size("tile")
    half = tiles // 2
    planes = [slab * tiles + far * half for slab in range(slabs) for far in range(2)]
    groups = [[plane + i for i in range(core, half, 2)] for plane in planes for core in range(2)]
    return lax.all_to_all(x, ("slab", "tile"), 0, 0, tiled=True, axis_index_groups=groups)


def swap_far(x):
    slabs, tiles = lax.axis_size("slab"), lax.axis_size("tile")
    half = tiles // 2
    pairs = [
        (slab * tiles + tile, (slabs - 1 - slab) * tiles + (tile + half) % tiles)
        for slab in range(slabs)
        for tile in range(tiles)
    ]
    return lax.ppermute(x, ("slab", "tile"), pairs)


def swap_slab(x):
    return lax.ppermute(x, "slab", [(0, 1), (1, 0)])


def shards(transmission, probe, scan_offsets, amplitudes):
    tables = jnp.asarray(make_tables())
    index = lax.axis_index("slab").astype(jnp.int32)
    where = (index.reshape(1), scan_offsets)
    info = jnp.where(index == 0, scan_offsets, scan_offsets[::-1]).reshape(4, 1)
    info = jnp.broadcast_to(jnp.concatenate([info, info]), (8, HALF))
    own = transmission
    part, whole, band = (2, 2, HALO, WIDTH), (2, 2, WIDTH, WIDTH), (2, 2, HALO, COLS)

    own_hbm, offsets_hbm = (pltpu.with_memory_space_constraint(x, pltpu.HBM) for x in (own, scan_offsets))
    core = call(
        core_kernel,
        part,
        (),
        (offsets_hbm, own_hbm),
        "core",
        scratch=[
            pltpu.SMEM((2, 2), jnp.int32),
            pltpu.VMEM((4, HALO, HALF), F32),
            pltpu.VMEM((4, HALO, HALF), F32),
            pltpu.SemaphoreType.DMA((3, 5)),
        ],
        ins=(HBM, HBM),
    )
    core = swap_slab(core)
    beside, across = swap_tile(own, 1), swap_tile(own, 0)
    rolled = call(roll_probe_kernel, (2, WIDTH, WIDTH), where, (probe,), "roll")
    amp = call(amp_kernel, (WIDTH, WIDTH), where, (amplitudes,), "amp")
    halo = swap_slab(call(halo_kernel, part, (), (info, across, beside), "halo"))
    windows = call(window_kernel, whole, (), (info, own, across, beside), "window")

    tiles = (WIDTH // 8, 2, 8, HALF)
    keep, send, cores, beside, early, late = call(
        position_kernel,
        (tiles, tiles, (4, 2, HALO, WIDTH), (8 * HALO + 8, WIDTH), (4 * HALO + 8, WIDTH), (4 * HALO, WIDTH)),
        (),
        (info, scan_offsets, tables, rolled, amp, windows, core, halo),
        "position",
        scratch=[
            pltpu.VMEM((3, 2, WIDTH, WIDTH), F32),
            pltpu.VMEM((4, 2, WIDTH, WIDTH), F32),
            pltpu.VMEM((5, 2 * HALO, WIDTH), F32),
            pltpu.SMEM((2, 2), jnp.int32),
            pltpu.SemaphoreType.DMA((2, 6)),
        ],
        ins=(VMEM, HBM) + (VMEM,) * 6,
        flops=3_300_000_000,
        nbytes=10_000_000,
        outs=(VMEM, VMEM, VMEM, HBM, HBM, HBM),
    )
    sides = (info, cores, swap_tile(early, 0), swap_tile(beside, 1))
    parts = (WIDTH // 16, 4, 8, HALF)
    kept = call(add_kernel, tiles, (), (keep, swap_core(send)), "add").reshape(parts)
    kept = call(reduce_kernel, parts[1:], (), (among_columns(kept),), "reduce")
    late, kept = lax.optimization_barrier((late, kept))
    late = swap_tile(late, 0)
    kept = call(add_kernel, parts[1:], (), (kept, swap_slab(kept)), "add_slabs")
    got = swap_slab(call(sum_kernel, band, (), sides + (kept,), "sum"))
    kept = call(total_kernel, parts, (), (kept, swap_far(kept)), "total")
    kept = among_columns(kept)
    other = swap_core(kept)
    object_grad, token = call(object_kernel, (band, (8, HALF)), (), sides + (late, got, kept), "object")
    probe_grad = call(
        probe_kernel,
        probe.shape,
        (),
        (token, kept.reshape(tiles), other.reshape(tiles)),
        "probe",
    )
    return object_grad, probe_grad


def solution(mesh):
    placed = (P("slab", None, "tile", None), P(), P("tile", None), P("tile", None, None))
    return jax.shard_map(
        shards,
        mesh=mesh,
        in_specs=placed,
        out_specs=(P("slab", None, "tile", None), P()),
        check_vma=False,
    )
```

```python
import functools

import jax
import jax.numpy as jnp
import numpy as np
from jax import lax
from jax.experimental import pallas as pl
from jax.experimental.pallas import tpu as pltpu
from jax.sharding import PartitionSpec as P

WIDTH = 256
HALF = 128
HALO = 128
COLS = 384
PROP_STRENGTH = 12.0
BF16 = jnp.bfloat16
F32 = jnp.float32
VMEM = pl.BlockSpec(memory_space=pltpu.VMEM)
SMEM = pl.BlockSpec(memory_space=pltpu.SMEM)
HBM = pl.BlockSpec(memory_space=pltpu.HBM)


def high_low(table):
    table = table.astype(np.float32)
    high = table.astype(jnp.bfloat16)
    low = (table - high.astype(np.float32)).astype(jnp.bfloat16)
    return np.stack([high, low])


def on_right(m):
    return high_low(np.block([[m.real, m.imag], [-m.imag, m.real]]))


def on_left(m):
    return high_low(np.block([[m.real, -m.imag], [m.imag, m.real]]))


def make_tables():
    index = np.arange(WIDTH)
    dft = np.exp(-2j * np.pi / WIDTH * (index[:, None] * index[None, :] % WIDTH)) / np.sqrt(WIDTH)
    freq = ((index + WIDTH // 2) % WIDTH - WIDTH // 2) / WIDTH
    phase = np.exp(-1j * PROP_STRENGTH * freq**2)
    prop = dft.conj() @ (phase[:, None] * dft)
    far = phase[:, None] * dft
    p, q = prop[:HALF, :HALF], prop[:HALF, HALF:]
    props = ((p + q) / 2, (p - q) / 2)
    fars = (far[0::2, :HALF], far[1::2, :HALF])
    return np.stack(
        [
            np.stack([on_right(m) for m in props]),
            np.stack([on_left(m) for m in props]),
            np.stack([on_right(m.T) for m in fars]),
            np.stack([on_left(m) for m in fars]),
            np.stack([on_right(m) for m in fars]),
            np.stack([on_left(m.T) for m in fars]),
        ]
    )


PROP_RIGHT, PROP_LEFT, FAR_RIGHT, FAR_LEFT, BACK_RIGHT, BACK_LEFT = range(6)


def split(x):
    high = x.astype(BF16)
    low = (x - high.astype(F32)).astype(BF16)
    return high, low


def dot(a, b):
    return jnp.dot(a, b, preferred_element_type=F32)


def fold(x):
    x = jnp.concatenate([x[:HALF] + x[HALF:], x[:HALF] - x[HALF:]], axis=0)
    return jnp.concatenate([x[:, :HALF] + x[:, HALF:], x[:, :HALF] - x[:, HALF:]], axis=1)


def right_mult(x, tables, which):
    re, im = [], []
    for h in range(2):
        part = slice(h * HALF, (h + 1) * HALF)
        high, low = split(jnp.concatenate([x[0][:, part], x[1][:, part]], axis=1))
        th, tl = tables[which, h, 0], tables[which, h, 1]
        out = dot(jnp.concatenate([high, low, high], axis=1), jnp.concatenate([th, th, tl], axis=0))
        re.append(out[:, :HALF])
        im.append(out[:, HALF:])
    return jnp.concatenate(re, axis=1), jnp.concatenate(im, axis=1)


def left_mult(x, tables, which):
    re, im = [], []
    for h in range(2):
        part = slice(h * HALF, (h + 1) * HALF)
        high, low = split(jnp.concatenate([x[0][part], x[1][part]], axis=0))
        th, tl = tables[which, h, 0], tables[which, h, 1]
        out = dot(jnp.concatenate([th, th, tl], axis=1), jnp.concatenate([high, low, high], axis=0))
        re.append(out[:HALF])
        im.append(out[HALF:])
    return jnp.concatenate(re, axis=0), jnp.concatenate(im, axis=0)


def propagate(x, tables):
    y = right_mult((fold(x[0]), fold(x[1])), tables, PROP_RIGHT)
    y = left_mult(y, tables, PROP_LEFT)
    return fold(y[0]), fold(y[1])


def times(a, b):
    return a[0] * b[0] - a[1] * b[1], a[0] * b[1] + a[1] * b[0]


def here():
    half = lax.axis_size("tile") // 2
    within = lax.axis_index("tile") % half
    turned = jnp.where((within == 0) | (within == half - 1), 1, 0)
    return lax.axis_index("slab"), within % 2, turned


def masks(info_ref, which):
    row = jnp.broadcast_to(info_ref[2 * which : 2 * which + 1], (HALO, HALF))
    col = jnp.broadcast_to(info_ref[2 * which + 1 : 2 * which + 2], (HALO, HALF))
    line = lax.broadcasted_iota(jnp.int32, (HALO, HALF), 0)
    lane = lax.broadcasted_iota(jnp.int32, (HALO, HALF), 1)
    return jnp.where(line >= row, 1, 0) == here()[1], lane >= col


def columns_of(x, kept):
    return jnp.where(kept, x(0), x(2)), x(1)


def halo_of(across_ref, beside_ref, at, from_beside, kept):
    def column(i):
        cols = slice(i * HALF, (i + 1) * HALF)
        return jnp.where(from_beside, beside_ref[at + (slice(None), cols)], across_ref[at + (slice(None), cols)])

    return columns_of(column, kept)


def roll_probe_kernel(place_ref, offsets_ref, probe_ref, out_ref):
    row, col = offsets_ref[place_ref[0], 0], offsets_ref[place_ref[0], 1]
    for c in range(2):
        out_ref[c] = pltpu.roll(pltpu.roll(probe_ref[c], row, 0), col, 1)


def core_kernel(offsets_ref, own_ref, out_ref, offsets, left, right, sems):
    load = pltpu.make_async_copy(offsets_ref, offsets, sems.at[0, 4])
    load.start()
    loads = []
    for i in range(4):
        at = (i // 2, i % 2, slice(None))
        loads.append(
            [
                pltpu.make_async_copy(own_ref.at[at + (slice(0, HALF),)], left.at[i], sems.at[0, i]),
                pltpu.make_async_copy(own_ref.at[at + (slice(WIDTH, COLS),)], right.at[i], sems.at[1, i]),
                pltpu.make_async_copy(
                    own_ref.at[at + (slice(HALF, WIDTH),)], out_ref.at[at + (slice(HALF, WIDTH),)], sems.at[2, i]
                ),
            ]
        )
        for copy in loads[i]:
            copy.start()
    load.wait()
    lane = lax.broadcasted_iota(jnp.int32, (HALO, HALF), 1)
    kept = lane >= offsets[1 - lax.axis_index("slab"), 1]
    for i in range(4):
        loads[i][0].wait()
        loads[i][1].wait()
        out_ref[i // 2, i % 2, :, :HALF] = jnp.where(kept, left[i], right[i])
    for i in range(4):
        loads[i][2].wait()


def amp_kernel(place_ref, offsets_ref, amp_ref, out_ref):
    x = amp_ref[place_ref[0]]
    line = lax.broadcasted_iota(jnp.int32, (WIDTH, WIDTH), 0)
    lane = lax.broadcasted_iota(jnp.int32, (WIDTH, WIDTH), 1)
    rows = jnp.where(lane == 2 * (line % HALF) + line // HALF, 1.0, 0.0).astype(BF16)
    cols = jnp.where(line == 2 * (lane % HALF) + lane // HALF, 1.0, 0.0).astype(BF16)

    def parts(value):
        high, rest = split(value)
        return high, rest, (value - high.astype(F32) - rest.astype(F32)).astype(BF16)

    x = sum(dot(rows, part) for part in parts(x))
    out_ref[...] = sum(dot(part, cols) for part in parts(x))


def halo_kernel(info_ref, across_ref, beside_ref, first_out, second_out):
    from_beside, kept = masks(info_ref, 1)
    for j, out_ref in enumerate((first_out, second_out)):
        for c in range(2):
            left, right = halo_of(across_ref, beside_ref, (j, c), from_beside, kept)
            out_ref[c, :, :HALF] = left
            out_ref[c, :, HALF:] = right


def window_kernel(info_ref, own_ref, across_ref, beside_ref, out_ref):
    from_beside, kept = masks(info_ref, 0)
    for j in range(2):
        for c in range(2):
            left, right = halo_of(across_ref, beside_ref, (j, c), from_beside, kept)
            out_ref[j, c, :HALO, :HALF] = left
            out_ref[j, c, :HALO, HALF:] = right
            left, right = columns_of(lambda i: own_ref[j, c, :, i * HALF : (i + 1) * HALF], kept)
            out_ref[j, c, HALO:, :HALF] = left
            out_ref[j, c, HALO:, HALF:] = right


def selector(info_ref, own_ref, core_ref, halo_refs):
    place, odd, turned = here()
    from_beside = masks(info_ref, 0)[0]
    turned = jnp.where(jnp.concatenate([from_beside, from_beside], axis=1), 0, turned)

    def window_of(s):
        mine = jnp.where(place == s // 2, 1, 0)
        out = []
        for c in range(2):
            halo = jnp.where(turned == mine, halo_refs[s % 2][c], own_ref[s % 2, c, :HALO])
            core = jnp.where(mine == 1, own_ref[s % 2, c, HALO:], core_ref[s % 2, c])
            out.append(jnp.concatenate([halo, core], axis=0))
        return out

    return window_of


def first_kernel(info_ref, tables_ref, probe_ref, own_ref, core_ref, halo_ref, wave_out, window_out):
    window = selector(info_ref, own_ref, core_ref, (halo_ref, None))(0)
    window_out[0], window_out[1] = window
    wave_out[0], wave_out[1] = propagate(times((probe_ref[0], probe_ref[1]), window), tables_ref)


def position_kernel(
    info_ref,
    offsets_ref,
    tables_ref,
    probe_ref,
    amp_ref,
    own_ref,
    core_ref,
    halo_ref,
    second_halo_ref,
    first_wave_ref,
    first_window_ref,
    keep_out,
    send_out,
    core_out,
    beside_out,
    early_out,
    late_out,
    waves,
    windows,
    halos,
    offsets,
    sems,
):
    place, odd, across_turned = here()
    load = pltpu.make_async_copy(offsets_ref, offsets, sems.at[0, 5])
    load.start()
    window_of = selector(info_ref, own_ref, core_ref, (halo_ref, second_halo_ref))
    wave = (first_wave_ref[0], first_wave_ref[1])
    for s in range(1, 4):
        if s > 1:
            waves[s - 2, 0], waves[s - 2, 1] = wave
        window = window_of(s)
        windows[s - 1, 0], windows[s - 1, 1] = window
        prod = times(wave, window)
        if s < 3:
            wave = propagate(prod, tables_ref)

    def before(s):
        ref = (probe_ref, first_wave_ref, waves.at[0], waves.at[1])[s]
        return ref[0], ref[1]

    def window_at(s):
        ref = first_window_ref if s == 0 else windows.at[s - 1]
        return ref[0], ref[1]

    field = right_mult((fold(prod[0]), fold(prod[1])), tables_ref, FAR_RIGHT)
    field = left_mult(field, tables_ref, FAR_LEFT)
    model = jnp.sqrt(field[0] * field[0] + field[1] * field[1] + 1.0)
    ratio = (model - amp_ref[...]) / model
    grad = (field[0] * ratio, -(field[1] * ratio))
    grad = right_mult(grad, tables_ref, BACK_RIGHT)
    grad = left_mult(grad, tables_ref, BACK_LEFT)
    grad = (fold(grad[0]), fold(grad[1]))
    copies = []
    for s in range(3, -1, -1):
        object_grad = times(before(s), grad)
        slot = jnp.where(place == s // 2, s % 2, 2 + s % 2)
        for c in range(2):
            value = object_grad[c] if c == 0 else -object_grad[c]
            core_out[slot, c] = value[HALO:]
            halos[slot, pl.ds(c * HALO, HALO)] = value[:HALO]
        start = pl.multiple_of(slot * 2 * HALO, HALO)
        copy = pltpu.make_async_copy(halos.at[slot], beside_out.at[pl.ds(start, 2 * HALO)], sems.at[0, s])
        copy.start()
        copies.append(copy)
        start = pl.multiple_of(s % 2 * 2 * HALO, HALO)
        early = jnp.where(slot // 2 == 1, 1, 0) != across_turned
        for which, ref in enumerate((late_out, early_out)):
            copy = pltpu.make_async_copy(halos.at[slot], ref.at[pl.ds(start, 2 * HALO)], sems.at[1, s])

            @pl.when(early == (which == 1))
            def _():
                copy.start()

        copies.append(copy)
        grad = times(window_at(s), grad)
        if s > 0:
            grad = propagate(grad, tables_ref)
    meta = info_ref[...].astype(F32)
    halos[4, :8] = jnp.concatenate([meta, meta], axis=1)
    for i, (ref, start) in enumerate(((beside_out, 8 * HALO), (early_out, 4 * HALO))):
        copy = pltpu.make_async_copy(halos.at[4, :8], ref.at[pl.ds(start, 8)], sems.at[i, 4])
        copy.start()
        copies.append(copy)
    load.wait()
    row, col = offsets[place, 0], offsets[place, 1]
    value = [grad[0], -grad[1]]
    for c in range(2):
        value[c] = pltpu.roll(value[c], lax.rem(WIDTH - row, WIDTH), 0)
        value[c] = pltpu.roll(value[c], lax.rem(WIDTH - col, WIDTH), 1)
    for ref, which in ((keep_out, odd), (send_out, 1 - odd)):
        part = jnp.where(which == 0, value[0], value[1])
        for h in range(2):
            ref[:, h] = part[:, h * HALF : (h + 1) * HALF].reshape(WIDTH // 8, 8, HALF)
    for copy in copies:
        copy.wait()


def widen(x, kept):
    left, right = x[..., :HALF], x[..., HALF:]
    return jnp.concatenate([jnp.where(kept, left, 0.0), right, jnp.where(kept, 0.0, left)], axis=-1)


def add_halos(info_ref, core_ref, across_ref, early_ref, beside_ref, out_ref, first, extra=None):
    odd = here()[1]
    own_kept = masks(info_ref, 0)[1]
    line = lax.broadcasted_iota(jnp.int32, (HALO, WIDTH), 0).astype(F32)
    column = lax.broadcasted_iota(jnp.int32, (HALO, HALF), 1).astype(F32)
    sides = []
    for ref, base, meta, after in (
        (across_ref, 0, early_ref[4 * HALO :], odd),
        (beside_ref, first * 2 * HALO, beside_ref[8 * HALO :], 1 - odd),
    ):
        kept = column >= meta[1:2, :HALF]
        mask = jnp.where(line >= meta[0:1], 1, 0) == after
        sides.append((ref, base, mask, kept))
    for j in range(2):
        for c in range(2):
            total = widen(core_ref[first + j, c], own_kept)
            for ref, base, mask, kept in sides:
                start = base + (j * 2 + c) * HALO
                total = total + widen(jnp.where(mask, ref[start : start + HALO], 0.0), kept)
            out_ref[j, c] = total if extra is None else total + extra[j, c]


def add_kernel(keep_ref, got_ref, out_ref):
    out_ref[...] = keep_ref[...] + got_ref[...]


def reduce_kernel(parts_ref, out_ref):
    out_ref[...] = jnp.sum(parts_ref[...], axis=0)


def total_kernel(first_ref, second_ref, out_ref):
    total = first_ref[...] + second_ref[...]
    out_ref[...] = jnp.broadcast_to(total[None], out_ref.shape)


def sum_kernel(info_ref, core_ref, early_ref, beside_ref, after_ref, out_ref):
    add_halos(info_ref, core_ref, early_ref, early_ref, beside_ref, out_ref, 2)


def object_kernel(info_ref, core_ref, early_ref, beside_ref, late_ref, swapped_ref, after_ref, out_ref, token_ref):
    token_ref[...] = jnp.zeros(token_ref.shape, F32)
    add_halos(info_ref, core_ref, late_ref, early_ref, beside_ref, out_ref, 0, swapped_ref)


def probe_kernel(after_ref, keep_ref, got_ref, out_ref):
    odd = here()[1]
    for ref, which in ((keep_ref, odd), (got_ref, 1 - odd)):
        for h in range(2):
            out_ref[which, :, h * HALF : (h + 1) * HALF] = ref[:, h].reshape(WIDTH, HALF)


def call(kernel, shapes, smem, vmem, name, scratch=(), flops=0, nbytes=2_000_000, ins=None, outs=None, vmem_limit=40):
    single = isinstance(shapes[0], int)
    shapes = (shapes,) if single else shapes
    out = pl.pallas_call(
        kernel,
        out_shape=tuple(jax.ShapeDtypeStruct(shape, F32) for shape in shapes),
        in_specs=[SMEM] * len(smem) + list(ins or [VMEM] * len(vmem)),
        out_specs=outs or (VMEM,) * len(shapes),
        scratch_shapes=scratch,
        compiler_params=pltpu.CompilerParams(vmem_limit_bytes=vmem_limit * 1024 * 1024),
        cost_estimate=pl.CostEstimate(flops=flops, bytes_accessed=nbytes, transcendentals=0),
        name=name,
    )(*smem, *vmem)
    return out[0] if single else out


def swap_tile(x, beside):
    slabs, tiles = lax.axis_size("slab"), lax.axis_size("tile")
    pairs = []
    for slab in range(slabs):
        for tile in range(tiles):
            to = (tile + (1 if tile % 2 != beside else -1)) % tiles
            turned = tile // (tiles // 2) != to // (tiles // 2)
            pairs.append((slab * tiles + tile, (slab ^ turned) * tiles + to))
    return lax.ppermute(x, ("slab", "tile"), pairs)


def swap_core(x):
    count = lax.axis_size("tile")
    return lax.ppermute(x, "tile", [(i, i ^ 1) for i in range(count)])


def among_columns(x):
    slabs, tiles = lax.axis_size("slab"), lax.axis_size("tile")
    half = tiles // 2
    planes = [slab * tiles + far * half for slab in range(slabs) for far in range(2)]
    groups = [[plane + i for i in range(core, half, 2)] for plane in planes for core in range(2)]
    return lax.all_to_all(x, ("slab", "tile"), 0, 0, tiled=True, axis_index_groups=groups)


def swap_far(x):
    slabs, tiles = lax.axis_size("slab"), lax.axis_size("tile")
    half = tiles // 2
    pairs = [
        (slab * tiles + tile, (slabs - 1 - slab) * tiles + (tile + half) % tiles)
        for slab in range(slabs)
        for tile in range(tiles)
    ]
    return lax.ppermute(x, ("slab", "tile"), pairs)


def swap_slab(x):
    return lax.ppermute(x, "slab", [(0, 1), (1, 0)])


def shards(transmission, probe, scan_offsets, amplitudes):
    tables = jnp.asarray(make_tables())
    index = lax.axis_index("slab").astype(jnp.int32)
    where = (index.reshape(1), scan_offsets)
    info = jnp.where(index == 0, scan_offsets, scan_offsets[::-1]).reshape(4, 1)
    info = jnp.broadcast_to(jnp.concatenate([info, info]), (8, HALF))
    own = transmission
    part, whole, band = (2, 2, HALO, WIDTH), (2, 2, WIDTH, WIDTH), (2, 2, HALO, COLS)

    own_hbm, offsets_hbm = (pltpu.with_memory_space_constraint(x, pltpu.HBM) for x in (own, scan_offsets))
    core = call(
        core_kernel,
        part,
        (),
        (offsets_hbm, own_hbm),
        "core",
        scratch=[
            pltpu.SMEM((2, 2), jnp.int32),
            pltpu.VMEM((4, HALO, HALF), F32),
            pltpu.VMEM((4, HALO, HALF), F32),
            pltpu.SemaphoreType.DMA((3, 5)),
        ],
        ins=(HBM, HBM),
    )
    core = swap_slab(core)
    beside, across = swap_tile(own, 1), swap_tile(own, 0)
    rolled = call(roll_probe_kernel, (2, WIDTH, WIDTH), where, (probe,), "roll")
    amp = call(amp_kernel, (WIDTH, WIDTH), where, (amplitudes,), "amp")
    halo, second_halo = call(halo_kernel, (part[1:],) * 2, (), (info, across, beside), "halo")
    halo, second_halo = swap_slab(halo), swap_slab(second_halo)
    windows = call(window_kernel, whole, (), (info, own, across, beside), "window")

    wave, window = call(
        first_kernel,
        (probe.shape, probe.shape),
        (),
        (info, tables, rolled, windows, core, halo),
        "first",
    )
    tiles = (WIDTH // 8, 2, 8, HALF)
    keep, send, cores, beside, early, late = call(
        position_kernel,
        (tiles, tiles, (4, 2, HALO, WIDTH), (8 * HALO + 8, WIDTH), (4 * HALO + 8, WIDTH), (4 * HALO, WIDTH)),
        (),
        (info, scan_offsets, tables, rolled, amp, windows, core, halo, second_halo, wave, window),
        "position",
        scratch=[
            pltpu.VMEM((2, 2, WIDTH, WIDTH), F32),
            pltpu.VMEM((3, 2, WIDTH, WIDTH), F32),
            pltpu.VMEM((5, 2 * HALO, WIDTH), F32),
            pltpu.SMEM((2, 2), jnp.int32),
            pltpu.SemaphoreType.DMA((2, 6)),
        ],
        ins=(VMEM, HBM) + (VMEM,) * 9,
        flops=3_300_000_000,
        nbytes=10_000_000,
        outs=(VMEM, VMEM, VMEM, HBM, HBM, HBM),
    )
    sides = (info, cores, swap_tile(early, 0), swap_tile(beside, 1))
    parts = (WIDTH // 16, 4, 8, HALF)
    kept = call(add_kernel, tiles, (), (keep, swap_core(send)), "add").reshape(parts)
    kept = call(reduce_kernel, parts[1:], (), (among_columns(kept),), "reduce")
    late, kept = lax.optimization_barrier((late, kept))
    late = swap_tile(late, 0)
    kept = call(add_kernel, parts[1:], (), (kept, swap_slab(kept)), "add_slabs")
    got = swap_slab(call(sum_kernel, band, (), sides + (kept,), "sum"))
    kept = call(total_kernel, parts, (), (kept, swap_far(kept)), "total")
    kept = among_columns(kept)
    other = swap_core(kept)
    object_grad, token = call(object_kernel, (band, (8, HALF)), (), sides + (late, got, kept), "object")
    probe_grad = call(
        probe_kernel,
        probe.shape,
        (),
        (token, kept.reshape(tiles), other.reshape(tiles)),
        "probe",
    )
    return object_grad, probe_grad


def solution(mesh):
    placed = (P("slab", None, "tile", None), P(), P("tile", None), P("tile", None, None))
    return jax.shard_map(
        shards,
        mesh=mesh,
        in_specs=placed,
        out_specs=(P("slab", None, "tile", None), P()),
        check_vma=False,
    )
```

```python
import functools

import jax
import jax.numpy as jnp
import numpy as np
from jax import lax
from jax.experimental import pallas as pl
from jax.experimental.pallas import tpu as pltpu
from jax.sharding import PartitionSpec as P

WIDTH = 256
HALF = 128
HALO = 128
COLS = 384
PROP_STRENGTH = 12.0
BF16 = jnp.bfloat16
F32 = jnp.float32
VMEM = pl.BlockSpec(memory_space=pltpu.VMEM)
SMEM = pl.BlockSpec(memory_space=pltpu.SMEM)
HBM = pl.BlockSpec(memory_space=pltpu.HBM)


def high_low(table):
    table = table.astype(np.float32)
    high = table.astype(jnp.bfloat16)
    low = (table - high.astype(np.float32)).astype(jnp.bfloat16)
    return np.stack([high, low])


def on_right(m):
    return high_low(np.block([[m.real, m.imag], [-m.imag, m.real]]))


def on_left(m):
    return high_low(np.block([[m.real, -m.imag], [m.imag, m.real]]))


def make_tables():
    index = np.arange(WIDTH)
    dft = np.exp(-2j * np.pi / WIDTH * (index[:, None] * index[None, :] % WIDTH)) / np.sqrt(WIDTH)
    freq = ((index + WIDTH // 2) % WIDTH - WIDTH // 2) / WIDTH
    phase = np.exp(-1j * PROP_STRENGTH * freq**2)
    prop = dft.conj() @ (phase[:, None] * dft)
    far = phase[:, None] * dft
    p, q = prop[:HALF, :HALF], prop[:HALF, HALF:]
    props = ((p + q) / 2, (p - q) / 2)
    fars = (far[0::2, :HALF], far[1::2, :HALF])
    return np.stack(
        [
            np.stack([on_right(m) for m in props]),
            np.stack([on_left(m) for m in props]),
            np.stack([on_right(m.T) for m in fars]),
            np.stack([on_left(m) for m in fars]),
            np.stack([on_right(m) for m in fars]),
            np.stack([on_left(m.T) for m in fars]),
        ]
    )


PROP_RIGHT, PROP_LEFT, FAR_RIGHT, FAR_LEFT, BACK_RIGHT, BACK_LEFT = range(6)


def split(x):
    high = x.astype(BF16)
    low = (x - high.astype(F32)).astype(BF16)
    return high, low


def dot(a, b):
    return jnp.dot(a, b, preferred_element_type=F32)


def fold(x):
    x = jnp.concatenate([x[:HALF] + x[HALF:], x[:HALF] - x[HALF:]], axis=0)
    return jnp.concatenate([x[:, :HALF] + x[:, HALF:], x[:, :HALF] - x[:, HALF:]], axis=1)


def fold_columns(x):
    return jnp.concatenate([x[:, :HALF] + x[:, HALF:], x[:, :HALF] - x[:, HALF:]], axis=1)


def right_mult(x, tables, which):
    re, im = [], []
    for h in range(2):
        part = slice(h * HALF, (h + 1) * HALF)
        high, low = split(jnp.concatenate([x[0][:, part], x[1][:, part]], axis=1))
        th, tl = tables[which, h, 0], tables[which, h, 1]
        out = dot(jnp.concatenate([high, low, high], axis=1), jnp.concatenate([th, th, tl], axis=0))
        re.append(out[:, :HALF])
        im.append(out[:, HALF:])
    return jnp.concatenate(re, axis=1), jnp.concatenate(im, axis=1)


def left_mult(x, tables, which):
    re, im = [], []
    for h in range(2):
        part = slice(h * HALF, (h + 1) * HALF)
        high, low = split(jnp.concatenate([x[0][part], x[1][part]], axis=0))
        th, tl = tables[which, h, 0], tables[which, h, 1]
        out = dot(jnp.concatenate([th, th, tl], axis=1), jnp.concatenate([high, low, high], axis=0))
        re.append(out[:HALF])
        im.append(out[HALF:])
    return jnp.concatenate(re, axis=0), jnp.concatenate(im, axis=0)


def propagate(x, tables):
    y = right_mult((fold(x[0]), fold(x[1])), tables, PROP_RIGHT)
    y = left_mult(y, tables, PROP_LEFT)
    return fold(y[0]), fold(y[1])


def times(a, b):
    return a[0] * b[0] - a[1] * b[1], a[0] * b[1] + a[1] * b[0]


def here():
    half = lax.axis_size("tile") // 2
    within = lax.axis_index("tile") % half
    turned = jnp.where((within == 0) | (within == half - 1), 1, 0)
    return lax.axis_index("slab"), within % 2, turned


def masks(info_ref, which):
    row = jnp.broadcast_to(info_ref[2 * which : 2 * which + 1], (HALO, HALF))
    col = jnp.broadcast_to(info_ref[2 * which + 1 : 2 * which + 2], (HALO, HALF))
    line = lax.broadcasted_iota(jnp.int32, (HALO, HALF), 0)
    lane = lax.broadcasted_iota(jnp.int32, (HALO, HALF), 1)
    return jnp.where(line >= row, 1, 0) == here()[1], lane >= col


def columns_of(x, kept):
    return jnp.where(kept, x(0), x(2)), x(1)


def halo_of(across_ref, beside_ref, at, from_beside, kept):
    def column(i):
        cols = slice(i * HALF, (i + 1) * HALF)
        return jnp.where(from_beside, beside_ref[at + (slice(None), cols)], across_ref[at + (slice(None), cols)])

    return columns_of(column, kept)


def roll_probe_kernel(place_ref, offsets_ref, probe_ref, out_ref):
    row, col = offsets_ref[place_ref[0], 0], offsets_ref[place_ref[0], 1]
    for c in range(2):
        out_ref[c] = pltpu.roll(pltpu.roll(probe_ref[c], row, 0), col, 1)


def core_kernel(offsets_ref, own_ref, out_ref, offsets, left, right, sems):
    load = pltpu.make_async_copy(offsets_ref, offsets, sems.at[0, 4])
    load.start()
    loads = []
    for i in range(4):
        at = (i // 2, i % 2, slice(None))
        loads.append(
            [
                pltpu.make_async_copy(own_ref.at[at + (slice(0, HALF),)], left.at[i], sems.at[0, i]),
                pltpu.make_async_copy(own_ref.at[at + (slice(WIDTH, COLS),)], right.at[i], sems.at[1, i]),
                pltpu.make_async_copy(
                    own_ref.at[at + (slice(HALF, WIDTH),)], out_ref.at[at + (slice(HALF, WIDTH),)], sems.at[2, i]
                ),
            ]
        )
        for copy in loads[i]:
            copy.start()
    load.wait()
    lane = lax.broadcasted_iota(jnp.int32, (HALO, HALF), 1)
    kept = lane >= offsets[1 - lax.axis_index("slab"), 1]
    for i in range(4):
        loads[i][0].wait()
        loads[i][1].wait()
        out_ref[i // 2, i % 2, :, :HALF] = jnp.where(kept, left[i], right[i])
    for i in range(4):
        loads[i][2].wait()


def amp_kernel(place_ref, offsets_ref, amp_ref, out_ref):
    x = amp_ref[place_ref[0]]
    line = lax.broadcasted_iota(jnp.int32, (WIDTH, WIDTH), 0)
    lane = lax.broadcasted_iota(jnp.int32, (WIDTH, WIDTH), 1)
    rows = jnp.where(lane == 2 * (line % HALF) + line // HALF, 1.0, 0.0).astype(BF16)
    cols = jnp.where(line == 2 * (lane % HALF) + lane // HALF, 1.0, 0.0).astype(BF16)

    def parts(value):
        high, rest = split(value)
        return high, rest, (value - high.astype(F32) - rest.astype(F32)).astype(BF16)

    x = sum(dot(rows, part) for part in parts(x))
    out_ref[...] = sum(dot(part, cols) for part in parts(x))


def halo_kernel(info_ref, across_ref, beside_ref, first_out, second_out):
    from_beside, kept = masks(info_ref, 1)
    for j, out_ref in enumerate((first_out, second_out)):
        for c in range(2):
            left, right = halo_of(across_ref, beside_ref, (j, c), from_beside, kept)
            out_ref[c, :, :HALF] = left
            out_ref[c, :, HALF:] = right


def window_kernel(info_ref, own_ref, across_ref, beside_ref, out_ref):
    from_beside, kept = masks(info_ref, 0)
    for j in range(2):
        for c in range(2):
            left, right = halo_of(across_ref, beside_ref, (j, c), from_beside, kept)
            out_ref[j, c, :HALO, :HALF] = left
            out_ref[j, c, :HALO, HALF:] = right
            left, right = columns_of(lambda i: own_ref[j, c, :, i * HALF : (i + 1) * HALF], kept)
            out_ref[j, c, HALO:, :HALF] = left
            out_ref[j, c, HALO:, HALF:] = right


def selector(info_ref, own_ref, core_ref, halo_refs):
    place, odd, turned = here()
    from_beside = masks(info_ref, 0)[0]
    turned = jnp.where(jnp.concatenate([from_beside, from_beside], axis=1), 0, turned)

    def window_of(s):
        mine = jnp.where(place == s // 2, 1, 0)
        out = []
        for c in range(2):
            halo = jnp.where(turned == mine, halo_refs[s % 2][c], own_ref[s % 2, c, :HALO])
            core = jnp.where(mine == 1, own_ref[s % 2, c, HALO:], core_ref[s % 2, c])
            out.append(jnp.concatenate([halo, core], axis=0))
        return out

    return window_of


def first_kernel(info_ref, tables_ref, probe_ref, own_ref, core_ref, halo_ref, wave_out, window_out, lower_out):
    window = selector(info_ref, own_ref, core_ref, (halo_ref, None))(0)
    window_out[0], window_out[1] = window
    wave = propagate(times((probe_ref[0], probe_ref[1]), window), tables_ref)
    wave_out[0], wave_out[1] = wave
    mine = here()[0] == 0
    core = [jnp.where(mine, own_ref[1, c, HALO:], core_ref[1, c]) for c in range(2)]
    lower = times((wave[0][HALO:], wave[1][HALO:]), core)
    lower = right_mult((fold_columns(lower[0]), fold_columns(lower[1])), tables_ref, PROP_RIGHT)
    lower_out[0], lower_out[1] = lower


def position_kernel(
    info_ref,
    offsets_ref,
    tables_ref,
    probe_ref,
    amp_ref,
    own_ref,
    core_ref,
    halo_ref,
    second_halo_ref,
    first_wave_ref,
    first_window_ref,
    lower_ref,
    keep_out,
    send_out,
    core_out,
    beside_out,
    early_out,
    late_out,
    waves,
    windows,
    offsets,
    sems,
):
    place, odd, across_turned = here()
    load = pltpu.make_async_copy(offsets_ref, offsets, sems.at[0, 5])
    load.start()
    window_of = selector(info_ref, own_ref, core_ref, (halo_ref, second_halo_ref))
    wave = (first_wave_ref[0], first_wave_ref[1])
    for s in range(1, 4):
        if s > 1:
            waves[s - 2, 0], waves[s - 2, 1] = wave
        window = window_of(s)
        windows[s - 1, 0], windows[s - 1, 1] = window
        if s == 1:
            upper = times((wave[0][:HALO], wave[1][:HALO]), (window[0][:HALO], window[1][:HALO]))
            upper = right_mult((fold_columns(upper[0]), fold_columns(upper[1])), tables_ref, PROP_RIGHT)
            rows = [
                jnp.concatenate([upper[c] + lower_ref[c], upper[c] - lower_ref[c]], axis=0) for c in range(2)
            ]
            rows = left_mult(rows, tables_ref, PROP_LEFT)
            wave = (fold(rows[0]), fold(rows[1]))
            continue
        prod = times(wave, window)
        if s < 3:
            wave = propagate(prod, tables_ref)

    def before(s):
        ref = (probe_ref, first_wave_ref, waves.at[0], waves.at[1])[s]
        return ref[0], ref[1]

    def window_at(s):
        ref = first_window_ref if s == 0 else windows.at[s - 1]
        return ref[0], ref[1]

    field = right_mult((fold(prod[0]), fold(prod[1])), tables_ref, FAR_RIGHT)
    field = left_mult(field, tables_ref, FAR_LEFT)
    model = jnp.sqrt(field[0] * field[0] + field[1] * field[1] + 1.0)
    ratio = (model - amp_ref[...]) / model
    grad = (field[0] * ratio, -(field[1] * ratio))
    grad = right_mult(grad, tables_ref, BACK_RIGHT)
    grad = left_mult(grad, tables_ref, BACK_LEFT)
    grad = (fold(grad[0]), fold(grad[1]))
    copies = []
    for s in range(3, -1, -1):
        object_grad = times(before(s), grad)
        slot = jnp.where(place == s // 2, s % 2, 2 + s % 2)
        start = pl.multiple_of(slot * 2 * HALO, HALO)
        for c in range(2):
            value = object_grad[c] if c == 0 else -object_grad[c]
            core_out[slot, c] = value[HALO:]
            beside_out[pl.ds(start + c * HALO, HALO)] = value[:HALO]
        source = beside_out.at[pl.ds(start, 2 * HALO)]
        target = pl.multiple_of(s % 2 * 2 * HALO, HALO)
        early = jnp.where(slot // 2 == 1, 1, 0) != across_turned
        for which, ref in enumerate((late_out, early_out)):
            copy = pltpu.make_async_copy(source, ref.at[pl.ds(target, 2 * HALO)], sems.at[1, s])

            @pl.when(early == (which == 1))
            def _():
                copy.start()

        copies.append(copy)
        grad = times(window_at(s), grad)
        if s > 0:
            grad = propagate(grad, tables_ref)
    meta = info_ref[...].astype(F32)
    beside_out[8 * HALO :] = jnp.concatenate([meta, meta], axis=1)
    copy = pltpu.make_async_copy(beside_out.at[pl.ds(8 * HALO, 8)], early_out.at[pl.ds(4 * HALO, 8)], sems.at[1, 4])
    copy.start()
    copies.append(copy)
    load.wait()
    row, col = offsets[place, 0], offsets[place, 1]
    value = [grad[0], -grad[1]]
    for c in range(2):
        value[c] = pltpu.roll(value[c], lax.rem(WIDTH - row, WIDTH), 0)
        value[c] = pltpu.roll(value[c], lax.rem(WIDTH - col, WIDTH), 1)
    for ref, which in ((keep_out, odd), (send_out, 1 - odd)):
        part = jnp.where(which == 0, value[0], value[1])
        for h in range(2):
            ref[:, h] = part[:, h * HALF : (h + 1) * HALF].reshape(WIDTH // 8, 8, HALF)
    for copy in copies:
        copy.wait()


def widen(x, kept):
    left, right = x[..., :HALF], x[..., HALF:]
    return jnp.concatenate([jnp.where(kept, left, 0.0), right, jnp.where(kept, 0.0, left)], axis=-1)


def add_halos(info_ref, core_ref, across_ref, early_ref, beside_ref, out_ref, first, extra=None):
    odd = here()[1]
    own_kept = masks(info_ref, 0)[1]
    line = lax.broadcasted_iota(jnp.int32, (HALO, WIDTH), 0).astype(F32)
    column = lax.broadcasted_iota(jnp.int32, (HALO, HALF), 1).astype(F32)
    sides = []
    for ref, base, meta, after in (
        (across_ref, 0, early_ref[4 * HALO :], odd),
        (beside_ref, first * 2 * HALO, beside_ref[8 * HALO :], 1 - odd),
    ):
        kept = column >= meta[1:2, :HALF]
        mask = jnp.where(line >= meta[0:1], 1, 0) == after
        sides.append((ref, base, mask, kept))
    for j in range(2):
        for c in range(2):
            total = widen(core_ref[first + j, c], own_kept)
            for ref, base, mask, kept in sides:
                start = base + (j * 2 + c) * HALO
                total = total + widen(jnp.where(mask, ref[start : start + HALO], 0.0), kept)
            out_ref[j, c] = total if extra is None else total + extra[j, c]


def add_kernel(keep_ref, got_ref, out_ref):
    out_ref[...] = keep_ref[...] + got_ref[...]


def reduce_kernel(parts_ref, out_ref):
    out_ref[...] = jnp.sum(parts_ref[...], axis=0)


def total_kernel(first_ref, second_ref, out_ref):
    total = first_ref[...] + second_ref[...]
    out_ref[...] = jnp.broadcast_to(total[None], out_ref.shape)


def sum_kernel(info_ref, core_ref, early_ref, beside_ref, after_ref, out_ref):
    add_halos(info_ref, core_ref, early_ref, early_ref, beside_ref, out_ref, 2)


def object_kernel(info_ref, core_ref, early_ref, beside_ref, late_ref, swapped_ref, after_ref, out_ref, token_ref):
    token_ref[...] = jnp.zeros(token_ref.shape, F32)
    add_halos(info_ref, core_ref, late_ref, early_ref, beside_ref, out_ref, 0, swapped_ref)


def probe_kernel(after_ref, keep_ref, got_ref, out_ref):
    odd = here()[1]
    for ref, which in ((keep_ref, odd), (got_ref, 1 - odd)):
        for h in range(2):
            out_ref[which, :, h * HALF : (h + 1) * HALF] = ref[:, h].reshape(WIDTH, HALF)


def call(kernel, shapes, smem, vmem, name, scratch=(), flops=0, nbytes=2_000_000, ins=None, outs=None, vmem_limit=40):
    single = isinstance(shapes[0], int)
    shapes = (shapes,) if single else shapes
    out = pl.pallas_call(
        kernel,
        out_shape=tuple(jax.ShapeDtypeStruct(shape, F32) for shape in shapes),
        in_specs=[SMEM] * len(smem) + list(ins or [VMEM] * len(vmem)),
        out_specs=outs or (VMEM,) * len(shapes),
        scratch_shapes=scratch,
        compiler_params=pltpu.CompilerParams(vmem_limit_bytes=vmem_limit * 1024 * 1024),
        cost_estimate=pl.CostEstimate(flops=flops, bytes_accessed=nbytes, transcendentals=0),
        name=name,
    )(*smem, *vmem)
    return out[0] if single else out


def swap_tile(x, beside):
    slabs, tiles = lax.axis_size("slab"), lax.axis_size("tile")
    pairs = []
    for slab in range(slabs):
        for tile in range(tiles):
            to = (tile + (1 if tile % 2 != beside else -1)) % tiles
            turned = tile // (tiles // 2) != to // (tiles // 2)
            pairs.append((slab * tiles + tile, (slab ^ turned) * tiles + to))
    return lax.ppermute(x, ("slab", "tile"), pairs)


def swap_core(x):
    count = lax.axis_size("tile")
    return lax.ppermute(x, "tile", [(i, i ^ 1) for i in range(count)])


def among_columns(x):
    slabs, tiles = lax.axis_size("slab"), lax.axis_size("tile")
    half = tiles // 2
    planes = [slab * tiles + far * half for slab in range(slabs) for far in range(2)]
    groups = [[plane + i for i in range(core, half, 2)] for plane in planes for core in range(2)]
    return lax.all_to_all(x, ("slab", "tile"), 0, 0, tiled=True, axis_index_groups=groups)


def swap_far(x):
    slabs, tiles = lax.axis_size("slab"), lax.axis_size("tile")
    half = tiles // 2
    pairs = [
        (slab * tiles + tile, (slabs - 1 - slab) * tiles + (tile + half) % tiles)
        for slab in range(slabs)
        for tile in range(tiles)
    ]
    return lax.ppermute(x, ("slab", "tile"), pairs)


def swap_slab(x):
    return lax.ppermute(x, "slab", [(0, 1), (1, 0)])


def shards(transmission, probe, scan_offsets, amplitudes):
    tables = jnp.asarray(make_tables())
    index = lax.axis_index("slab").astype(jnp.int32)
    where = (index.reshape(1), scan_offsets)
    info = jnp.where(index == 0, scan_offsets, scan_offsets[::-1]).reshape(4, 1)
    info = jnp.broadcast_to(jnp.concatenate([info, info]), (8, HALF))
    own = transmission
    part, whole, band = (2, 2, HALO, WIDTH), (2, 2, WIDTH, WIDTH), (2, 2, HALO, COLS)

    own_hbm, offsets_hbm = (pltpu.with_memory_space_constraint(x, pltpu.HBM) for x in (own, scan_offsets))
    core = call(
        core_kernel,
        part,
        (),
        (offsets_hbm, own_hbm),
        "core",
        scratch=[
            pltpu.SMEM((2, 2), jnp.int32),
            pltpu.VMEM((4, HALO, HALF), F32),
            pltpu.VMEM((4, HALO, HALF), F32),
            pltpu.SemaphoreType.DMA((3, 5)),
        ],
        ins=(HBM, HBM),
    )
    core = swap_slab(core)
    beside, across = swap_tile(own, 1), swap_tile(own, 0)
    rolled = call(roll_probe_kernel, (2, WIDTH, WIDTH), where, (probe,), "roll")
    amp = call(amp_kernel, (WIDTH, WIDTH), where, (amplitudes,), "amp")
    halo, second_halo = call(halo_kernel, (part[1:],) * 2, (), (info, across, beside), "halo")
    halo, second_halo = swap_slab(halo), swap_slab(second_halo)
    windows = call(window_kernel, whole, (), (info, own, across, beside), "window")

    wave, window, lower = call(
        first_kernel,
        (probe.shape, probe.shape, part[1:]),
        (),
        (info, tables, rolled, windows, core, halo),
        "first",
    )
    tiles = (WIDTH // 8, 2, 8, HALF)
    keep, send, cores, beside, early, late = call(
        position_kernel,
        (tiles, tiles, (4, 2, HALO, WIDTH), (8 * HALO + 8, WIDTH), (4 * HALO + 8, WIDTH), (4 * HALO, WIDTH)),
        (),
        (info, scan_offsets, tables, rolled, amp, windows, core, halo, second_halo, wave, window, lower),
        "position",
        scratch=[
            pltpu.VMEM((2, 2, WIDTH, WIDTH), F32),
            pltpu.VMEM((3, 2, WIDTH, WIDTH), F32),
            pltpu.SMEM((2, 2), jnp.int32),
            pltpu.SemaphoreType.DMA((2, 6)),
        ],
        ins=(VMEM, HBM) + (VMEM,) * 10,
        flops=3_300_000_000,
        nbytes=10_000_000,
        outs=(VMEM, VMEM, VMEM, VMEM, HBM, HBM),
    )
    sides = (info, cores, swap_tile(early, 0), swap_tile(beside, 1))
    parts = (WIDTH // 16, 4, 8, HALF)
    kept = call(add_kernel, tiles, (), (keep, swap_core(send)), "add").reshape(parts)
    kept = call(reduce_kernel, parts[1:], (), (among_columns(kept),), "reduce")
    late, kept = lax.optimization_barrier((late, kept))
    late = swap_tile(late, 0)
    kept = call(add_kernel, parts[1:], (), (kept, swap_slab(kept)), "add_slabs")
    got = swap_slab(call(sum_kernel, band, (), sides + (kept,), "sum"))
    kept = call(total_kernel, parts, (), (kept, swap_far(kept)), "total")
    kept = among_columns(kept)
    other = swap_core(kept)
    object_grad, token = call(object_kernel, (band, (8, HALF)), (), sides + (late, got, kept), "object")
    probe_grad = call(
        probe_kernel,
        probe.shape,
        (),
        (token, kept.reshape(tiles), other.reshape(tiles)),
        "probe",
    )
    return object_grad, probe_grad


def solution(mesh):
    placed = (P("slab", None, "tile", None), P(), P("tile", None), P("tile", None, None))
    return jax.shard_map(
        shards,
        mesh=mesh,
        in_specs=placed,
        out_specs=(P("slab", None, "tile", None), P()),
        check_vma=False,
    )
```

```python
import functools

import jax
import jax.numpy as jnp
import numpy as np
from jax import lax
from jax.experimental import pallas as pl
from jax.experimental.pallas import tpu as pltpu
from jax.sharding import PartitionSpec as P

WIDTH = 256
HALF = 128
HALO = 128
COLS = 384
PROP_STRENGTH = 12.0
BF16 = jnp.bfloat16
F32 = jnp.float32
VMEM = pl.BlockSpec(memory_space=pltpu.VMEM)
SMEM = pl.BlockSpec(memory_space=pltpu.SMEM)
HBM = pl.BlockSpec(memory_space=pltpu.HBM)


def high_low(table):
    table = table.astype(np.float32)
    high = table.astype(jnp.bfloat16)
    low = (table - high.astype(np.float32)).astype(jnp.bfloat16)
    return np.stack([high, low])


def on_right(m):
    return high_low(np.block([[m.real, m.imag], [-m.imag, m.real]]))


def on_left(m):
    return high_low(np.block([[m.real, -m.imag], [m.imag, m.real]]))


def make_tables():
    index = np.arange(WIDTH)
    dft = np.exp(-2j * np.pi / WIDTH * (index[:, None] * index[None, :] % WIDTH)) / np.sqrt(WIDTH)
    freq = ((index + WIDTH // 2) % WIDTH - WIDTH // 2) / WIDTH
    phase = np.exp(-1j * PROP_STRENGTH * freq**2)
    prop = dft.conj() @ (phase[:, None] * dft)
    far = phase[:, None] * dft
    p, q = prop[:HALF, :HALF], prop[:HALF, HALF:]
    props = ((p + q) / 2, (p - q) / 2)
    fars = (far[0::2, :HALF], far[1::2, :HALF])
    return np.stack(
        [
            np.stack([on_right(m) for m in props]),
            np.stack([on_left(m) for m in props]),
            np.stack([on_right(m.T) for m in fars]),
            np.stack([on_left(m) for m in fars]),
            np.stack([on_right(m) for m in fars]),
            np.stack([on_left(m.T) for m in fars]),
        ]
    )


PROP_RIGHT, PROP_LEFT, FAR_RIGHT, FAR_LEFT, BACK_RIGHT, BACK_LEFT = range(6)


def split(x):
    high = x.astype(BF16)
    low = (x - high.astype(F32)).astype(BF16)
    return high, low


def dot(a, b):
    return jnp.dot(a, b, preferred_element_type=F32)


def fold(x):
    x = jnp.concatenate([x[:HALF] + x[HALF:], x[:HALF] - x[HALF:]], axis=0)
    return jnp.concatenate([x[:, :HALF] + x[:, HALF:], x[:, :HALF] - x[:, HALF:]], axis=1)


def fold_columns(x):
    return jnp.concatenate([x[:, :HALF] + x[:, HALF:], x[:, :HALF] - x[:, HALF:]], axis=1)


def right_mult(x, tables, which):
    re, im = [], []
    for h in range(2):
        part = slice(h * HALF, (h + 1) * HALF)
        high, low = split(jnp.concatenate([x[0][:, part], x[1][:, part]], axis=1))
        th, tl = tables[which, h, 0], tables[which, h, 1]
        out = dot(jnp.concatenate([high, low, high], axis=1), jnp.concatenate([th, th, tl], axis=0))
        re.append(out[:, :HALF])
        im.append(out[:, HALF:])
    return jnp.concatenate(re, axis=1), jnp.concatenate(im, axis=1)


def left_mult(x, tables, which):
    re, im = [], []
    for h in range(2):
        part = slice(h * HALF, (h + 1) * HALF)
        high, low = split(jnp.concatenate([x[0][part], x[1][part]], axis=0))
        th, tl = tables[which, h, 0], tables[which, h, 1]
        out = dot(jnp.concatenate([th, th, tl], axis=1), jnp.concatenate([high, low, high], axis=0))
        re.append(out[:HALF])
        im.append(out[HALF:])
    return jnp.concatenate(re, axis=0), jnp.concatenate(im, axis=0)


def propagate(x, tables):
    y = right_mult((fold(x[0]), fold(x[1])), tables, PROP_RIGHT)
    y = left_mult(y, tables, PROP_LEFT)
    return fold(y[0]), fold(y[1])


def times(a, b):
    return a[0] * b[0] - a[1] * b[1], a[0] * b[1] + a[1] * b[0]


def here():
    half = lax.axis_size("tile") // 2
    within = lax.axis_index("tile") % half
    turned = jnp.where((within == 0) | (within == half - 1), 1, 0)
    return lax.axis_index("slab"), within % 2, turned


def masks(info_ref, which):
    row = jnp.broadcast_to(info_ref[2 * which : 2 * which + 1], (HALO, HALF))
    col = jnp.broadcast_to(info_ref[2 * which + 1 : 2 * which + 2], (HALO, HALF))
    line = lax.broadcasted_iota(jnp.int32, (HALO, HALF), 0)
    lane = lax.broadcasted_iota(jnp.int32, (HALO, HALF), 1)
    return jnp.where(line >= row, 1, 0) == here()[1], lane >= col


def columns_of(x, kept):
    return jnp.where(kept, x(0), x(2)), x(1)


def halo_of(across_ref, beside_ref, at, from_beside, kept):
    def column(i):
        cols = slice(i * HALF, (i + 1) * HALF)
        return jnp.where(from_beside, beside_ref[at + (slice(None), cols)], across_ref[at + (slice(None), cols)])

    return columns_of(column, kept)


def roll_probe_kernel(place_ref, offsets_ref, probe_ref, out_ref):
    row, col = offsets_ref[place_ref[0], 0], offsets_ref[place_ref[0], 1]
    for c in range(2):
        out_ref[c] = pltpu.roll(pltpu.roll(probe_ref[c], row, 0), col, 1)


def core_kernel(offsets_ref, own_ref, out_ref, offsets, left, right, sems):
    load = pltpu.make_async_copy(offsets_ref, offsets, sems.at[0, 4])
    load.start()
    loads = []
    for i in range(4):
        at = (i // 2, i % 2, slice(None))
        loads.append(
            [
                pltpu.make_async_copy(own_ref.at[at + (slice(0, HALF),)], left.at[i], sems.at[0, i]),
                pltpu.make_async_copy(own_ref.at[at + (slice(WIDTH, COLS),)], right.at[i], sems.at[1, i]),
                pltpu.make_async_copy(
                    own_ref.at[at + (slice(HALF, WIDTH),)], out_ref.at[at + (slice(HALF, WIDTH),)], sems.at[2, i]
                ),
            ]
        )
        for copy in loads[i]:
            copy.start()
    load.wait()
    lane = lax.broadcasted_iota(jnp.int32, (HALO, HALF), 1)
    kept = lane >= offsets[1 - lax.axis_index("slab"), 1]
    for i in range(4):
        loads[i][0].wait()
        loads[i][1].wait()
        out_ref[i // 2, i % 2, :, :HALF] = jnp.where(kept, left[i], right[i])
    for i in range(4):
        loads[i][2].wait()


def amp_kernel(place_ref, offsets_ref, amp_ref, out_ref):
    x = amp_ref[place_ref[0]]
    line = lax.broadcasted_iota(jnp.int32, (WIDTH, WIDTH), 0)
    lane = lax.broadcasted_iota(jnp.int32, (WIDTH, WIDTH), 1)
    rows = jnp.where(lane == 2 * (line % HALF) + line // HALF, 1.0, 0.0).astype(BF16)
    cols = jnp.where(line == 2 * (lane % HALF) + lane // HALF, 1.0, 0.0).astype(BF16)

    def parts(value):
        high, rest = split(value)
        return high, rest, (value - high.astype(F32) - rest.astype(F32)).astype(BF16)

    x = sum(dot(rows, part) for part in parts(x))
    out_ref[...] = sum(dot(part, cols) for part in parts(x))


def halo_kernel(info_ref, across_ref, beside_ref, first_out, second_out):
    from_beside, kept = masks(info_ref, 1)
    for j, out_ref in enumerate((first_out, second_out)):
        for c in range(2):
            left, right = halo_of(across_ref, beside_ref, (j, c), from_beside, kept)
            out_ref[c, :, :HALF] = left
            out_ref[c, :, HALF:] = right


def window_kernel(info_ref, own_ref, across_ref, beside_ref, out_ref):
    from_beside, kept = masks(info_ref, 0)
    for j in range(2):
        for c in range(2):
            left, right = halo_of(across_ref, beside_ref, (j, c), from_beside, kept)
            out_ref[j, c, :HALO, :HALF] = left
            out_ref[j, c, :HALO, HALF:] = right
            left, right = columns_of(lambda i: own_ref[j, c, :, i * HALF : (i + 1) * HALF], kept)
            out_ref[j, c, HALO:, :HALF] = left
            out_ref[j, c, HALO:, HALF:] = right


def selector(info_ref, own_ref, core_ref, halo_refs):
    place, odd, turned = here()
    from_beside = masks(info_ref, 0)[0]
    turned = jnp.where(jnp.concatenate([from_beside, from_beside], axis=1), 0, turned)

    def window_of(s):
        mine = jnp.where(place == s // 2, 1, 0)
        out = []
        for c in range(2):
            halo = jnp.where(turned == mine, halo_refs[s % 2][c], own_ref[s % 2, c, :HALO])
            core = jnp.where(mine == 1, own_ref[s % 2, c, HALO:], core_ref[s % 2, c])
            out.append(jnp.concatenate([halo, core], axis=0))
        return out

    return window_of


def first_kernel(info_ref, tables_ref, probe_ref, own_ref, core_ref, halo_ref, wave_out, window_out, lower_out):
    window = selector(info_ref, own_ref, core_ref, (halo_ref, None))(0)
    window_out[0], window_out[1] = window
    wave = propagate(times((probe_ref[0], probe_ref[1]), window), tables_ref)
    wave_out[0], wave_out[1] = wave
    mine = here()[0] == 0
    core = [jnp.where(mine, own_ref[1, c, HALO:], core_ref[1, c]) for c in range(2)]
    lower = times((wave[0][HALO:], wave[1][HALO:]), core)
    lower = right_mult((fold_columns(lower[0]), fold_columns(lower[1])), tables_ref, PROP_RIGHT)
    lower_out[0], lower_out[1] = lower


def position_kernel(
    info_ref,
    offsets_ref,
    tables_ref,
    probe_ref,
    amp_ref,
    own_ref,
    core_ref,
    halo_ref,
    second_halo_ref,
    first_wave_ref,
    first_window_ref,
    lower_ref,
    keep_out,
    send_out,
    core_out,
    beside_out,
    early_out,
    late_out,
    waves,
    windows,
    offsets,
    sems,
):
    place, odd, across_turned = here()
    load = pltpu.make_async_copy(offsets_ref, offsets, sems.at[0, 5])
    load.start()
    window_of = selector(info_ref, own_ref, core_ref, (halo_ref, second_halo_ref))
    wave = (first_wave_ref[0], first_wave_ref[1])
    for s in range(1, 4):
        if s > 1:
            waves[s - 2, 0], waves[s - 2, 1] = wave
        window = window_of(s)
        windows[s - 1, 0], windows[s - 1, 1] = window
        if s == 1:
            upper = times((wave[0][:HALO], wave[1][:HALO]), (window[0][:HALO], window[1][:HALO]))
            upper = right_mult((fold_columns(upper[0]), fold_columns(upper[1])), tables_ref, PROP_RIGHT)
            rows = [
                jnp.concatenate([upper[c] + lower_ref[c], upper[c] - lower_ref[c]], axis=0) for c in range(2)
            ]
            rows = left_mult(rows, tables_ref, PROP_LEFT)
            wave = (fold(rows[0]), fold(rows[1]))
            continue
        prod = times(wave, window)
        if s < 3:
            wave = propagate(prod, tables_ref)

    def before(s):
        ref = (probe_ref, first_wave_ref, waves.at[0], waves.at[1])[s]
        return ref[0], ref[1]

    def window_at(s):
        ref = first_window_ref if s == 0 else windows.at[s - 1]
        return ref[0], ref[1]

    field = right_mult((fold(prod[0]), fold(prod[1])), tables_ref, FAR_RIGHT)
    field = left_mult(field, tables_ref, FAR_LEFT)
    model = jnp.sqrt(field[0] * field[0] + field[1] * field[1] + 1.0)
    ratio = (model - amp_ref[...]) / model
    grad = (field[0] * ratio, -(field[1] * ratio))
    grad = right_mult(grad, tables_ref, BACK_RIGHT)
    grad = left_mult(grad, tables_ref, BACK_LEFT)
    grad = (fold(grad[0]), fold(grad[1]))
    copies = []
    for s in range(3, -1, -1):
        object_grad = times(before(s), grad)
        slot = jnp.where(place == s // 2, s % 2, 2 + s % 2)
        start = pl.multiple_of(slot * 2 * HALO, HALO)
        for c in range(2):
            value = object_grad[c] if c == 0 else -object_grad[c]
            core_out[slot, c] = value[HALO:]
            beside_out[pl.ds(start + c * HALO, HALO)] = value[:HALO]
        source = beside_out.at[pl.ds(start, 2 * HALO)]
        target = pl.multiple_of(s % 2 * 2 * HALO, HALO)
        early = jnp.where(slot // 2 == 1, 1, 0) != across_turned
        for which, ref in enumerate((late_out, early_out)):
            copy = pltpu.make_async_copy(source, ref.at[pl.ds(target, 2 * HALO)], sems.at[1, s])

            @pl.when(early == (which == 1))
            def _():
                copy.start()

        copies.append(copy)
        grad = times(window_at(s), grad)
        if s > 0:
            grad = propagate(grad, tables_ref)
    meta = info_ref[...].astype(F32)
    beside_out[8 * HALO :] = jnp.concatenate([meta, meta], axis=1)
    copy = pltpu.make_async_copy(beside_out.at[pl.ds(8 * HALO, 8)], early_out.at[pl.ds(4 * HALO, 8)], sems.at[1, 4])
    copy.start()
    copies.append(copy)
    load.wait()
    row, col = offsets[place, 0], offsets[place, 1]
    value = [grad[0], -grad[1]]
    for c in range(2):
        value[c] = pltpu.roll(value[c], lax.rem(WIDTH - row, WIDTH), 0)
        value[c] = pltpu.roll(value[c], lax.rem(WIDTH - col, WIDTH), 1)
    for ref, which in ((keep_out, odd), (send_out, 1 - odd)):
        part = jnp.where(which == 0, value[0], value[1])
        for h in range(2):
            ref[:, h] = part[:, h * HALF : (h + 1) * HALF].reshape(WIDTH // 8, 8, HALF)
    for copy in copies:
        copy.wait()


def widen(x, kept):
    left, right = x[..., :HALF], x[..., HALF:]
    return jnp.concatenate([jnp.where(kept, left, 0.0), right, jnp.where(kept, 0.0, left)], axis=-1)


def add_halos(info_ref, core_ref, across_ref, early_ref, beside_ref, out_ref, first, extra=None):
    odd = here()[1]
    own_kept = masks(info_ref, 0)[1]
    line = lax.broadcasted_iota(jnp.int32, (HALO, WIDTH), 0).astype(F32)
    column = lax.broadcasted_iota(jnp.int32, (HALO, HALF), 1).astype(F32)
    sides = []
    for ref, base, meta, after in (
        (across_ref, 0, early_ref[4 * HALO :], odd),
        (beside_ref, first * 2 * HALO, beside_ref[8 * HALO :], 1 - odd),
    ):
        kept = column >= meta[1:2, :HALF]
        mask = jnp.where(line >= meta[0:1], 1, 0) == after
        sides.append((ref, base, mask, kept))
    for j in range(2):
        for c in range(2):
            total = widen(core_ref[first + j, c], own_kept)
            for ref, base, mask, kept in sides:
                start = base + (j * 2 + c) * HALO
                total = total + widen(jnp.where(mask, ref[start : start + HALO], 0.0), kept)
            out_ref[j, c] = total if extra is None else total + extra[j, c]


def add_kernel(keep_ref, got_ref, out_ref):
    out_ref[...] = keep_ref[...] + got_ref[...]


def reduce_kernel(parts_ref, after_ref, out_ref):
    out_ref[...] = jnp.sum(parts_ref[...], axis=0)


def total_kernel(first_ref, second_ref, out_ref):
    total = first_ref[...] + second_ref[...]
    out_ref[...] = jnp.broadcast_to(total[None], out_ref.shape)


def sum_kernel(info_ref, core_ref, early_ref, beside_ref, after_ref, out_ref):
    add_halos(info_ref, core_ref, early_ref, early_ref, beside_ref, out_ref, 2)


def object_kernel(info_ref, core_ref, early_ref, beside_ref, late_ref, swapped_ref, after_ref, out_ref, token_ref):
    token_ref[...] = jnp.zeros(token_ref.shape, F32)
    add_halos(info_ref, core_ref, late_ref, early_ref, beside_ref, out_ref, 0, swapped_ref)


def probe_kernel(after_ref, keep_ref, got_ref, out_ref):
    odd = here()[1]
    for ref, which in ((keep_ref, odd), (got_ref, 1 - odd)):
        for h in range(2):
            out_ref[which, :, h * HALF : (h + 1) * HALF] = ref[:, h].reshape(WIDTH, HALF)


def call(kernel, shapes, smem, vmem, name, scratch=(), flops=0, nbytes=2_000_000, ins=None, outs=None, vmem_limit=40):
    single = isinstance(shapes[0], int)
    shapes = (shapes,) if single else shapes
    out = pl.pallas_call(
        kernel,
        out_shape=tuple(jax.ShapeDtypeStruct(shape, F32) for shape in shapes),
        in_specs=[SMEM] * len(smem) + list(ins or [VMEM] * len(vmem)),
        out_specs=outs or (VMEM,) * len(shapes),
        scratch_shapes=scratch,
        compiler_params=pltpu.CompilerParams(vmem_limit_bytes=vmem_limit * 1024 * 1024),
        cost_estimate=pl.CostEstimate(flops=flops, bytes_accessed=nbytes, transcendentals=0),
        name=name,
    )(*smem, *vmem)
    return out[0] if single else out


def swap_tile(x, beside):
    slabs, tiles = lax.axis_size("slab"), lax.axis_size("tile")
    pairs = []
    for slab in range(slabs):
        for tile in range(tiles):
            to = (tile + (1 if tile % 2 != beside else -1)) % tiles
            turned = tile // (tiles // 2) != to // (tiles // 2)
            pairs.append((slab * tiles + tile, (slab ^ turned) * tiles + to))
    return lax.ppermute(x, ("slab", "tile"), pairs)


def swap_core(x):
    count = lax.axis_size("tile")
    return lax.ppermute(x, "tile", [(i, i ^ 1) for i in range(count)])


def among_columns(x):
    slabs, tiles = lax.axis_size("slab"), lax.axis_size("tile")
    half = tiles // 2
    planes = [slab * tiles + far * half for slab in range(slabs) for far in range(2)]
    groups = [[plane + i for i in range(core, half, 2)] for plane in planes for core in range(2)]
    return lax.all_to_all(x, ("slab", "tile"), 0, 0, tiled=True, axis_index_groups=groups)


def swap_far(x):
    slabs, tiles = lax.axis_size("slab"), lax.axis_size("tile")
    half = tiles // 2
    pairs = [
        (slab * tiles + tile, (slabs - 1 - slab) * tiles + (tile + half) % tiles)
        for slab in range(slabs)
        for tile in range(tiles)
    ]
    return lax.ppermute(x, ("slab", "tile"), pairs)


def swap_slab(x):
    return lax.ppermute(x, "slab", [(0, 1), (1, 0)])


def shards(transmission, probe, scan_offsets, amplitudes):
    tables = jnp.asarray(make_tables())
    index = lax.axis_index("slab").astype(jnp.int32)
    where = (index.reshape(1), scan_offsets)
    info = jnp.where(index == 0, scan_offsets, scan_offsets[::-1]).reshape(4, 1)
    info = jnp.broadcast_to(jnp.concatenate([info, info]), (8, HALF))
    own = transmission
    part, whole, band = (2, 2, HALO, WIDTH), (2, 2, WIDTH, WIDTH), (2, 2, HALO, COLS)

    own_hbm, offsets_hbm = (pltpu.with_memory_space_constraint(x, pltpu.HBM) for x in (own, scan_offsets))
    core = call(
        core_kernel,
        part,
        (),
        (offsets_hbm, own_hbm),
        "core",
        scratch=[
            pltpu.SMEM((2, 2), jnp.int32),
            pltpu.VMEM((4, HALO, HALF), F32),
            pltpu.VMEM((4, HALO, HALF), F32),
            pltpu.SemaphoreType.DMA((3, 5)),
        ],
        ins=(HBM, HBM),
    )
    core = swap_slab(core)
    beside, across = swap_tile(own, 1), swap_tile(own, 0)
    rolled = call(roll_probe_kernel, (2, WIDTH, WIDTH), where, (probe,), "roll")
    amp = call(amp_kernel, (WIDTH, WIDTH), where, (amplitudes,), "amp")
    halo, second_halo = call(halo_kernel, (part[1:],) * 2, (), (info, across, beside), "halo")
    halo, second_halo = swap_slab(halo), swap_slab(second_halo)
    windows = call(window_kernel, whole, (), (info, own, across, beside), "window")

    wave, window, lower = call(
        first_kernel,
        (probe.shape, probe.shape, part[1:]),
        (),
        (info, tables, rolled, windows, core, halo),
        "first",
    )
    tiles = (WIDTH // 8, 2, 8, HALF)
    keep, send, cores, beside, early, late = call(
        position_kernel,
        (tiles, tiles, (4, 2, HALO, WIDTH), (8 * HALO + 8, WIDTH), (4 * HALO + 8, WIDTH), (4 * HALO, WIDTH)),
        (),
        (info, scan_offsets, tables, rolled, amp, windows, core, halo, second_halo, wave, window, lower),
        "position",
        scratch=[
            pltpu.VMEM((2, 2, WIDTH, WIDTH), F32),
            pltpu.VMEM((3, 2, WIDTH, WIDTH), F32),
            pltpu.SMEM((2, 2), jnp.int32),
            pltpu.SemaphoreType.DMA((2, 6)),
        ],
        ins=(VMEM, HBM) + (VMEM,) * 10,
        flops=3_300_000_000,
        nbytes=10_000_000,
        outs=(VMEM, VMEM, VMEM, VMEM, HBM, HBM),
    )
    early = swap_tile(early, 0)
    parts = (WIDTH // 16, 4, 8, HALF)
    kept = call(add_kernel, tiles, (), (keep, swap_core(send)), "add").reshape(parts)
    kept = call(reduce_kernel, parts[1:], (), (among_columns(kept), early), "reduce")
    beside, late, kept = lax.optimization_barrier((beside, late, kept))
    sides = (info, cores, early, swap_tile(beside, 1))
    late = swap_tile(late, 0)
    kept = call(add_kernel, parts[1:], (), (kept, swap_slab(kept)), "add_slabs")
    got = swap_slab(call(sum_kernel, band, (), sides + (kept,), "sum"))
    kept = call(total_kernel, parts, (), (kept, swap_far(kept)), "total")
    kept = among_columns(kept)
    other = swap_core(kept)
    object_grad, token = call(object_kernel, (band, (8, HALF)), (), sides + (late, got, kept), "object")
    probe_grad = call(
        probe_kernel,
        probe.shape,
        (),
        (token, kept.reshape(tiles), other.reshape(tiles)),
        "probe",
    )
    return object_grad, probe_grad


def solution(mesh):
    placed = (P("slab", None, "tile", None), P(), P("tile", None), P("tile", None, None))
    return jax.shard_map(
        shards,
        mesh=mesh,
        in_specs=placed,
        out_specs=(P("slab", None, "tile", None), P()),
        check_vma=False,
    )
```

```python
import functools

import jax
import jax.numpy as jnp
import numpy as np
from jax import lax
from jax.experimental import pallas as pl
from jax.experimental.pallas import tpu as pltpu
from jax.sharding import PartitionSpec as P

WIDTH = 256
HALF = 128
HALO = 128
COLS = 384
PROP_STRENGTH = 12.0
BF16 = jnp.bfloat16
F32 = jnp.float32
VMEM = pl.BlockSpec(memory_space=pltpu.VMEM)
SMEM = pl.BlockSpec(memory_space=pltpu.SMEM)
HBM = pl.BlockSpec(memory_space=pltpu.HBM)


def high_low(table):
    table = table.astype(np.float32)
    high = table.astype(jnp.bfloat16)
    low = (table - high.astype(np.float32)).astype(jnp.bfloat16)
    return np.stack([high, low])


def on_right(m):
    return high_low(np.block([[m.real, m.imag], [-m.imag, m.real]]))


def on_left(m):
    return high_low(np.block([[m.real, -m.imag], [m.imag, m.real]]))


def make_tables():
    index = np.arange(WIDTH)
    dft = np.exp(-2j * np.pi / WIDTH * (index[:, None] * index[None, :] % WIDTH)) / np.sqrt(WIDTH)
    freq = ((index + WIDTH // 2) % WIDTH - WIDTH // 2) / WIDTH
    phase = np.exp(-1j * PROP_STRENGTH * freq**2)
    prop = dft.conj() @ (phase[:, None] * dft)
    far = phase[:, None] * dft
    p, q = prop[:HALF, :HALF], prop[:HALF, HALF:]
    props = ((p + q) / 2, (p - q) / 2)
    fars = (far[0::2, :HALF], far[1::2, :HALF])
    return np.stack(
        [
            np.stack([on_right(m) for m in props]),
            np.stack([on_left(m) for m in props]),
            np.stack([on_right(m.T) for m in fars]),
            np.stack([on_left(m) for m in fars]),
            np.stack([on_right(m) for m in fars]),
            np.stack([on_left(m.T) for m in fars]),
        ]
    )


PROP_RIGHT, PROP_LEFT, FAR_RIGHT, FAR_LEFT, BACK_RIGHT, BACK_LEFT = range(6)


def split(x):
    high = x.astype(BF16)
    low = (x - high.astype(F32)).astype(BF16)
    return high, low


def dot(a, b):
    return jnp.dot(a, b, preferred_element_type=F32)


def fold(x):
    x = jnp.concatenate([x[:HALF] + x[HALF:], x[:HALF] - x[HALF:]], axis=0)
    return jnp.concatenate([x[:, :HALF] + x[:, HALF:], x[:, :HALF] - x[:, HALF:]], axis=1)


def fold_columns(x):
    return jnp.concatenate([x[:, :HALF] + x[:, HALF:], x[:, :HALF] - x[:, HALF:]], axis=1)


def right_mult(x, tables, which):
    re, im = [], []
    for h in range(2):
        part = slice(h * HALF, (h + 1) * HALF)
        high, low = split(jnp.concatenate([x[0][:, part], x[1][:, part]], axis=1))
        th, tl = tables[which, h, 0], tables[which, h, 1]
        out = dot(jnp.concatenate([high, low, high], axis=1), jnp.concatenate([th, th, tl], axis=0))
        re.append(out[:, :HALF])
        im.append(out[:, HALF:])
    return jnp.concatenate(re, axis=1), jnp.concatenate(im, axis=1)


def left_mult(x, tables, which):
    re, im = [], []
    for h in range(2):
        part = slice(h * HALF, (h + 1) * HALF)
        high, low = split(jnp.concatenate([x[0][part], x[1][part]], axis=0))
        th, tl = tables[which, h, 0], tables[which, h, 1]
        out = dot(jnp.concatenate([th, th, tl], axis=1), jnp.concatenate([high, low, high], axis=0))
        re.append(out[:HALF])
        im.append(out[HALF:])
    return jnp.concatenate(re, axis=0), jnp.concatenate(im, axis=0)


def propagate(x, tables):
    y = right_mult((fold(x[0]), fold(x[1])), tables, PROP_RIGHT)
    y = left_mult(y, tables, PROP_LEFT)
    return fold(y[0]), fold(y[1])


def times(a, b):
    return a[0] * b[0] - a[1] * b[1], a[0] * b[1] + a[1] * b[0]


def here():
    half = lax.axis_size("tile") // 2
    within = lax.axis_index("tile") % half
    turned = jnp.where((within == 0) | (within == half - 1), 1, 0)
    return lax.axis_index("slab"), within % 2, turned


def masks(info_ref, which):
    row = jnp.broadcast_to(info_ref[2 * which : 2 * which + 1], (HALO, HALF))
    col = jnp.broadcast_to(info_ref[2 * which + 1 : 2 * which + 2], (HALO, HALF))
    line = lax.broadcasted_iota(jnp.int32, (HALO, HALF), 0)
    lane = lax.broadcasted_iota(jnp.int32, (HALO, HALF), 1)
    return jnp.where(line >= row, 1, 0) == here()[1], lane >= col


def columns_of(x, kept):
    return jnp.where(kept, x(0), x(2)), x(1)


def halo_of(across_ref, beside_ref, at, from_beside, kept):
    def column(i):
        cols = slice(i * HALF, (i + 1) * HALF)
        return jnp.where(from_beside, beside_ref[at + (slice(None), cols)], across_ref[at + (slice(None), cols)])

    return columns_of(column, kept)


def roll_probe_kernel(place_ref, offsets_ref, probe_ref, out_ref):
    row, col = offsets_ref[place_ref[0], 0], offsets_ref[place_ref[0], 1]
    for c in range(2):
        out_ref[c] = pltpu.roll(pltpu.roll(probe_ref[c], row, 0), col, 1)


def core_kernel(offsets_ref, own_ref, out_ref, offsets, left, right, sems):
    load = pltpu.make_async_copy(offsets_ref, offsets, sems.at[0, 4])
    load.start()
    loads = []
    for i in range(4):
        at = (i // 2, i % 2, slice(None))
        loads.append(
            [
                pltpu.make_async_copy(own_ref.at[at + (slice(0, HALF),)], left.at[i], sems.at[0, i]),
                pltpu.make_async_copy(own_ref.at[at + (slice(WIDTH, COLS),)], right.at[i], sems.at[1, i]),
                pltpu.make_async_copy(
                    own_ref.at[at + (slice(HALF, WIDTH),)], out_ref.at[at + (slice(HALF, WIDTH),)], sems.at[2, i]
                ),
            ]
        )
        for copy in loads[i]:
            copy.start()
    load.wait()
    lane = lax.broadcasted_iota(jnp.int32, (HALO, HALF), 1)
    kept = lane >= offsets[1 - lax.axis_index("slab"), 1]
    for i in range(4):
        loads[i][0].wait()
        loads[i][1].wait()
        out_ref[i // 2, i % 2, :, :HALF] = jnp.where(kept, left[i], right[i])
    for i in range(4):
        loads[i][2].wait()


def amp_kernel(place_ref, offsets_ref, amp_ref, out_ref):
    x = amp_ref[place_ref[0]]
    line = lax.broadcasted_iota(jnp.int32, (WIDTH, WIDTH), 0)
    lane = lax.broadcasted_iota(jnp.int32, (WIDTH, WIDTH), 1)
    rows = jnp.where(lane == 2 * (line % HALF) + line // HALF, 1.0, 0.0).astype(BF16)
    cols = jnp.where(line == 2 * (lane % HALF) + lane // HALF, 1.0, 0.0).astype(BF16)

    def parts(value):
        high, rest = split(value)
        return high, rest, (value - high.astype(F32) - rest.astype(F32)).astype(BF16)

    x = sum(dot(rows, part) for part in parts(x))
    out_ref[...] = sum(dot(part, cols) for part in parts(x))


def halo_kernel(info_ref, across_ref, beside_ref, first_out, second_out):
    from_beside, kept = masks(info_ref, 1)
    for j, out_ref in enumerate((first_out, second_out)):
        for c in range(2):
            left, right = halo_of(across_ref, beside_ref, (j, c), from_beside, kept)
            out_ref[c, :, :HALF] = left
            out_ref[c, :, HALF:] = right


def window_kernel(info_ref, own_ref, across_ref, beside_ref, out_ref):
    from_beside, kept = masks(info_ref, 0)
    for j in range(2):
        for c in range(2):
            left, right = halo_of(across_ref, beside_ref, (j, c), from_beside, kept)
            out_ref[j, c, :HALO, :HALF] = left
            out_ref[j, c, :HALO, HALF:] = right
            left, right = columns_of(lambda i: own_ref[j, c, :, i * HALF : (i + 1) * HALF], kept)
            out_ref[j, c, HALO:, :HALF] = left
            out_ref[j, c, HALO:, HALF:] = right


def selector(info_ref, own_ref, core_ref, halo_refs):
    place, odd, turned = here()
    from_beside = masks(info_ref, 0)[0]
    turned = jnp.where(jnp.concatenate([from_beside, from_beside], axis=1), 0, turned)

    def window_of(s):
        mine = jnp.where(place == s // 2, 1, 0)
        out = []
        for c in range(2):
            halo = jnp.where(turned == mine, halo_refs[s % 2][c], own_ref[s % 2, c, :HALO])
            core = jnp.where(mine == 1, own_ref[s % 2, c, HALO:], core_ref[s % 2, c])
            out.append(jnp.concatenate([halo, core], axis=0))
        return out

    return window_of


def first_kernel(info_ref, tables_ref, probe_ref, own_ref, core_ref, halo_ref, wave_out, window_out, third_out, lower_out):
    window_of = selector(info_ref, own_ref, core_ref, (halo_ref, None))
    window = window_of(0)
    third_out[0], third_out[1] = window_of(2)
    window_out[0], window_out[1] = window
    wave = propagate(times((probe_ref[0], probe_ref[1]), window), tables_ref)
    wave_out[0], wave_out[1] = wave
    mine = here()[0] == 0
    core = [jnp.where(mine, own_ref[1, c, HALO:], core_ref[1, c]) for c in range(2)]
    lower = times((wave[0][HALO:], wave[1][HALO:]), core)
    lower = right_mult((fold_columns(lower[0]), fold_columns(lower[1])), tables_ref, PROP_RIGHT)
    lower_out[0], lower_out[1] = lower


def position_kernel(
    info_ref,
    offsets_ref,
    tables_ref,
    probe_ref,
    amp_ref,
    own_ref,
    core_ref,
    halo_ref,
    second_halo_ref,
    first_wave_ref,
    first_window_ref,
    third_window_ref,
    lower_ref,
    keep_out,
    send_out,
    core_out,
    beside_out,
    early_out,
    late_out,
    waves,
    windows,
    offsets,
    sems,
):
    place, odd, across_turned = here()
    load = pltpu.make_async_copy(offsets_ref, offsets, sems.at[0, 5])
    load.start()
    window_of = selector(info_ref, own_ref, core_ref, (halo_ref, second_halo_ref))
    wave = (first_wave_ref[0], first_wave_ref[1])
    for s in range(1, 4):
        if s > 1:
            waves[s - 2, 0], waves[s - 2, 1] = wave
        if s == 2:
            window = (third_window_ref[0], third_window_ref[1])
        else:
            window = window_of(s)
            windows[s // 2, 0], windows[s // 2, 1] = window
        if s == 1:
            upper = times((wave[0][:HALO], wave[1][:HALO]), (window[0][:HALO], window[1][:HALO]))
            upper = right_mult((fold_columns(upper[0]), fold_columns(upper[1])), tables_ref, PROP_RIGHT)
            rows = [
                jnp.concatenate([upper[c] + lower_ref[c], upper[c] - lower_ref[c]], axis=0) for c in range(2)
            ]
            rows = left_mult(rows, tables_ref, PROP_LEFT)
            wave = (fold(rows[0]), fold(rows[1]))
            continue
        prod = times(wave, window)
        if s < 3:
            wave = propagate(prod, tables_ref)

    def before(s):
        ref = (probe_ref, first_wave_ref, waves.at[0], waves.at[1])[s]
        return ref[0], ref[1]

    def window_at(s):
        ref = (first_window_ref, windows.at[0], third_window_ref, windows.at[1])[s]
        return ref[0], ref[1]

    field = right_mult((fold(prod[0]), fold(prod[1])), tables_ref, FAR_RIGHT)
    field = left_mult(field, tables_ref, FAR_LEFT)
    model = jnp.sqrt(field[0] * field[0] + field[1] * field[1] + 1.0)
    ratio = (model - amp_ref[...]) / model
    grad = (field[0] * ratio, -(field[1] * ratio))
    grad = right_mult(grad, tables_ref, BACK_RIGHT)
    grad = left_mult(grad, tables_ref, BACK_LEFT)
    grad = (fold(grad[0]), fold(grad[1]))
    copies = []
    for s in range(3, -1, -1):
        object_grad = times(before(s), grad)
        slot = jnp.where(place == s // 2, s % 2, 2 + s % 2)
        start = pl.multiple_of(slot * 2 * HALO, HALO)
        for c in range(2):
            value = object_grad[c] if c == 0 else -object_grad[c]
            core_out[slot, c] = value[HALO:]
            beside_out[pl.ds(start + c * HALO, HALO)] = value[:HALO]
        source = beside_out.at[pl.ds(start, 2 * HALO)]
        target = pl.multiple_of(s % 2 * 2 * HALO, HALO)
        early = jnp.where(slot // 2 == 1, 1, 0) != across_turned
        for which, ref in enumerate((late_out, early_out)):
            copy = pltpu.make_async_copy(source, ref.at[pl.ds(target, 2 * HALO)], sems.at[1, s])

            @pl.when(early == (which == 1))
            def _():
                copy.start()

        copies.append(copy)
        grad = times(window_at(s), grad)
        if s > 0:
            grad = propagate(grad, tables_ref)
    meta = info_ref[...].astype(F32)
    beside_out[8 * HALO :] = jnp.concatenate([meta, meta], axis=1)
    copy = pltpu.make_async_copy(beside_out.at[pl.ds(8 * HALO, 8)], early_out.at[pl.ds(4 * HALO, 8)], sems.at[1, 4])
    copy.start()
    copies.append(copy)
    load.wait()
    row, col = offsets[place, 0], offsets[place, 1]
    value = [grad[0], -grad[1]]
    for c in range(2):
        value[c] = pltpu.roll(value[c], lax.rem(WIDTH - row, WIDTH), 0)
        value[c] = pltpu.roll(value[c], lax.rem(WIDTH - col, WIDTH), 1)
    for ref, which in ((keep_out, odd), (send_out, 1 - odd)):
        part = jnp.where(which == 0, value[0], value[1])
        for h in range(2):
            ref[:, h] = part[:, h * HALF : (h + 1) * HALF].reshape(WIDTH // 8, 8, HALF)
    for copy in copies:
        copy.wait()


def widen(x, kept):
    left, right = x[..., :HALF], x[..., HALF:]
    return jnp.concatenate([jnp.where(kept, left, 0.0), right, jnp.where(kept, 0.0, left)], axis=-1)


def add_halos(info_ref, core_ref, across_ref, early_ref, beside_ref, out_ref, first, extra=None):
    odd = here()[1]
    own_kept = masks(info_ref, 0)[1]
    line = lax.broadcasted_iota(jnp.int32, (HALO, WIDTH), 0).astype(F32)
    column = lax.broadcasted_iota(jnp.int32, (HALO, HALF), 1).astype(F32)
    sides = []
    for ref, base, meta, after in (
        (across_ref, 0, early_ref[4 * HALO :], odd),
        (beside_ref, first * 2 * HALO, beside_ref[8 * HALO :], 1 - odd),
    ):
        kept = column >= meta[1:2, :HALF]
        mask = jnp.where(line >= meta[0:1], 1, 0) == after
        sides.append((ref, base, mask, kept))
    for j in range(2):
        for c in range(2):
            total = widen(core_ref[first + j, c], own_kept)
            for ref, base, mask, kept in sides:
                start = base + (j * 2 + c) * HALO
                total = total + widen(jnp.where(mask, ref[start : start + HALO], 0.0), kept)
            out_ref[j, c] = total if extra is None else total + extra[j, c]


def add_kernel(keep_ref, got_ref, out_ref):
    out_ref[...] = keep_ref[...] + got_ref[...]


def reduce_kernel(parts_ref, after_ref, out_ref):
    out_ref[...] = jnp.sum(parts_ref[...], axis=0)


def total_kernel(first_ref, second_ref, out_ref):
    total = first_ref[...] + second_ref[...]
    out_ref[...] = jnp.broadcast_to(total[None], out_ref.shape)


def sum_kernel(info_ref, core_ref, early_ref, beside_ref, after_ref, out_ref):
    add_halos(info_ref, core_ref, early_ref, early_ref, beside_ref, out_ref, 2)


def object_kernel(info_ref, core_ref, early_ref, beside_ref, late_ref, swapped_ref, after_ref, out_ref, token_ref):
    token_ref[...] = jnp.zeros(token_ref.shape, F32)
    add_halos(info_ref, core_ref, late_ref, early_ref, beside_ref, out_ref, 0, swapped_ref)


def probe_kernel(after_ref, keep_ref, got_ref, out_ref):
    odd = here()[1]
    for ref, which in ((keep_ref, odd), (got_ref, 1 - odd)):
        for h in range(2):
            out_ref[which, :, h * HALF : (h + 1) * HALF] = ref[:, h].reshape(WIDTH, HALF)


def call(kernel, shapes, smem, vmem, name, scratch=(), flops=0, nbytes=2_000_000, ins=None, outs=None, vmem_limit=40):
    single = isinstance(shapes[0], int)
    shapes = (shapes,) if single else shapes
    out = pl.pallas_call(
        kernel,
        out_shape=tuple(jax.ShapeDtypeStruct(shape, F32) for shape in shapes),
        in_specs=[SMEM] * len(smem) + list(ins or [VMEM] * len(vmem)),
        out_specs=outs or (VMEM,) * len(shapes),
        scratch_shapes=scratch,
        compiler_params=pltpu.CompilerParams(vmem_limit_bytes=vmem_limit * 1024 * 1024),
        cost_estimate=pl.CostEstimate(flops=flops, bytes_accessed=nbytes, transcendentals=0),
        name=name,
    )(*smem, *vmem)
    return out[0] if single else out


def swap_tile(x, beside):
    slabs, tiles = lax.axis_size("slab"), lax.axis_size("tile")
    pairs = []
    for slab in range(slabs):
        for tile in range(tiles):
            to = (tile + (1 if tile % 2 != beside else -1)) % tiles
            turned = tile // (tiles // 2) != to // (tiles // 2)
            pairs.append((slab * tiles + tile, (slab ^ turned) * tiles + to))
    return lax.ppermute(x, ("slab", "tile"), pairs)


def swap_core(x):
    count = lax.axis_size("tile")
    return lax.ppermute(x, "tile", [(i, i ^ 1) for i in range(count)])


def among_columns(x):
    slabs, tiles = lax.axis_size("slab"), lax.axis_size("tile")
    half = tiles // 2
    planes = [slab * tiles + far * half for slab in range(slabs) for far in range(2)]
    groups = [[plane + i for i in range(core, half, 2)] for plane in planes for core in range(2)]
    return lax.all_to_all(x, ("slab", "tile"), 0, 0, tiled=True, axis_index_groups=groups)


def swap_far(x):
    slabs, tiles = lax.axis_size("slab"), lax.axis_size("tile")
    half = tiles // 2
    pairs = [
        (slab * tiles + tile, (slabs - 1 - slab) * tiles + (tile + half) % tiles)
        for slab in range(slabs)
        for tile in range(tiles)
    ]
    return lax.ppermute(x, ("slab", "tile"), pairs)


def swap_slab(x):
    return lax.ppermute(x, "slab", [(0, 1), (1, 0)])


def shards(transmission, probe, scan_offsets, amplitudes):
    tables = jnp.asarray(make_tables())
    index = lax.axis_index("slab").astype(jnp.int32)
    where = (index.reshape(1), scan_offsets)
    info = jnp.where(index == 0, scan_offsets, scan_offsets[::-1]).reshape(4, 1)
    info = jnp.broadcast_to(jnp.concatenate([info, info]), (8, HALF))
    own = transmission
    part, whole, band = (2, 2, HALO, WIDTH), (2, 2, WIDTH, WIDTH), (2, 2, HALO, COLS)

    own_hbm, offsets_hbm = (pltpu.with_memory_space_constraint(x, pltpu.HBM) for x in (own, scan_offsets))
    core = call(
        core_kernel,
        part,
        (),
        (offsets_hbm, own_hbm),
        "core",
        scratch=[
            pltpu.SMEM((2, 2), jnp.int32),
            pltpu.VMEM((4, HALO, HALF), F32),
            pltpu.VMEM((4, HALO, HALF), F32),
            pltpu.SemaphoreType.DMA((3, 5)),
        ],
        ins=(HBM, HBM),
    )
    core = swap_slab(core)
    beside, across = swap_tile(own, 1), swap_tile(own, 0)
    rolled = call(roll_probe_kernel, (2, WIDTH, WIDTH), where, (probe,), "roll")
    amp = call(amp_kernel, (WIDTH, WIDTH), where, (amplitudes,), "amp")
    halo, second_halo = call(halo_kernel, (part[1:],) * 2, (), (info, across, beside), "halo")
    halo, second_halo = swap_slab(halo), swap_slab(second_halo)
    windows = call(window_kernel, whole, (), (info, own, across, beside), "window")

    wave, window, third, lower = call(
        first_kernel,
        (probe.shape, probe.shape, probe.shape, part[1:]),
        (),
        (info, tables, rolled, windows, core, halo),
        "first",
    )
    tiles = (WIDTH // 8, 2, 8, HALF)
    keep, send, cores, beside, early, late = call(
        position_kernel,
        (tiles, tiles, (4, 2, HALO, WIDTH), (8 * HALO + 8, WIDTH), (4 * HALO + 8, WIDTH), (4 * HALO, WIDTH)),
        (),
        (info, scan_offsets, tables, rolled, amp, windows, core, halo, second_halo, wave, window, third, lower),
        "position",
        scratch=[
            pltpu.VMEM((2, 2, WIDTH, WIDTH), F32),
            pltpu.VMEM((2, 2, WIDTH, WIDTH), F32),
            pltpu.SMEM((2, 2), jnp.int32),
            pltpu.SemaphoreType.DMA((2, 6)),
        ],
        ins=(VMEM, HBM) + (VMEM,) * 11,
        flops=3_300_000_000,
        nbytes=10_000_000,
        outs=(VMEM, VMEM, VMEM, VMEM, HBM, HBM),
    )
    early = swap_tile(early, 0)
    parts = (WIDTH // 16, 4, 8, HALF)
    kept = call(add_kernel, tiles, (), (keep, swap_core(send)), "add").reshape(parts)
    kept = call(reduce_kernel, parts[1:], (), (among_columns(kept), early), "reduce")
    beside, late, kept = lax.optimization_barrier((beside, late, kept))
    sides = (info, cores, early, swap_tile(beside, 1))
    late = swap_tile(late, 0)
    kept = call(add_kernel, parts[1:], (), (kept, swap_slab(kept)), "add_slabs")
    got = swap_slab(call(sum_kernel, band, (), sides + (kept,), "sum"))
    kept = call(total_kernel, parts, (), (kept, swap_far(kept)), "total")
    kept = among_columns(kept)
    other = swap_core(kept)
    object_grad, token = call(object_kernel, (band, (8, HALF)), (), sides + (late, got, kept), "object")
    probe_grad = call(
        probe_kernel,
        probe.shape,
        (),
        (token, kept.reshape(tiles), other.reshape(tiles)),
        "probe",
    )
    return object_grad, probe_grad


def solution(mesh):
    placed = (P("slab", None, "tile", None), P(), P("tile", None), P("tile", None, None))
    return jax.shard_map(
        shards,
        mesh=mesh,
        in_specs=placed,
        out_specs=(P("slab", None, "tile", None), P()),
        check_vma=False,
    )
```
